128 devices in a mesh: section: 4 (over z), sky: 32 (over y, x, core).
Axes of the slice: x: 4, y: 4, z: 4, core: 2. Of those that a mesh axis runs over, the one named last changes fastest.
Arguments:
- exposures: bfloat16 [256, 256, 1024], P('sky', 'section'), may hold values from -6 to 6
- coef_code: int32 [256, 27], P('sky'), may hold values from 0 to 63
- coef_table: float32 [27, 64], replicated, may hold values from -1.25 to 1.25
- basis_rows: float32 [27, 23], replicated, may hold values from -1.25 to 1.25
- basis_cols: float32 [27, 23], replicated, may hold values from -1.25 to 1.25
- exposure_weight: int32 [256], P('sky'), may hold values from 1 to 8
- intersection_patch: int32 [256, 8], P('sky'), may hold values from 0 to 31, all different within a row; in each aligned block of 8 rows (0 to 7, 8 to 15, ...) at most 4 rows name the same one
- intersection_shift: int32 [256, 8], P('sky'), may hold values from 0 to 128
- psf_kernels: bfloat16 [3, 41, 41], replicated, may hold values from -0.15625 to 0.15625
Outputs:
- coadd: float32 [32, 256, 1024], P('sky', 'section')
- detect: float32 [32, 3, 256, 1024], P('sky', None, 'section')
The draws below stay inside these ranges and needn't reach their ends.
Inputs may be any that keep to these rules, and one draw needn't show every extreme that they name: `intersection_patch`: no exposure names a patch twice. Within the exposures of one device (aligned blocks of 8 exposures) no patch is named by more than 4 entries, a bound that some block reaches. Every patch is named by some exposure.
All inputs are finite; a program needn't handle non-finite values.
Results may differ from the reference program's by a relative error of at most 0.005.
Values may be sent and summed in bfloat16 or wider, within the bound.
No kernel may reach another device: no remote copies, remote signals or barrier semaphores. Data moves between devices by JAX's collectives and lax.ppermute only.
A program may use at most 192 MiB of HBM per device.

```python
import math
import jax
import jax.numpy as jnp
import numpy as np
from jax import lax

COLS = 1024
E_DEV = 8
OV = 8
KW = 23
NB = 27
LEVELS = 64
DW = 41
SCALES = 3
CAP = 4
MAXOFF = 128
EXPOS = 256
HEIGHT = 256
PATCHES = 32
N_SKY = 32


def with_ends(drawn, stream_key, smallest, top_value):
    extent = drawn.shape
    index_at = [jax.random.randint(jax.random.fold_in(stream_key, axis), (), 0, extent[axis]) for axis in range(len(extent))]
    drawn = drawn.at[tuple(index_at)].set(smallest)
    longest = extent.index(max(extent))
    index_at[longest] = (index_at[longest] + 1) % extent[longest]
    return drawn.at[tuple(index_at)].set(top_value)


def levels(rng, dims, shards, least, high):
    def one(dim, shards_of):
        heights = jax.random.uniform(jax.random.fold_in(jax.random.fold_in(rng, 6), dim), (shards_of,), jnp.float32, least / len(shards), high / len(shards))
        return jnp.repeat(jnp.exp(heights), dims[dim] // shards_of).reshape((-1,) + (1,) * (len(dims) - dim - 1))

    factor_of = one(*shards[0])
    for cut in shards[1:]:
        factor_of = factor_of * one(*cut)
    return factor_of


def deal_out(stream_key, own, number, rows, number_of, top, limit, lean):
    ranking = jax.random.permutation(stream_key, number_of)
    crowded, usual = shares(number_of, rows * top, limit, lean, True), shares(number_of, rows * top, limit, lean, False)
    places = jnp.arange(number_of)

    def named(lengths, offset_by):
        used = int((lengths > 0).sum())
        fixed = max(1, used // 4)
        shifted = fixed + (places - fixed + offset_by * (used - fixed)) % max(1, number_of - fixed)
        return jnp.zeros((number_of,), jnp.int32).at[ranking[jnp.where(places < fixed, places, shifted)]].set(jnp.asarray(lengths, jnp.int32))

    lengths = jnp.where(number % 4 == 0, named(crowded, number // 4), named(usual, number - number // 4 - 1))
    mixed = jax.random.permutation(jax.random.fold_in(own, 3), number_of)
    giver, sink = mixed[0:number_of // 2 * 2:2], mixed[1:number_of // 2 * 2:2]
    margin = jnp.minimum(lengths[giver] - 1, limit - lengths[sink]) // 2
    margin = jnp.where((giver == ranking[0]) | (sink == ranking[0]) | (lengths[sink] == 0), 0, jnp.maximum(margin, 0))
    shifted = jax.random.randint(jax.random.fold_in(own, 4), (number_of // 2,), 0, 1 << 20) % (margin + 1)
    lengths = lengths.at[giver].add(-shifted).at[sink].add(shifted)
    items = jnp.searchsorted(jnp.cumsum(lengths), jnp.arange(rows * top), side="right").astype(jnp.int32)
    grid = items.reshape(top, rows).T
    grid = grid[jax.random.permutation(jax.random.fold_in(own, 1), rows)]
    offset_by = jax.random.randint(jax.random.fold_in(own, 2), (rows, 1), 0, top)
    return jnp.take_along_axis(grid, (jnp.arange(top)[None, :] + offset_by) % top, axis=1)


def shares(amount, total, reach, skew, full):
    portions = [(1 << 20) // math.isqrt(grade ** skew) + 1 for grade in range(1, amount + 1)]
    largest = reach if full else min(reach, max(-(-total // amount), total * portions[0] // sum(portions)))
    least = 1 if total - largest >= amount - 1 else 0
    given, surplus = [largest] + [least] * (amount - 1), total - largest - least * (amount - 1)
    while surplus > 0:
        movable = [i for i in range(1, amount) if given[i] < largest] or [i for i in range(1, amount) if given[i] < reach]
        pool, remaining = sum([portions[i] for i in movable]), surplus
        for i in movable:
            addition = min(reach - given[i], max(1, remaining * portions[i] // pool), surplus)
            given[i] = given[i] + addition
            surplus = surplus - addition
    return np.array(given)


def noise(key, dims, scale, most, shards=(), held_as=jnp.bfloat16):
    factor_of = levels(key, dims, shards, -0.22, 0.18) if shards else 1.0
    values = jax.random.normal(key, dims, jnp.float32) * scale * factor_of
    return jnp.minimum(jnp.maximum(values, -most), most).astype(held_as)


def setup_inputs(seed: int = 0) -> dict:
    seeds = jax.random.split(jax.random.key(seed), 10)
    exposures = noise(seeds[0], (EXPOS, HEIGHT, COLS), 1.0, 6.0, ((0, 32), (1, 4)))
    coef_code = with_ends(jax.random.randint(seeds[1], (EXPOS, NB), 0, LEVELS), jax.random.fold_in(seeds[1], 1), 0, LEVELS - 1).astype(jnp.int32)
    coef_table = noise(seeds[2], (NB, LEVELS), NB ** -0.5, 1.25, (), jnp.float32)
    basis_rows = noise(seeds[3], (NB, KW), KW ** -0.5, 1.25, (), jnp.float32)
    basis_cols = noise(seeds[4], (NB, KW), KW ** -0.5, 1.25, (), jnp.float32)
    exposure_weight = with_ends(jax.random.randint(seeds[5], (EXPOS,), 1, 9), jax.random.fold_in(seeds[5], 1), 1, 8).astype(jnp.int32)
    intersection_patch_keys = jax.random.split(jax.random.fold_in(seeds[6], 1), EXPOS // E_DEV)
    intersection_patch_turns = jax.random.permutation(jax.random.fold_in(seeds[6], 3), EXPOS // E_DEV)
    intersection_patch = jax.vmap(lambda own, number: deal_out(jax.random.fold_in(seeds[6], 2), own, number, E_DEV, N_SKY, OV, CAP, 2))(intersection_patch_keys, intersection_patch_turns).reshape((EXPOS, OV))
    intersection_shift = with_ends(jax.random.randint(seeds[7], (EXPOS, OV), 0, MAXOFF + 1), jax.random.fold_in(seeds[7], 1), 0, MAXOFF).astype(jnp.int32)
    psf_kernels = noise(seeds[8], (SCALES, DW, DW), (DW * DW) ** -0.5, 0.15625)
    return dict(exposures=exposures, coef_code=coef_code, coef_table=coef_table, basis_rows=basis_rows, basis_cols=basis_cols, exposure_weight=exposure_weight, intersection_patch=intersection_patch, intersection_shift=intersection_shift, psf_kernels=psf_kernels)


def correlate(plane, kernels):
    half_taps = kernels.shape[-1] // 2
    result = lax.conv_general_dilated(plane[None, None], kernels[:, None], (1, 1), ((half_taps, half_taps), (half_taps, half_taps)), precision=lax.Precision.HIGHEST)
    return result[0]


def reference(exposures, coef_code, coef_table, basis_rows, basis_cols, exposure_weight, intersection_patch, intersection_shift, psf_kernels):
    coefficient = jnp.take_along_axis(coef_table.T, coef_code, axis=0)
    kernel = jnp.einsum('eb,bi,bj->eij', coefficient, basis_rows, basis_cols, precision=lax.Precision.HIGHEST).astype(jnp.bfloat16)
    kernel = lax.optimization_barrier(kernel)

    def warp_one(packed):
        plane, kernel_one = packed
        return correlate(plane.astype(jnp.float32), kernel_one[None].astype(jnp.float32))[0].astype(jnp.bfloat16)

    matched = lax.optimization_barrier(lax.map(warp_one, (exposures, kernel)))
    widened = jnp.pad(matched, ((0, 0), (0, 0), (MAXOFF, 0)))
    column = jnp.arange(COLS).astype(jnp.int32)

    def add_entry(entry_id, carry):
        numerator, denominator = carry
        member = entry_id // OV
        slot_index = entry_id % OV
        patch_id = intersection_patch[member, slot_index]
        offset = intersection_shift[member, slot_index].astype(jnp.int32)
        weight = exposure_weight[member].astype(jnp.float32)
        piece = lax.dynamic_slice_in_dim(widened[member], (MAXOFF - offset).astype(jnp.int32), COLS, 1).astype(jnp.float32)
        numerator = numerator.at[patch_id].add(weight * piece)
        coverage = (column >= offset).astype(jnp.float32)
        denominator = denominator.at[patch_id].add(weight * coverage)
        return numerator, denominator

    initial = (jnp.zeros((PATCHES, HEIGHT, COLS), jnp.float32), jnp.zeros((PATCHES, COLS), jnp.float32))
    numerator, denominator = lax.fori_loop(0, EXPOS * OV, add_entry, initial)
    coadd = numerator / jnp.maximum(denominator, 1.0)[:, None, :]

    def detect_one(plane):
        rounded = lax.optimization_barrier(plane.astype(jnp.bfloat16))
        return correlate(rounded.astype(jnp.float32), psf_kernels.astype(jnp.float32))

    detect = lax.map(detect_one, coadd)
    return coadd, detect
```

```python
import functools

import jax
import jax.numpy as jnp
from jax import lax
from jax.experimental import pallas as pl
from jax.experimental.pallas import tpu as pltpu
from jax.sharding import Mesh, PartitionSpec as P

f32 = jnp.float32
bf16 = jnp.bfloat16

lanes = 128
half = 64
group = 4
vmem_bytes = 56 * 1024 * 1024


def neighbours(count):
    up = [(i, i + 1) for i in range(count - 1)]
    return up, [(b, a) for a, b in up]


def profile_rows(profile, taps):
    lead = profile.shape[:-1]
    zeros = lambda n: jnp.zeros(lead + (n,), profile.dtype)
    first = jnp.concatenate(
        [profile[..., :1], zeros(lanes - taps), profile[..., :0:-1]], axis=-1
    )
    second = jnp.concatenate(
        [zeros(half - taps + 1), profile[..., ::-1], zeros(lanes - half - 1)], axis=-1
    )
    return first, second


def pad_rows(rows, low, high):
    return jnp.pad(rows, [(0, 0)] * (rows.ndim - 2) + [(low, high), (0, 0)])


def lane_ids(rows):
    return lax.broadcasted_iota(jnp.int32, (rows, lanes), 1)


def band_mask(depth, taps):
    k = lax.broadcasted_iota(jnp.int32, (depth, lanes), 0)
    gap = k - lane_ids(depth) % half
    return (gap >= 0) & (gap < taps)


def band_tile(row, mask):
    depth = mask.shape[0]
    wide = jnp.broadcast_to(row, (depth, lanes))
    turned = pltpu.roll(wide, 0, 1, stride=1, stride_axis=0)
    return jnp.where(mask, turned, 0.0).astype(bf16)


def put_frame(frame, tiles, row, reach):
    count = len(tiles)
    rows = tiles[0].shape[0]
    lane = lane_ids(rows)
    zero = jnp.zeros((rows, lanes), f32)
    right = [pltpu.roll(t, reach, 1) for t in tiles]
    left = [pltpu.roll(t, half + reach, 1) for t in tiles]
    for m in range(count):
        before = right[m - 1] if m else zero
        frame[0, m, row : row + rows, :] = jnp.where(lane < reach, before, right[m])
        after = left[m + 1] if m + 1 < count else zero
        frame[1, m, row : row + rows, :] = jnp.where(lane < half + reach, left[m], after)


def put_lhs(lhs, frame, spans, row):
    tiles = frame.shape[1]
    for t in range(spans):
        for par in range(2):
            for m in range(tiles):
                at = (par * tiles + m) * 16
                piece = frame[par, m, pl.ds(row + t, 16, stride=group), :]
                lhs[at : at + 16, t * lanes : (t + 1) * lanes] = piece.astype(bf16)


def split_rows(even, odd, lane):
    first = jnp.where(lane < half, even, pltpu.roll(odd, half, 1))
    second = jnp.where(lane < half, pltpu.roll(even, half, 1), odd)
    return first, second


def match_body(taps, code, table, g, x, lo, hi, out, frame, lhs, w):
    e = pl.program_id(0)
    reach = taps // 2
    count = x.shape[2] // lanes
    depth = 96

    @pl.when(e == 0)
    def _():
        w[...] = jnp.zeros_like(w)

    total = jnp.zeros(g.shape[1:], f32)
    for b in range(g.shape[0]):
        total = total + table[b, code[e, b]] * g[b]
    total = total.astype(bf16).astype(f32)
    mask = band_mask(depth, taps)
    for u in range(taps + 1):
        tile = band_tile(total[u : u + 1, :], mask)
        w[u * lanes : u * lanes + depth, 0:lanes] = tile
        w[(u + 2) * lanes : (u + 2) * lanes + depth, lanes : 2 * lanes] = tile

    for ref, row in ((lo, 16 - reach), (x, 16), (hi, 80)):
        rows = ref[0].astype(f32)
        put_frame(frame, [rows[:, m * lanes : (m + 1) * lanes] for m in range(count)], row, reach)
    put_lhs(lhs, frame, taps + 3, 16 - reach)
    acc = jnp.dot(lhs[...], w[...], preferred_element_type=f32)
    lane = lane_ids(16)
    for m in range(count):
        for h in range(2):
            even = acc[m * 16 : m * 16 + 16, h * lanes : (h + 1) * lanes]
            odd = acc[(count + m) * 16 : (count + m) * 16 + 16, h * lanes : (h + 1) * lanes]
            for b, part in enumerate(split_rows(even, odd, lane)):
                at = (2 * h + b) * 16
                out[0, at : at + 16, m * lanes : (m + 1) * lanes] = part.astype(bf16)


def match(code, table, g, x, lo, hi, taps):
    number, rows, cols = x.shape
    smem = pl.BlockSpec(memory_space=pltpu.SMEM)
    one = lambda n: pl.BlockSpec((1, n, cols), lambda e: (e, 0, 0))
    spans = taps + 3
    return pl.pallas_call(
        functools.partial(match_body, taps),
        grid=(number,),
        in_specs=[smem, smem, pl.BlockSpec(g.shape, lambda e: (0, 0, 0)),
                  one(rows), one(lo.shape[1]), one(hi.shape[1])],
        out_specs=one(rows),
        out_shape=jax.ShapeDtypeStruct((number, rows, cols), bf16),
        scratch_shapes=[
            pltpu.VMEM((2, cols // lanes, 96, lanes), f32),
            pltpu.VMEM((256, spans * lanes), bf16),
            pltpu.VMEM((spans * lanes, 256), bf16),
        ],
        compiler_params=pltpu.CompilerParams(vmem_limit_bytes=vmem_bytes),
        cost_estimate=pl.CostEstimate(
            flops=number * 2 * 256 * 256 * spans * lanes, bytes_accessed=4 * x.size, transcendentals=0
        ),
        name="match",
    )(code, table, g, x, lo, hi)


def pile_body(core, weight, patch, shift, mine, other, out, planes, counts, source, offset):
    i = pl.program_id(0)
    number, rows, cols = mine.shape
    tiles = cols // lanes
    per = patch.shape[1]
    slots = 8
    patches = counts.shape[0]

    @pl.when(i == 0)
    def _():
        for e in range(2 * number):
            ref = mine if e < number else other
            scale = weight[e].astype(f32)
            value = ref[e % number].astype(f32) * scale
            for m in range(tiles):
                planes[e, m] = value[:, m * lanes : (m + 1) * lanes]
        planes[2 * number] = jnp.zeros((tiles, rows, lanes), f32)

        def clear(p, _):
            counts[p] = 0
            for s in range(slots):
                source[p * slots + s] = 2 * number
                offset[p * slots + s] = 0
            return 0

        lax.fori_loop(0, patches, clear, 0)

        def enter(e, _):
            for k in range(per):
                p = patch[e, k]
                at = counts[p]
                source[p * slots + at] = e
                offset[p * slots + at] = shift[e, k]
                counts[p] = at + 1
            return 0

        lax.fori_loop(0, 2 * number, enter, 0)

    p = 2 * i + core[0]
    lane = lane_ids(16)
    for c in range(rows // 16):
        total = [None] * tiles
        for s in range(slots):
            e = source[p * slots + s]
            o = offset[p * slots + s]
            keep = lane < o
            before = jnp.zeros((16, lanes), f32)
            for m in range(tiles):
                turned = pltpu.roll(planes[e, m, c * 16 : c * 16 + 16, :], o, 1)
                part = jnp.where(keep, before, turned)
                before = turned
                total[m] = part if s == 0 else total[m] + part
        for m in range(tiles):
            out[0, c * 16 : c * 16 + 16, m * lanes : (m + 1) * lanes] = total[m].astype(bf16)


def pile(core, weight, patch, shift, mine, other, patches):
    number, rows, cols = mine.shape
    smem = pl.BlockSpec(memory_space=pltpu.SMEM)
    whole = pl.BlockSpec(mine.shape, lambda i: (0, 0, 0))
    return pl.pallas_call(
        pile_body,
        grid=(patches // 2,),
        in_specs=[smem] * 4 + [whole] * 2,
        out_specs=pl.BlockSpec((1, rows, cols), lambda i: (i, 0, 0)),
        out_shape=jax.ShapeDtypeStruct((patches // 2, rows, cols), bf16),
        scratch_shapes=[
            pltpu.VMEM((2 * number + 1, cols // lanes, rows, lanes), f32),
            pltpu.SMEM((patches,), jnp.int32),
            pltpu.SMEM((patches * 8,), jnp.int32),
            pltpu.SMEM((patches * 8,), jnp.int32),
        ],
        compiler_params=pltpu.CompilerParams(vmem_limit_bytes=vmem_bytes),
        name="pile",
    )(core, weight, patch, shift, mine, other)


def coadd_body(reach, parts, cover, coadd, low, high, stage):
    count, rows, cols = parts.shape
    tiles = cols // lanes
    for m in range(tiles):
        scale = jnp.maximum(cover[0:1, m * lanes : (m + 1) * lanes], 1.0)
        for b in range(group):
            total = jnp.zeros((16, lanes), f32)
            for n in range(count):
                total = total + parts[n, b * 16 : b * 16 + 16, m * lanes : (m + 1) * lanes].astype(f32)
            stage[m, pl.ds(b, 16, stride=group), :] = total / scale
    for m in range(tiles):
        cut = slice(m * lanes, (m + 1) * lanes)
        coadd[:, cut] = stage[m]
        low[:, cut] = stage[m, 0:reach, :].astype(bf16)
        high[:, cut] = stage[m, rows - reach : rows, :].astype(bf16)


def coadd_of(parts, cover, reach):
    count, rows, cols = parts.shape
    edge = jax.ShapeDtypeStruct((reach, cols), bf16)
    return pl.pallas_call(
        functools.partial(coadd_body, reach),
        out_shape=(jax.ShapeDtypeStruct((rows, cols), f32), edge, edge),
        scratch_shapes=[pltpu.VMEM((cols // lanes, rows, lanes), f32)],
        compiler_params=pltpu.CompilerParams(vmem_limit_bytes=vmem_bytes),
        name="coadd",
    )(parts, cover)


def detect_body(taps, profile, x, lo, hi, out, frame, lhs, w, stage):
    reach = taps // 2
    rows, cols = x.shape
    count = cols // lanes
    scales = profile.shape[0]
    depth = 112
    mask = band_mask(depth, taps)
    w[...] = jnp.zeros_like(w)
    for s in range(scales):
        for u in range(taps + 1):
            tile = band_tile(profile[s, u : u + 1, :], mask)
            w[u * lanes : u * lanes + depth, 2 * s * lanes : (2 * s + 1) * lanes] = tile
            w[(u + 2) * lanes : (u + 2) * lanes + depth, (2 * s + 1) * lanes : (2 * s + 2) * lanes] = tile
    for ref, row in ((lo, 24 - reach), (x, 24), (hi, 24 + rows)):
        value = ref[...].astype(bf16).astype(f32)
        put_frame(frame, [value[:, m * lanes : (m + 1) * lanes] for m in range(count)], row, reach)
    put_lhs(lhs, frame, taps + 3, 24 - reach)
    lane = lane_ids(16)
    for s in range(scales):
        acc = jnp.dot(
            lhs[...], w[:, 2 * s * lanes : (2 * s + 2) * lanes], preferred_element_type=f32
        )
        for m in range(count):
            for h in range(2):
                even = acc[m * 16 : m * 16 + 16, h * lanes : (h + 1) * lanes]
                odd = acc[(count + m) * 16 : (count + m) * 16 + 16, h * lanes : (h + 1) * lanes]
                for b, part in enumerate(split_rows(even, odd, lane)):
                    stage[m, pl.ds(2 * h + b, 16, stride=group), :] = part
            out[s, :, m * lanes : (m + 1) * lanes] = stage[m]


def detect_of(profile, x, lo, hi, taps):
    rows, cols = x.shape
    scales = profile.shape[0]
    spans = taps + 3
    return pl.pallas_call(
        functools.partial(detect_body, taps),
        out_shape=jax.ShapeDtypeStruct((scales, rows, cols), f32),
        scratch_shapes=[
            pltpu.VMEM((2, cols // lanes, 24 + rows + 24, lanes), f32),
            pltpu.VMEM((256, spans * lanes), bf16),
            pltpu.VMEM((spans * lanes, scales * 256), bf16),
            pltpu.VMEM((cols // lanes, rows, lanes), f32),
        ],
        compiler_params=pltpu.CompilerParams(vmem_limit_bytes=vmem_bytes),
        name="detect",
    )(profile, x, lo, hi)


def on_device(
    exposures,
    coef_code,
    coef_table,
    basis_rows,
    basis_cols,
    exposure_weight,
    intersection_patch,
    intersection_shift,
    psf_kernels,
):
    number, rows, cols = exposures.shape
    taps = basis_rows.shape[1]
    reach = taps // 2
    wide = psf_kernels.shape[-1]
    wide_reach = wide // 2
    sections = lax.axis_size("section")
    across = ("sy", "sx")
    patches = lax.axis_size("sy") * lax.axis_size("sx") * 2
    core = lax.axis_index("core")
    up, down = neighbours(sections)

    lo = lax.ppermute(exposures[:, rows - reach :, :], "section", up)
    hi = lax.ppermute(exposures[:, :reach, :], "section", down)

    labels = jnp.concatenate(
        [exposure_weight[:, None], intersection_patch, intersection_shift], axis=1
    )
    everyone = lax.all_gather(labels, ("sy", "sx", "core"), axis=0)
    me = lax.axis_index(across) * 2 + core
    partner = lax.dynamic_index_in_dim(everyone, me + 1 - 2 * core, 0, keepdims=False)
    per = intersection_patch.shape[1]
    both = jnp.concatenate([labels, partner], axis=0)
    flat = everyone.reshape(-1, 1 + 2 * per)
    strength = jnp.where(flat[:, 1 : 1 + per] == me, flat[:, :1], 0).astype(f32)
    column = jnp.arange(lanes)
    cover = jnp.sum(
        jnp.where(column[:, None, None] >= flat[None, :, 1 + per :], strength[None], 0.0), axis=(1, 2)
    )
    cover = jnp.concatenate([cover, jnp.broadcast_to(jnp.sum(strength), (cols - lanes,))])[None]

    cols_a, cols_b = profile_rows(basis_cols, taps)
    rows_a = jnp.pad(basis_rows, ((0, 0), (0, 1)))
    rows_b = jnp.pad(basis_rows, ((0, 0), (1, 0)))
    g = rows_a[:, :, None] * cols_a[:, None, :] + rows_b[:, :, None] * cols_b[:, None, :]
    psf_a, psf_b = profile_rows(psf_kernels.astype(f32), wide)
    profile = pad_rows(psf_a, 0, 1) + pad_rows(psf_b, 1, 0)

    matched = match(coef_code, coef_table, g, exposures, lo, hi, taps)
    other = lax.ppermute(matched, "core", [(0, 1), (1, 0)])
    partial = pile(
        core[None], both[:, 0], both[:, 1 : 1 + per], both[:, 1 + per :], matched, other, patches
    )
    parts = lax.all_to_all(partial, across, split_axis=0, concat_axis=0, tiled=True)
    coadd, low, high = coadd_of(parts, cover, wide_reach)
    lo = lax.ppermute(high, "section", up)
    hi = lax.ppermute(low, "section", down)
    detect = detect_of(profile, coadd, lo, hi, wide)
    return (coadd[None], detect[None])


def solution(mesh):
    sections, sky = mesh.devices.shape
    grid = Mesh(mesh.devices.reshape(sections, 4, sky // 8, 2), ("section", "sy", "sx", "core"))
    sky = ("sy", "sx", "core")
    return jax.shard_map(
        on_device,
        mesh=grid,
        in_specs=(
            P(sky, "section", None),
            P(sky, None),
            P(),
            P(),
            P(),
            P(sky),
            P(sky, None),
            P(sky, None),
            P(),
        ),
        out_specs=(P(sky, "section", None), P(sky, None, "section", None)),
        check_vma=False,
    )
```

```python
import functools

import jax
import jax.numpy as jnp
from jax import lax
from jax.experimental import pallas as pl
from jax.experimental.pallas import tpu as pltpu
from jax.sharding import Mesh, PartitionSpec as P

f32 = jnp.float32
bf16 = jnp.bfloat16

lanes = 128
half = 64
group = 4
vmem_bytes = 56 * 1024 * 1024


def neighbours(count):
    up = [(i, i + 1) for i in range(count - 1)]
    return up, [(b, a) for a, b in up]


def profile_rows(profile, taps):
    lead = profile.shape[:-1]
    zeros = lambda n: jnp.zeros(lead + (n,), profile.dtype)
    first = jnp.concatenate(
        [profile[..., :1], zeros(lanes - taps), profile[..., :0:-1]], axis=-1
    )
    second = jnp.concatenate(
        [zeros(half - taps + 1), profile[..., ::-1], zeros(lanes - half - 1)], axis=-1
    )
    return first, second


def pad_rows(rows, low, high):
    return jnp.pad(rows, [(0, 0)] * (rows.ndim - 2) + [(low, high), (0, 0)])


def lane_ids(rows):
    return lax.broadcasted_iota(jnp.int32, (rows, lanes), 1)


def band_mask(depth, taps):
    k = lax.broadcasted_iota(jnp.int32, (depth, lanes), 0)
    gap = k - lane_ids(depth) % half
    return (gap >= 0) & (gap < taps)


def band_tile(row, mask):
    depth = mask.shape[0]
    wide = jnp.broadcast_to(row, (depth, lanes))
    turned = pltpu.roll(wide, 0, 1, stride=1, stride_axis=0)
    return jnp.where(mask, turned, 0.0).astype(bf16)


def put_frame(frame, tiles, row, reach):
    count = len(tiles)
    rows = tiles[0].shape[0]
    lane = lane_ids(rows)
    zero = jnp.zeros((rows, lanes), f32)
    right = [pltpu.roll(t, reach, 1).astype(f32) for t in tiles]
    left = [pltpu.roll(t, half + reach, 1).astype(f32) for t in tiles]
    for m in range(count):
        before = right[m - 1] if m else zero
        frame[0, m, row : row + rows, :] = jnp.where(lane < reach, before, right[m])
        after = left[m + 1] if m + 1 < count else zero
        frame[1, m, row : row + rows, :] = jnp.where(lane < half + reach, left[m], after)


def put_lhs(lhs, frame, spans, row):
    tiles = frame.shape[1]
    for t in range(spans):
        for par in range(2):
            for m in range(tiles):
                at = (par * tiles + m) * 16
                piece = frame[par, m, pl.ds(row + t, 16, stride=group), :]
                lhs[at : at + 16, t * lanes : (t + 1) * lanes] = piece.astype(bf16)


def split_rows(even, odd, lane):
    first = jnp.where(lane < half, even, pltpu.roll(odd, half, 1))
    second = jnp.where(lane < half, pltpu.roll(even, half, 1), odd)
    return first, second


def match_body(taps, code, table, g, x, lo, hi, out, frame, lhs, w):
    reach = taps // 2
    number, _, cols = x.shape
    count = cols // lanes
    depth = 96
    w[...] = jnp.zeros_like(w)
    mask = band_mask(depth, taps)
    lane = lane_ids(16)

    def one(e, _):
        total = jnp.zeros(g.shape[1:], f32)
        for b in range(g.shape[0]):
            total = total + table[b, code[e, b]] * g[b]
        total = total.astype(bf16).astype(f32)
        for u in range(taps + 1):
            tile = band_tile(total[u : u + 1, :], mask)
            w[u * lanes : u * lanes + depth, 0:lanes] = tile
            w[(u + 2) * lanes : (u + 2) * lanes + depth, lanes : 2 * lanes] = tile
        for ref, row in ((lo, 16 - reach), (x, 16), (hi, 80)):
            rows = ref[e]
            put_frame(frame, [rows[:, m * lanes : (m + 1) * lanes] for m in range(count)], row, reach)
        put_lhs(lhs, frame, taps + 3, 16 - reach)
        acc = jnp.dot(lhs[...], w[...], preferred_element_type=f32)
        for m in range(count):
            for h in range(2):
                cut = slice(h * lanes, (h + 1) * lanes)
                even = acc[m * 16 : m * 16 + 16, cut]
                odd = acc[(count + m) * 16 : (count + m) * 16 + 16, cut]
                for b, part in enumerate(split_rows(even, odd, lane)):
                    at = (2 * h + b) * 16
                    out[e, at : at + 16, m * lanes : (m + 1) * lanes] = part.astype(bf16)
        return 0

    lax.fori_loop(0, number, one, 0)


def match(code, table, g, x, lo, hi, taps):
    number, rows, cols = x.shape
    smem = pl.BlockSpec(memory_space=pltpu.SMEM)
    vmem = pl.BlockSpec(memory_space=pltpu.VMEM)
    spans = taps + 3
    return pl.pallas_call(
        functools.partial(match_body, taps),
        in_specs=[smem, smem, vmem, vmem, vmem, vmem],
        out_specs=vmem,
        out_shape=jax.ShapeDtypeStruct((number, rows, cols), bf16),
        scratch_shapes=[
            pltpu.VMEM((2, cols // lanes, 96, lanes), f32),
            pltpu.VMEM((256, spans * lanes), bf16),
            pltpu.VMEM((spans * lanes, 256), bf16),
        ],
        compiler_params=pltpu.CompilerParams(vmem_limit_bytes=vmem_bytes),
        cost_estimate=pl.CostEstimate(
            flops=number * 2 * 256 * 256 * spans * lanes, bytes_accessed=4 * x.size, transcendentals=0
        ),
        name="match",
    )(code, table, g, x, lo, hi)


def pile_body(core, mine_labels, other_labels, mine, other, out, counts, source, offset, scale, planes):
    number, rows, cols = mine.shape
    tiles = cols // lanes
    per = (mine_labels.shape[1] - 1) // 2
    patches = counts.shape[0]
    slots = 8

    def clear(p, _):
        counts[p] = 0
        for s in range(slots):
            source[p * slots + s] = 0
            offset[p * slots + s] = 0
            scale[p * slots + s] = 0.0
        return 0

    lax.fori_loop(0, patches, clear, 0)

    def enter(base, labels):
        def one(e, _):
            weight = labels[e, 0].astype(f32)
            for k in range(per):
                p = labels[e, 1 + k]
                at = counts[p]
                source[p * slots + at] = base + e
                offset[p * slots + at] = labels[e, 1 + per + k]
                scale[p * slots + at] = weight
                counts[p] = at + 1
            return 0

        lax.fori_loop(0, number, one, 0)

    enter(0, mine_labels)
    enter(number, other_labels)
    planes[0:number] = mine[...]
    planes[number:] = other[...]
    lane = lane_ids(16)

    def patch(i, _):
        p = 2 * i + core[0]

        def some(used):
            entries = [
                (source[p * slots + s], offset[p * slots + s], scale[p * slots + s])
                for s in range(used)
            ]
            for c in range(rows // 16):
                total = [jnp.zeros((16, lanes), f32)] * tiles
                for e, o, weight in entries:
                    keep = lane < o
                    before = jnp.zeros((16, lanes), f32)
                    for m in range(tiles):
                        piece = planes[e, c * 16 : c * 16 + 16, m * lanes : (m + 1) * lanes]
                        turned = pltpu.roll(piece, o, 1).astype(f32)
                        total[m] = total[m] + weight * jnp.where(keep, before, turned)
                        before = turned
                for m in range(tiles):
                    at = m * rows + c * 16
                    out[i, at : at + 16, :] = total[m].astype(bf16)
            cover = jnp.zeros((16, lanes), f32)
            whole = jnp.zeros((16, lanes), f32)
            for e, o, weight in entries:
                cover = cover + jnp.where(lane < o, 0.0, weight)
                whole = whole + weight
            row = lax.broadcasted_iota(jnp.int32, (16, lanes), 0)
            out[i, tiles * rows : tiles * rows + 16, :] = jnp.where(row == 0, cover, whole).astype(bf16)

        used = counts[p]
        for top in range(2, slots + 1, 2):
            low = top - 2 if top > 2 else -1

            @pl.when((used > low) & (used <= top))
            def _():
                some(top)

        return 0

    lax.fori_loop(0, patches // 2, patch, 0)


def pile(core, mine_labels, other_labels, mine, other, patches):
    number, rows, cols = mine.shape
    smem = pl.BlockSpec(memory_space=pltpu.SMEM)
    vmem = pl.BlockSpec(memory_space=pltpu.VMEM)
    length = cols // lanes * rows + 16
    return pl.pallas_call(
        pile_body,
        in_specs=[smem] * 3 + [vmem] * 2,
        out_specs=vmem,
        out_shape=jax.ShapeDtypeStruct((patches // 2, length, lanes), bf16),
        scratch_shapes=[
            pltpu.SMEM((patches,), jnp.int32),
            pltpu.SMEM((patches * 8,), jnp.int32),
            pltpu.SMEM((patches * 8,), jnp.int32),
            pltpu.SMEM((patches * 8,), f32),
            pltpu.VMEM((2 * number, rows, cols), bf16),
        ],
        compiler_params=pltpu.CompilerParams(vmem_limit_bytes=vmem_bytes),
        name="pile",
    )(core, mine_labels, other_labels, mine, other)


def coadd_body(reach, parts, coadd, low, high, stage):
    count = parts.shape[0]
    rows, cols = coadd.shape
    tiles = cols // lanes

    def add(at):
        total = parts[0, at : at + 16, :].astype(f32)
        for n in range(1, count):
            total = total + parts[n, at : at + 16, :].astype(f32)
        return total

    cover = add(tiles * rows)
    scales = [1.0 / jnp.maximum(cover[r : r + 1, :], 1.0) for r in (0, 1)]
    for m in range(tiles):
        for b in range(group):
            value = add(m * rows + b * 16) * scales[min(m, 1)]
            stage[m, pl.ds(b, 16, stride=group), :] = value
    for m in range(tiles):
        cut = slice(m * lanes, (m + 1) * lanes)
        coadd[:, cut] = stage[m]
        low[:, cut] = stage[m, 0:reach, :].astype(bf16)
        high[:, cut] = stage[m, rows - reach : rows, :].astype(bf16)


def coadd_of(parts, rows, cols, reach):
    edge = jax.ShapeDtypeStruct((reach, cols), bf16)
    return pl.pallas_call(
        functools.partial(coadd_body, reach),
        out_shape=(jax.ShapeDtypeStruct((rows, cols), f32), edge, edge),
        scratch_shapes=[pltpu.VMEM((cols // lanes, rows, lanes), f32)],
        compiler_params=pltpu.CompilerParams(vmem_limit_bytes=vmem_bytes),
        name="coadd",
    )(parts)


def detect_body(taps, profile, x, lo, hi, out, frame, lhs, w, stage):
    reach = taps // 2
    rows, cols = x.shape
    count = cols // lanes
    scales = profile.shape[0]
    depth = 112
    mask = band_mask(depth, taps)
    w[...] = jnp.zeros_like(w)
    for s in range(scales):
        for u in range(taps + 1):
            tile = band_tile(profile[s, u : u + 1, :], mask)
            w[u * lanes : u * lanes + depth, 2 * s * lanes : (2 * s + 1) * lanes] = tile
            w[(u + 2) * lanes : (u + 2) * lanes + depth, (2 * s + 1) * lanes : (2 * s + 2) * lanes] = tile
    for ref, row in ((lo, 24 - reach), (x, 24), (hi, 24 + rows)):
        value = ref[...].astype(bf16)
        put_frame(frame, [value[:, m * lanes : (m + 1) * lanes] for m in range(count)], row, reach)
    put_lhs(lhs, frame, taps + 3, 24 - reach)
    lane = lane_ids(16)
    for s in range(scales):
        acc = jnp.dot(
            lhs[...], w[:, 2 * s * lanes : (2 * s + 2) * lanes], preferred_element_type=f32
        )
        for m in range(count):
            for h in range(2):
                even = acc[m * 16 : m * 16 + 16, h * lanes : (h + 1) * lanes]
                odd = acc[(count + m) * 16 : (count + m) * 16 + 16, h * lanes : (h + 1) * lanes]
                for b, part in enumerate(split_rows(even, odd, lane)):
                    stage[m, pl.ds(2 * h + b, 16, stride=group), :] = part
            out[s, :, m * lanes : (m + 1) * lanes] = stage[m]


def detect_of(profile, x, lo, hi, taps):
    rows, cols = x.shape
    scales = profile.shape[0]
    spans = taps + 3
    return pl.pallas_call(
        functools.partial(detect_body, taps),
        out_shape=jax.ShapeDtypeStruct((scales, rows, cols), f32),
        scratch_shapes=[
            pltpu.VMEM((2, cols // lanes, 24 + rows + 24, lanes), f32),
            pltpu.VMEM((256, spans * lanes), bf16),
            pltpu.VMEM((spans * lanes, scales * 256), bf16),
            pltpu.VMEM((cols // lanes, rows, lanes), f32),
        ],
        compiler_params=pltpu.CompilerParams(vmem_limit_bytes=vmem_bytes),
        name="detect",
    )(profile, x, lo, hi)


def on_device(
    exposures,
    coef_code,
    coef_table,
    basis_rows,
    basis_cols,
    exposure_weight,
    intersection_patch,
    intersection_shift,
    psf_kernels,
):
    number, rows, cols = exposures.shape
    taps = basis_rows.shape[1]
    reach = taps // 2
    wide = psf_kernels.shape[-1]
    wide_reach = wide // 2
    sections = lax.axis_size("section")
    across = ("sy", "sx")
    patches = lax.axis_size("sy") * lax.axis_size("sx") * 2
    core = lax.axis_index("core")
    up, down = neighbours(sections)

    lo = lax.ppermute(exposures[:, rows - reach :, :], "section", up)
    hi = lax.ppermute(exposures[:, :reach, :], "section", down)

    labels = jnp.concatenate(
        [exposure_weight[:, None], intersection_patch, intersection_shift], axis=1
    )
    swap = [(0, 1), (1, 0)]
    other_labels = lax.ppermute(labels, "core", swap)

    cols_a, cols_b = profile_rows(basis_cols, taps)
    rows_a = jnp.pad(basis_rows, ((0, 0), (0, 1)))
    rows_b = jnp.pad(basis_rows, ((0, 0), (1, 0)))
    g = rows_a[:, :, None] * cols_a[:, None, :] + rows_b[:, :, None] * cols_b[:, None, :]
    psf_a, psf_b = profile_rows(psf_kernels.astype(f32), wide)
    profile = pad_rows(psf_a, 0, 1) + pad_rows(psf_b, 1, 0)

    matched = match(coef_code, coef_table, g, exposures, lo, hi, taps)
    other = lax.ppermute(matched, "core", swap)
    partial = pile(core[None], labels, other_labels, matched, other, patches)
    parts = lax.all_to_all(partial, across, split_axis=0, concat_axis=0, tiled=True)
    coadd, low, high = coadd_of(parts, rows, cols, wide_reach)
    lo = lax.ppermute(high, "section", up)
    hi = lax.ppermute(low, "section", down)
    detect = detect_of(profile, coadd, lo, hi, wide)
    return (coadd[None], detect[None])


def solution(mesh):
    sections, sky = mesh.devices.shape
    grid = Mesh(mesh.devices.reshape(sections, 4, sky // 8, 2), ("section", "sy", "sx", "core"))
    sky = ("sy", "sx", "core")
    return jax.shard_map(
        on_device,
        mesh=grid,
        in_specs=(
            P(sky, "section", None),
            P(sky, None),
            P(),
            P(),
            P(),
            P(sky),
            P(sky, None),
            P(sky, None),
            P(),
        ),
        out_specs=(P(sky, "section", None), P(sky, None, "section", None)),
        check_vma=False,
    )
```

```python
import functools

import jax
import jax.numpy as jnp
from jax import lax
from jax.experimental import pallas as pl
from jax.experimental.pallas import tpu as pltpu
from jax.sharding import Mesh, PartitionSpec as P

f32 = jnp.float32
bf16 = jnp.bfloat16

lanes = 128
half = 64
group = 4
vmem_bytes = 56 * 1024 * 1024


def one_hot(rows, cols, at):
    row = lax.broadcasted_iota(jnp.int32, (rows, cols), 0)
    col = lax.broadcasted_iota(jnp.int32, (rows, cols), 1)
    return (col == at(row)).astype(f32)


def lane_places(taps):
    first = one_hot(taps, lanes, lambda j: (lanes - j) % lanes)
    second = one_hot(taps, lanes, lambda j: half - j)
    return first, second


def row_places(rows, taps):
    return one_hot(rows, taps, lambda t: t), one_hot(rows, taps, lambda t: t - 1)


def lane_ids(rows):
    return lax.broadcasted_iota(jnp.int32, (rows, lanes), 1)


def band_mask(depth, taps):
    k = lax.broadcasted_iota(jnp.int32, (depth, lanes), 0)
    gap = k - lane_ids(depth) % half
    return (gap >= 0) & (gap < taps)


def band_tile(row, mask):
    depth = mask.shape[0]
    wide = jnp.broadcast_to(row, (depth, lanes))
    turned = pltpu.roll(wide, 0, 1, stride=1, stride_axis=0)
    return jnp.where(mask, turned, 0.0).astype(bf16)


def put_frame(frame, tiles, row, reach):
    count = len(tiles)
    rows = tiles[0].shape[0]
    lane = lane_ids(rows)
    zero = jnp.zeros((rows, lanes), f32)
    right = [pltpu.roll(t, reach, 1).astype(f32) for t in tiles]
    left = [pltpu.roll(t, half + reach, 1).astype(f32) for t in tiles]
    for m in range(count):
        before = right[m - 1] if m else zero
        frame[0, m, row : row + rows, :] = jnp.where(lane < reach, before, right[m])
        after = left[m + 1] if m + 1 < count else zero
        frame[1, m, row : row + rows, :] = jnp.where(lane < half + reach, left[m], after)


def put_lhs(lhs, frame, spans, row):
    tiles = frame.shape[1]
    for t in range(spans):
        for par in range(2):
            for m in range(tiles):
                at = (par * tiles + m) * 16
                piece = frame[par, m, pl.ds(row + t, 16, stride=group), :]
                lhs[at : at + 16, t * lanes : (t + 1) * lanes] = piece.astype(bf16)


def split_rows(even, odd, lane):
    first = jnp.where(lane < half, even, pltpu.roll(odd, half, 1))
    second = jnp.where(lane < half, pltpu.roll(even, half, 1), odd)
    return first, second


def columns(rows):
    return [rows[:, m * lanes : (m + 1) * lanes] for m in range(rows.shape[1] // lanes)]


def put_band(w, profile, taps, mask, first, last, at):
    depth = mask.shape[0]
    for u in range(max(first - 2, 0), min(last, taps + 1)):
        tile = band_tile(profile[u : u + 1, :], mask)
        if u >= first:
            row = (u - first) * lanes
            w[row : row + depth, at : at + lanes] = tile
        if first <= u + 2 < last:
            row = (u + 2 - first) * lanes
            w[row : row + depth, at + lanes : at + 2 * lanes] = tile


def edge_spans(taps):
    return (taps // 2 + 1) // 2 * 2


def put_edge_lhs(lhs, frame, spans):
    tiles = frame.shape[1]
    for t in range(spans):
        for par in range(2):
            for m in range(0, tiles, 2):
                pair = [frame[par, m + i, pl.ds(t, 8, stride=group), :] for i in range(2)]
                at = (par * tiles + m) * 8
                lhs[at : at + 16, t * lanes : (t + 1) * lanes] = jnp.concatenate(pair, axis=0).astype(bf16)


def edge_scratch(taps, tiles, width):
    spans = edge_spans(taps)
    return [
        pltpu.VMEM((2, 2, tiles, 48, lanes), f32),
        pltpu.VMEM((2, 128, spans * lanes), bf16),
        pltpu.VMEM((2, spans * lanes, width), bf16),
    ]


def put_edges(taps, frame, lhs, lo, hi):
    reach = taps // 2
    spans = edge_spans(taps)
    put_frame(frame.at[0], columns(lo), 0, reach)
    put_frame(frame.at[1], columns(hi), 28 - reach + spans, reach)
    for side in range(2):
        put_edge_lhs(lhs.at[side], frame.at[side], spans)


def halo_pair(odd, first, second):
    return jnp.where(odd, first, second), jnp.where(odd, second, first)


def own_body(taps, code, table, base_rows, base_cols, x, acc, profile, g, frame, lhs, w):
    number, rows, _ = x.shape
    basis = base_rows.shape[0]
    reach = taps // 2
    spans = taps + 3
    exact = lax.Precision.HIGHEST
    cols_ab = [
        jnp.dot(base_cols[...], places, precision=exact, preferred_element_type=f32)
        for places in lane_places(taps)
    ]
    rows_ab = [
        lax.dot_general(
            places, base_rows[...], (((1,), (1,)), ((), ())), precision=exact, preferred_element_type=f32
        )
        for places in row_places(taps + 1, taps)
    ]
    for b in range(basis):
        g[b] = sum(r[:, b : b + 1] * c[b : b + 1, :] for r, c in zip(rows_ab, cols_ab))
    frame[...] = jnp.zeros_like(frame)
    w[...] = jnp.zeros_like(w)
    mask = band_mask(96, taps)

    def one(e, way):
        total = jnp.zeros(g.shape[1:], f32)
        for b in range(basis):
            total = total + table[b, code[e, b]] * g[b]
        total = total.astype(bf16).astype(f32)
        profile[e] = total
        put_band(w.at[way], total, taps, mask, 0, spans, 0)
        put_frame(frame.at[way], columns(x[e]), 16, reach)
        put_lhs(lhs.at[way], frame.at[way], spans, 16 - reach)
        acc[e] = jnp.dot(lhs[way], w[way], preferred_element_type=f32)

    def some(i, _):
        for way in range(ways):
            one(ways * i + way, way)
        return 0

    lax.fori_loop(0, number // ways, some, 0)


ways = 2


def match_own(code, table, base_rows, base_cols, x):
    number, rows, cols = x.shape
    basis, taps = base_rows.shape
    smem = pl.BlockSpec(memory_space=pltpu.SMEM)
    vmem = pl.BlockSpec(memory_space=pltpu.VMEM)
    spans = taps + 3
    return pl.pallas_call(
        functools.partial(own_body, taps),
        in_specs=[smem, smem, vmem, vmem, vmem],
        out_specs=(vmem, vmem),
        out_shape=(
            jax.ShapeDtypeStruct((number, 256, 256), f32),
            jax.ShapeDtypeStruct((number, taps + 1, lanes), f32),
        ),
        scratch_shapes=[
            pltpu.VMEM((basis, taps + 1, lanes), f32),
            pltpu.VMEM((ways, 2, cols // lanes, 96, lanes), f32),
            pltpu.VMEM((ways, 256, spans * lanes), bf16),
            pltpu.VMEM((ways, spans * lanes, 256), bf16),
        ],
        compiler_params=pltpu.CompilerParams(vmem_limit_bytes=vmem_bytes),
        cost_estimate=pl.CostEstimate(
            flops=number * 2 * 256 * 256 * spans * lanes, bytes_accessed=4 * x.size, transcendentals=0
        ),
        name="match_own",
    )(code, table, base_rows, base_cols, x)


def halo_body(taps, odd, profile, first, second, acc, out, frame, lhs, w):
    number, _, cols = out.shape
    count = cols // lanes
    spans = edge_spans(taps)
    frame[...] = jnp.zeros_like(frame)
    w[...] = jnp.zeros_like(w)
    mask = band_mask(96, taps)
    lane = lane_ids(16)

    def one(e, way):
        band = profile[e]
        put_band(w.at[way, 0], band, taps, mask, 0, spans, 0)
        put_band(w.at[way, 1], band, taps, mask, taps + 3 - spans, taps + 3, 0)
        lo, hi = halo_pair(odd[0] == 1, first[e], second[e])
        put_edges(taps, frame.at[way], lhs.at[way], lo, hi)
        ends = [
            jnp.dot(lhs[way, side], w[way, side], preferred_element_type=f32) for side in range(2)
        ]
        for m in range(count):
            for h in range(2):
                cut = slice(h * lanes, (h + 1) * lanes)
                blocks = []
                for n in (m, count + m):
                    more = jnp.concatenate([end[n * 8 : n * 8 + 8, cut] for end in ends], axis=0)
                    blocks.append(acc[e, n * 16 : n * 16 + 16, cut] + more)
                for b, part in enumerate(split_rows(*blocks, lane)):
                    at = (2 * h + b) * 16
                    out[e, at : at + 16, m * lanes : (m + 1) * lanes] = part.astype(bf16)

    def some(i, _):
        for way in range(ways):
            one(ways * i + way, way)
        return 0

    lax.fori_loop(0, number // ways, some, 0)


def match_halo(odd, profile, first, second, acc, rows, taps):
    number, _, cols = first.shape
    smem = pl.BlockSpec(memory_space=pltpu.SMEM)
    vmem = pl.BlockSpec(memory_space=pltpu.VMEM)
    scratch = edge_scratch(taps, cols // lanes, 256)
    return pl.pallas_call(
        functools.partial(halo_body, taps),
        in_specs=[smem, vmem, vmem, vmem, vmem],
        out_specs=vmem,
        out_shape=jax.ShapeDtypeStruct((number, rows, cols), bf16),
        scratch_shapes=[pltpu.VMEM((ways,) + each.shape, each.dtype) for each in scratch],
        compiler_params=pltpu.CompilerParams(vmem_limit_bytes=vmem_bytes),
        name="match_halo",
    )(odd, profile, first, second, acc)


def pile_body(core, mine_labels, other_labels, mine, other, out, counts, source, offset, scale, planes):
    number, rows, cols = mine.shape
    tiles = cols // lanes
    per = (mine_labels.shape[1] - 1) // 2
    patches = counts.shape[0]
    slots = 8

    def clear(p, _):
        counts[p] = 0
        for s in range(slots):
            source[p * slots + s] = 0
            offset[p * slots + s] = 0
            scale[p * slots + s] = 0.0
        return 0

    lax.fori_loop(0, patches, clear, 0)

    def enter(base, labels):
        def one(e, _):
            weight = labels[e, 0].astype(f32)
            for k in range(per):
                p = labels[e, 1 + k]
                at = counts[p]
                source[p * slots + at] = base + e
                offset[p * slots + at] = labels[e, 1 + per + k]
                scale[p * slots + at] = weight
                counts[p] = at + 1
            return 0

        lax.fori_loop(0, number, one, 0)

    enter(0, mine_labels)
    enter(number, other_labels)
    planes[0:number] = mine[...]
    planes[number:] = other[...]
    lane = lane_ids(16)

    def patch(i, _):
        p = 2 * i + core[0]

        def some(used):
            entries = [
                (source[p * slots + s], offset[p * slots + s], scale[p * slots + s])
                for s in range(used)
            ]
            for c in range(rows // 16):
                total = [jnp.zeros((16, lanes), f32)] * tiles
                for e, o, weight in entries:
                    keep = lane < o
                    before = jnp.zeros((16, lanes), f32)
                    for m in range(tiles):
                        piece = planes[e, c * 16 : c * 16 + 16, m * lanes : (m + 1) * lanes]
                        turned = pltpu.roll(piece, o, 1).astype(f32)
                        total[m] = total[m] + weight * jnp.where(keep, before, turned)
                        before = turned
                for m in range(tiles):
                    at = m * rows + c * 16
                    out[i, at : at + 16, :] = total[m].astype(bf16)
            cover = jnp.zeros((16, lanes), f32)
            whole = jnp.zeros((16, lanes), f32)
            for e, o, weight in entries:
                cover = cover + jnp.where(lane < o, 0.0, weight)
                whole = whole + weight
            row = lax.broadcasted_iota(jnp.int32, (16, lanes), 0)
            out[i, tiles * rows : tiles * rows + 16, :] = jnp.where(row == 0, cover, whole).astype(bf16)

        used = counts[p]
        for top in range(2, slots + 1, 2):
            low = top - 2 if top > 2 else -1

            @pl.when((used > low) & (used <= top))
            def _():
                some(top)

        return 0

    lax.fori_loop(0, patches // 2, patch, 0)


def pile(core, mine_labels, other_labels, mine, other, patches):
    number, rows, cols = mine.shape
    smem = pl.BlockSpec(memory_space=pltpu.SMEM)
    vmem = pl.BlockSpec(memory_space=pltpu.VMEM)
    length = cols // lanes * rows + 16
    return pl.pallas_call(
        pile_body,
        in_specs=[smem] * 3 + [vmem] * 2,
        out_specs=vmem,
        out_shape=jax.ShapeDtypeStruct((patches // 2, length, lanes), bf16),
        scratch_shapes=[
            pltpu.SMEM((patches,), jnp.int32),
            pltpu.SMEM((patches * 8,), jnp.int32),
            pltpu.SMEM((patches * 8,), jnp.int32),
            pltpu.SMEM((patches * 8,), f32),
            pltpu.VMEM((2 * number, rows, cols), bf16),
        ],
        compiler_params=pltpu.CompilerParams(vmem_limit_bytes=vmem_bytes),
        name="pile",
    )(core, mine_labels, other_labels, mine, other)


def coadd_body(reach, odd, parts, coadd, first, second, stage):
    count = parts.shape[0]
    rows, cols = coadd.shape
    tiles = cols // lanes

    def add(at):
        total = parts[0, at : at + 16, :].astype(f32)
        for n in range(1, count):
            total = total + parts[n, at : at + 16, :].astype(f32)
        return total

    cover = add(tiles * rows)
    scales = [1.0 / jnp.maximum(cover[r : r + 1, :], 1.0) for r in (0, 1)]
    for m in range(tiles):
        for b in range(group):
            value = add(m * rows + b * 16) * scales[min(m, 1)]
            stage[m, pl.ds(b, 16, stride=group), :] = value
    for m in range(tiles):
        cut = slice(m * lanes, (m + 1) * lanes)
        coadd[:, cut] = stage[m]
        low = stage[m, 0:reach, :]
        high = stage[m, rows - reach : rows, :]
        first[:, cut] = jnp.where(odd[0] == 1, low, high).astype(bf16)
        second[:, cut] = jnp.where(odd[0] == 1, high, low).astype(bf16)


def coadd_of(odd, parts, rows, cols, reach):
    edge = jax.ShapeDtypeStruct((reach, cols), bf16)
    smem = pl.BlockSpec(memory_space=pltpu.SMEM)
    vmem = pl.BlockSpec(memory_space=pltpu.VMEM)
    return pl.pallas_call(
        functools.partial(coadd_body, reach),
        in_specs=[smem, vmem],
        out_specs=(vmem, vmem, vmem),
        out_shape=(jax.ShapeDtypeStruct((rows, cols), f32), edge, edge),
        scratch_shapes=[pltpu.VMEM((cols // lanes, rows, lanes), f32)],
        compiler_params=pltpu.CompilerParams(vmem_limit_bytes=vmem_bytes),
        name="coadd",
    )(odd, parts)


def detect_own_body(taps, psf, x, acc, profile, frame, lhs, w):
    reach = taps // 2
    rows, cols = x.shape
    spans = taps + 3
    mask = band_mask(112, taps)
    frame[...] = jnp.zeros_like(frame)
    put_frame(frame, columns(x[...].astype(bf16)), 24, reach)
    put_lhs(lhs, frame, spans, 24 - reach)
    w[...] = jnp.zeros_like(w)
    for s in range(psf.shape[0]):
        total = 0.0
        for rows_at, cols_at in zip(row_places(profile.shape[1], taps), lane_places(taps)):
            moved = jnp.dot(rows_at.astype(bf16), psf[s], preferred_element_type=f32)
            total = total + jnp.dot(
                moved.astype(bf16), cols_at.astype(bf16), preferred_element_type=f32
            )
        profile[s] = total
        put_band(w, total, taps, mask, 0, spans, 256 * s)
        cut = slice(256 * s, 256 * s + 256)
        acc[:, cut] = jnp.dot(lhs[...], w[:, cut], preferred_element_type=f32)


def detect_own(psf, x):
    rows, cols = x.shape
    scales, _, taps = psf.shape
    spans = taps + 3
    return pl.pallas_call(
        functools.partial(detect_own_body, taps),
        out_shape=(
            jax.ShapeDtypeStruct((256, scales * 256), f32),
            jax.ShapeDtypeStruct((scales, 48, lanes), f32),
        ),
        scratch_shapes=[
            pltpu.VMEM((2, cols // lanes, 24 + rows + 24, lanes), f32),
            pltpu.VMEM((256, spans * lanes), bf16),
            pltpu.VMEM((spans * lanes, scales * 256), bf16),
        ],
        compiler_params=pltpu.CompilerParams(vmem_limit_bytes=vmem_bytes),
        cost_estimate=pl.CostEstimate(
            flops=scales * 2 * 256 * 256 * spans * lanes, bytes_accessed=4 * x.size, transcendentals=0
        ),
        name="detect_own",
    )(psf, x)


def detect_halo_body(taps, odd, profile, first, second, acc, out, frame, lhs, w, stage):
    scales, rows, cols = out.shape
    count = cols // lanes
    spans = edge_spans(taps)
    frame[...] = jnp.zeros_like(frame)
    w[...] = jnp.zeros_like(w)
    mask = band_mask(112, taps)
    lane = lane_ids(16)
    lo, hi = halo_pair(odd[0] == 1, first[...], second[...])
    put_edges(taps, frame, lhs, lo, hi)
    for s in range(scales):
        at = 256 * s
        put_band(w.at[0], profile[s], taps, mask, 0, spans, at)
        put_band(w.at[1], profile[s], taps, mask, taps + 3 - spans, taps + 3, at)
        ends = [
            jnp.dot(lhs[side], w[side, :, at : at + 256], preferred_element_type=f32)
            for side in range(2)
        ]
        for m in range(count):
            for h in range(2):
                cut = slice(h * lanes, (h + 1) * lanes)
                blocks = []
                for n in (m, count + m):
                    more = jnp.concatenate([end[n * 8 : n * 8 + 8, cut] for end in ends], axis=0)
                    own = acc[n * 16 : n * 16 + 16, at + h * lanes : at + (h + 1) * lanes]
                    blocks.append(own + more)
                for b, part in enumerate(split_rows(*blocks, lane)):
                    stage[s, m, pl.ds(2 * h + b, 16, stride=group), :] = part
            out[s, :, m * lanes : (m + 1) * lanes] = stage[s, m]


def detect_halo(odd, profile, first, second, acc, rows, taps):
    cols = first.shape[1]
    scales = profile.shape[0]
    smem = pl.BlockSpec(memory_space=pltpu.SMEM)
    vmem = pl.BlockSpec(memory_space=pltpu.VMEM)
    return pl.pallas_call(
        functools.partial(detect_halo_body, taps),
        in_specs=[smem, vmem, vmem, vmem, vmem],
        out_specs=vmem,
        out_shape=jax.ShapeDtypeStruct((scales, rows, cols), f32),
        scratch_shapes=edge_scratch(taps, cols // lanes, scales * 256)
        + [pltpu.VMEM((scales, cols // lanes, rows, lanes), f32)],
        compiler_params=pltpu.CompilerParams(vmem_limit_bytes=vmem_bytes),
        name="detect_halo",
    )(odd, profile, first, second, acc)


def trade(first, second):
    count = lax.axis_size("section")
    out = []
    for start, rows in ((0, first), (1, second)):
        pairs = [(i, i + 1) for i in range(start, count - 1, 2)]
        out.append(lax.ppermute(rows, "section", pairs + [(b, a) for a, b in pairs]))
    return out


def on_device(
    exposures,
    coef_code,
    coef_table,
    basis_rows,
    basis_cols,
    exposure_weight,
    intersection_patch,
    intersection_shift,
    psf_kernels,
):
    number, rows, cols = exposures.shape
    taps = basis_rows.shape[1]
    reach = taps // 2
    wide = psf_kernels.shape[-1]
    wide_reach = wide // 2
    across = ("sy", "sx")
    patches = lax.axis_size("sy") * lax.axis_size("sx") * 2
    core = lax.axis_index("core")
    odd = lax.axis_index("section") % 2

    low, high = exposures[:, :reach, :], exposures[:, rows - reach :, :]
    first, second = trade(jnp.where(odd == 1, low, high), jnp.where(odd == 1, high, low))
    odd = odd[None]

    labels = jnp.concatenate(
        [exposure_weight[:, None], intersection_patch, intersection_shift], axis=1
    )
    swap = [(0, 1), (1, 0)]
    other_labels = lax.ppermute(labels, "core", swap)

    acc, profile = match_own(coef_code, coef_table, basis_rows, basis_cols, exposures)
    matched = match_halo(odd, profile, first, second, acc, rows, taps)
    other = lax.ppermute(matched, "core", swap)
    partial = pile(core[None], labels, other_labels, matched, other, patches)
    parts = lax.all_to_all(partial, across, split_axis=0, concat_axis=0, tiled=True)
    coadd, first, second = coadd_of(odd, parts, rows, cols, wide_reach)
    first, second = trade(first, second)
    acc, profile = detect_own(psf_kernels, coadd)
    detect = detect_halo(odd, profile, first, second, acc, rows, wide)
    return (coadd[None], detect[None])


def solution(mesh):
    sections, sky = mesh.devices.shape
    grid = Mesh(mesh.devices.reshape(sections, 4, sky // 8, 2), ("section", "sy", "sx", "core"))
    sky = ("sy", "sx", "core")
    return jax.shard_map(
        on_device,
        mesh=grid,
        in_specs=(
            P(sky, "section", None),
            P(sky, None),
            P(),
            P(),
            P(),
            P(sky),
            P(sky, None),
            P(sky, None),
            P(),
        ),
        out_specs=(P(sky, "section", None), P(sky, None, "section", None)),
        check_vma=False,
    )
```

```python
import functools

import jax
import jax.numpy as jnp
from jax import lax
from jax.experimental import pallas as pl
from jax.experimental.pallas import tpu as pltpu
from jax.sharding import Mesh, PartitionSpec as P

f32 = jnp.float32
bf16 = jnp.bfloat16

lanes = 128
half = 64
group = 4
vmem_bytes = 56 * 1024 * 1024


def profile_rows(profile, taps):
    lead = profile.shape[:-1]
    zeros = lambda n: jnp.zeros(lead + (n,), profile.dtype)
    first = jnp.concatenate(
        [profile[..., :1], zeros(lanes - taps), profile[..., :0:-1]], axis=-1
    )
    second = jnp.concatenate(
        [zeros(half - taps + 1), profile[..., ::-1], zeros(lanes - half - 1)], axis=-1
    )
    return first, second


def one_hot(rows, cols, at):
    row = lax.broadcasted_iota(jnp.int32, (rows, cols), 0)
    col = lax.broadcasted_iota(jnp.int32, (rows, cols), 1)
    return (col == at(row)).astype(f32)


def lane_places(taps):
    first = one_hot(taps, lanes, lambda j: (lanes - j) % lanes)
    second = one_hot(taps, lanes, lambda j: half - j)
    return first, second


def row_places(rows, taps):
    return one_hot(rows, taps, lambda t: t), one_hot(rows, taps, lambda t: t - 1)


def lane_ids(rows):
    return lax.broadcasted_iota(jnp.int32, (rows, lanes), 1)


def band_mask(depth, taps):
    k = lax.broadcasted_iota(jnp.int32, (depth, lanes), 0)
    gap = k - lane_ids(depth) % half
    return (gap >= 0) & (gap < taps)


def band_tile(row, mask):
    depth = mask.shape[0]
    wide = jnp.broadcast_to(row, (depth, lanes))
    turned = pltpu.roll(wide, 0, 1, stride=1, stride_axis=0)
    return jnp.where(mask, turned, 0.0).astype(bf16)


def put_frame(frame, tiles, row, reach):
    count = len(tiles)
    rows = tiles[0].shape[0]
    lane = lane_ids(rows)
    zero = jnp.zeros((rows, lanes), f32)
    right = [pltpu.roll(t, reach, 1).astype(f32) for t in tiles]
    left = [pltpu.roll(t, half + reach, 1).astype(f32) for t in tiles]
    for m in range(count):
        before = right[m - 1] if m else zero
        frame[0, m, row : row + rows, :] = jnp.where(lane < reach, before, right[m])
        after = left[m + 1] if m + 1 < count else zero
        frame[1, m, row : row + rows, :] = jnp.where(lane < half + reach, left[m], after)


def put_lhs(lhs, frame, spans, row):
    tiles = frame.shape[1]
    for t in range(spans):
        for par in range(2):
            for m in range(tiles):
                at = (par * tiles + m) * 16
                piece = frame[par, m, pl.ds(row + t, 16, stride=group), :]
                lhs[at : at + 16, t * lanes : (t + 1) * lanes] = piece.astype(bf16)


def split_rows(even, odd, lane):
    first = jnp.where(lane < half, even, pltpu.roll(odd, half, 1))
    second = jnp.where(lane < half, pltpu.roll(even, half, 1), odd)
    return first, second


def columns(rows):
    return [rows[:, m * lanes : (m + 1) * lanes] for m in range(rows.shape[1] // lanes)]


def put_band(w, profile, taps, mask, first, last, at):
    depth = mask.shape[0]
    for u in range(max(first - 2, 0), min(last, taps + 1)):
        tile = band_tile(profile[u : u + 1, :], mask)
        if u >= first:
            row = (u - first) * lanes
            w[row : row + depth, at : at + lanes] = tile
        if first <= u + 2 < last:
            row = (u + 2 - first) * lanes
            w[row : row + depth, at + lanes : at + 2 * lanes] = tile


def clear_band(w, taps, depth, first, last):
    width = w.shape[1]
    for t in range(first, last):
        row = (t - first) * lanes
        w[row + depth : row + lanes, :] = jnp.zeros((lanes - depth, width), bf16)
        for u, at in ((t, 0), (t - 2, lanes)):
            if not 0 <= u <= taps:
                for n in range(at, width, 2 * lanes):
                    w[row : row + depth, n : n + lanes] = jnp.zeros((depth, lanes), bf16)


def edge_spans(taps):
    return (taps // 2 + 1) // 2 * 2


def put_edge_lhs(lhs, frame, spans):
    tiles = frame.shape[1]
    for t in range(spans):
        for par in range(2):
            for m in range(0, tiles, 2):
                pair = [frame[par, m + i, pl.ds(t, 8, stride=group), :] for i in range(2)]
                at = (par * tiles + m) * 8
                lhs[at : at + 16, t * lanes : (t + 1) * lanes] = jnp.concatenate(pair, axis=0).astype(bf16)


def edge_scratch(taps, tiles, width):
    spans = edge_spans(taps)
    return [
        pltpu.VMEM((2, 2, tiles, 48, lanes), f32),
        pltpu.VMEM((2, 128, spans * lanes), bf16),
        pltpu.VMEM((2, spans * lanes, width), bf16),
    ]


def put_edges(taps, frame, lhs, lo, hi):
    reach = taps // 2
    spans = edge_spans(taps)
    put_frame(frame.at[0], columns(lo), 0, reach)
    put_frame(frame.at[1], columns(hi), 28 - reach + spans, reach)
    for side in range(2):
        put_edge_lhs(lhs.at[side], frame.at[side], spans)


def halo_pair(odd, first, second):
    return jnp.where(odd, first, second), jnp.where(odd, second, first)


ways = 4


def match_body(taps, odd, code, table, g, x, first, second, out, frame, lhs, w):
    number, _, cols = x.shape
    reach = taps // 2
    spans = taps + 3
    count = cols // lanes
    depth = 96
    mask = band_mask(depth, taps)
    lane = lane_ids(16)
    for way in range(ways):
        clear_band(w.at[way], taps, depth, 0, spans)

    def one(e, way):
        total = jnp.zeros(g.shape[1:], f32)
        for b in range(g.shape[0]):
            total = total + table[b, code[e, b]] * g[b]
        total = total.astype(bf16).astype(f32)
        put_band(w.at[way], total, taps, mask, 0, spans, 0)
        lo, hi = halo_pair(odd[0] == 1, first[e], second[e])
        for piece, row in ((lo, 16 - reach), (x[e], 16), (hi, 80)):
            put_frame(frame.at[way], columns(piece), row, reach)
        put_lhs(lhs.at[way], frame.at[way], spans, 16 - reach)
        acc = jnp.dot(lhs[way], w[way], preferred_element_type=f32)
        for m in range(count):
            for h in range(2):
                cut = slice(h * lanes, (h + 1) * lanes)
                blocks = [acc[n * 16 : n * 16 + 16, cut] for n in (m, count + m)]
                for b, part in enumerate(split_rows(*blocks, lane)):
                    at = (2 * h + b) * 16
                    out[e, at : at + 16, m * lanes : (m + 1) * lanes] = part.astype(bf16)

    def some(i, _):
        for way in range(ways):
            one(ways * i + way, way)
        return 0

    lax.fori_loop(0, number // ways, some, 0)


def match(odd, code, table, g, x, first, second, taps):
    number, rows, cols = x.shape
    smem = pl.BlockSpec(memory_space=pltpu.SMEM)
    vmem = pl.BlockSpec(memory_space=pltpu.VMEM)
    spans = taps + 3
    return pl.pallas_call(
        functools.partial(match_body, taps),
        in_specs=[smem, smem, smem, vmem, vmem, vmem, vmem],
        out_specs=vmem,
        out_shape=jax.ShapeDtypeStruct((number, rows, cols), bf16),
        scratch_shapes=[
            pltpu.VMEM((ways, 2, cols // lanes, 96, lanes), f32),
            pltpu.VMEM((ways, 256, spans * lanes), bf16),
            pltpu.VMEM((ways, spans * lanes, 256), bf16),
        ],
        compiler_params=pltpu.CompilerParams(vmem_limit_bytes=vmem_bytes),
        cost_estimate=pl.CostEstimate(
            flops=number * 2 * 256 * 256 * spans * lanes, bytes_accessed=4 * x.size, transcendentals=0
        ),
        name="match",
    )(odd, code, table, g, x, first, second)


slots = 8


def slot_body(mine, other, out):
    number = mine.shape[0]
    per = (mine.shape[1] - 1) // 2
    patches = out.shape[0] // (slots + 1)

    def clear(p, _):
        out[p] = 0
        for s in range(slots):
            out[patches + p * slots + s] = 0
        return 0

    lax.fori_loop(0, patches, clear, 0)
    for base, labels in ((0, mine), (number, other)):

        def one(e, _):
            plane = (labels[e, 0] * 2 * number + base + e) * 256
            for k in range(per):
                p = labels[e, 1 + k]
                at = out[p]
                out[patches + p * slots + at] = plane + labels[e, 1 + per + k]
                out[p] = at + 1
            return 0

        lax.fori_loop(0, number, one, 0)


def slot_table(mine, other, patches):
    smem = pl.BlockSpec(memory_space=pltpu.SMEM)
    return pl.pallas_call(
        slot_body,
        in_specs=[smem, smem],
        out_specs=smem,
        out_shape=jax.ShapeDtypeStruct((patches * (slots + 1),), jnp.int32),
        name="slot_table",
    )(mine, other)


def pile_body(core, table, mine, other, out, planes, done, arrive, leave):
    number, rows, cols = mine.shape
    tiles = cols // lanes
    patches = table.shape[0] // (slots + 1)
    come = [
        pltpu.make_async_copy(ref, planes.at[pl.ds(i * number, number)], arrive.at[i])
        for i, ref in enumerate((mine, other))
    ]
    for copy in come:
        copy.start()
    for copy in come:
        copy.wait()
    lane = lane_ids(16)

    def patch(i, _):
        p = 2 * i + core[0]

        def some(used):
            entries = []
            for s in range(used):
                word = table[patches + p * slots + s]
                plane = word // 256
                entries.append(
                    (plane % (2 * number), word % 256, (plane // (2 * number)).astype(f32))
                )
            for c in range(rows // 16):
                total = [jnp.zeros((16, lanes), f32)] * tiles
                for e, o, weight in entries:
                    keep = lane < o
                    before = jnp.zeros((16, lanes), f32)
                    for m in range(tiles):
                        piece = planes[e, c * 16 : c * 16 + 16, m * lanes : (m + 1) * lanes]
                        turned = pltpu.roll(piece, o, 1).astype(f32)
                        total[m] = total[m] + weight * jnp.where(keep, before, turned)
                        before = turned
                for m in range(tiles):
                    at = m * rows + c * 16
                    done[i, at : at + 16, :] = total[m].astype(bf16)
            cover = jnp.zeros((16, lanes), f32)
            whole = jnp.zeros((16, lanes), f32)
            for e, o, weight in entries:
                cover = cover + jnp.where(lane < o, 0.0, weight)
                whole = whole + weight
            row = lax.broadcasted_iota(jnp.int32, (16, lanes), 0)
            done[i, tiles * rows : tiles * rows + 16, :] = jnp.where(row == 0, cover, whole).astype(bf16)

        used = table[p]
        for top in range(2, slots + 1, 2):
            low = top - 2 if top > 2 else -1

            @pl.when((used > low) & (used <= top))
            def _():
                some(top)

        pltpu.make_async_copy(done.at[i], out.at[i], leave.at[i]).start()
        return 0

    lax.fori_loop(0, patches // 2, patch, 0)

    def wait(i, _):
        pltpu.make_async_copy(done.at[i], out.at[i], leave.at[i]).wait()
        return 0

    lax.fori_loop(0, patches // 2, wait, 0)


def pile(core, table, mine, other):
    number, rows, cols = mine.shape
    patches = table.shape[0] // (slots + 1)
    smem = pl.BlockSpec(memory_space=pltpu.SMEM)
    far = pl.BlockSpec(memory_space=pl.ANY)
    shape = (patches // 2, cols // lanes * rows + 16, lanes)
    return pl.pallas_call(
        pile_body,
        in_specs=[smem, smem, far, far],
        out_specs=far,
        out_shape=jax.ShapeDtypeStruct(shape, bf16),
        scratch_shapes=[
            pltpu.VMEM((2 * number, rows, cols), bf16),
            pltpu.VMEM(shape, bf16),
            pltpu.SemaphoreType.DMA((2,)),
            pltpu.SemaphoreType.DMA((patches // 2,)),
        ],
        compiler_params=pltpu.CompilerParams(vmem_limit_bytes=vmem_bytes),
        name="pile",
    )(core, table, mine, other)


def coadd_body(reach, odd, far, coadd, first, second, parts, stage, arrive):
    count = parts.shape[0]
    rows, cols = coadd.shape
    tiles = cols // lanes
    starts = [tiles * rows] + [m * rows for m in range(tiles)]
    ends = [tiles * rows + 16] + [m * rows + rows for m in range(tiles)]
    come = []
    for i, (start, end) in enumerate(zip(starts, ends)):
        span = pl.ds(start, end - start)
        come.append(pltpu.make_async_copy(far.at[:, span, :], parts.at[:, span, :], arrive.at[i]))
        come[i].start()

    def add(at):
        total = parts[0, at : at + 16, :].astype(f32)
        for n in range(1, count):
            total = total + parts[n, at : at + 16, :].astype(f32)
        return total

    come[0].wait()
    cover = add(tiles * rows)
    scales = [1.0 / jnp.maximum(cover[r : r + 1, :], 1.0) for r in (0, 1)]
    for m in range(tiles):
        come[m + 1].wait()
        for b in range(group):
            value = add(m * rows + b * 16) * scales[min(m, 1)]
            stage[m, pl.ds(b, 16, stride=group), :] = value
        cut = slice(m * lanes, (m + 1) * lanes)
        coadd[:, cut] = stage[m]
        low = stage[m, 0:reach, :]
        high = stage[m, rows - reach : rows, :]
        first[:, cut] = jnp.where(odd[0] == 1, low, high).astype(bf16)
        second[:, cut] = jnp.where(odd[0] == 1, high, low).astype(bf16)


def coadd_of(odd, parts, rows, cols, reach):
    edge = jax.ShapeDtypeStruct((reach, cols), bf16)
    smem = pl.BlockSpec(memory_space=pltpu.SMEM)
    vmem = pl.BlockSpec(memory_space=pltpu.VMEM)
    return pl.pallas_call(
        functools.partial(coadd_body, reach),
        in_specs=[smem, pl.BlockSpec(memory_space=pl.ANY)],
        out_specs=(vmem, vmem, vmem),
        out_shape=(jax.ShapeDtypeStruct((rows, cols), f32), edge, edge),
        scratch_shapes=[
            pltpu.VMEM(parts.shape, bf16),
            pltpu.VMEM((cols // lanes, rows, lanes), f32),
            pltpu.SemaphoreType.DMA((cols // lanes + 1,)),
        ],
        compiler_params=pltpu.CompilerParams(vmem_limit_bytes=vmem_bytes),
        name="coadd",
    )(odd, parts)


def detect_own_body(taps, psf, x, acc, profile, frame, lhs, w):
    reach = taps // 2
    rows, cols = x.shape
    spans = taps + 3
    mask = band_mask(112, taps)
    for row in (0, 24 + rows):
        frame[:, :, row : row + 24, :] = jnp.zeros((2, cols // lanes, 24, lanes), f32)
    put_frame(frame, columns(x[...].astype(bf16)), 24, reach)
    put_lhs(lhs, frame, spans, 24 - reach)
    clear_band(w, taps, 112, 0, spans)
    for s in range(psf.shape[0]):
        total = 0.0
        for rows_at, cols_at in zip(row_places(profile.shape[1], taps), lane_places(taps)):
            moved = jnp.dot(rows_at.astype(bf16), psf[s], preferred_element_type=f32)
            total = total + jnp.dot(
                moved.astype(bf16), cols_at.astype(bf16), preferred_element_type=f32
            )
        profile[s] = total
        put_band(w, total, taps, mask, 0, spans, 256 * s)
        cut = slice(256 * s, 256 * s + 256)
        acc[:, cut] = jnp.dot(lhs[...], w[:, cut], preferred_element_type=f32)


def detect_own(psf, x):
    rows, cols = x.shape
    scales, _, taps = psf.shape
    spans = taps + 3
    return pl.pallas_call(
        functools.partial(detect_own_body, taps),
        out_shape=(
            jax.ShapeDtypeStruct((256, scales * 256), f32),
            jax.ShapeDtypeStruct((scales, 48, lanes), f32),
        ),
        scratch_shapes=[
            pltpu.VMEM((2, cols // lanes, 24 + rows + 24, lanes), f32),
            pltpu.VMEM((256, spans * lanes), bf16),
            pltpu.VMEM((spans * lanes, scales * 256), bf16),
        ],
        compiler_params=pltpu.CompilerParams(vmem_limit_bytes=vmem_bytes),
        cost_estimate=pl.CostEstimate(
            flops=scales * 2 * 256 * 256 * spans * lanes, bytes_accessed=4 * x.size, transcendentals=0
        ),
        name="detect_own",
    )(psf, x)


def detect_halo_body(taps, odd, profile, first, second, acc, out, frame, lhs, w, stage):
    scales, rows, cols = out.shape
    count = cols // lanes
    spans = edge_spans(taps)
    frame[...] = jnp.zeros_like(frame)
    clear_band(w.at[0], taps, 112, 0, spans)
    clear_band(w.at[1], taps, 112, taps + 3 - spans, taps + 3)
    mask = band_mask(112, taps)
    lane = lane_ids(16)
    lo, hi = halo_pair(odd[0] == 1, first[...], second[...])
    put_edges(taps, frame, lhs, lo, hi)
    for s in range(scales):
        at = 256 * s
        put_band(w.at[0], profile[s], taps, mask, 0, spans, at)
        put_band(w.at[1], profile[s], taps, mask, taps + 3 - spans, taps + 3, at)
        ends = [
            jnp.dot(lhs[side], w[side, :, at : at + 256], preferred_element_type=f32)
            for side in range(2)
        ]
        for m in range(count):
            for h in range(2):
                cut = slice(h * lanes, (h + 1) * lanes)
                blocks = []
                for n in (m, count + m):
                    more = jnp.concatenate([end[n * 8 : n * 8 + 8, cut] for end in ends], axis=0)
                    own = acc[n * 16 : n * 16 + 16, at + h * lanes : at + (h + 1) * lanes]
                    blocks.append(own + more)
                for b, part in enumerate(split_rows(*blocks, lane)):
                    stage[s, m, pl.ds(2 * h + b, 16, stride=group), :] = part
            out[s, :, m * lanes : (m + 1) * lanes] = stage[s, m]


def detect_halo(odd, profile, first, second, acc, rows, taps):
    cols = first.shape[1]
    scales = profile.shape[0]
    smem = pl.BlockSpec(memory_space=pltpu.SMEM)
    vmem = pl.BlockSpec(memory_space=pltpu.VMEM)
    return pl.pallas_call(
        functools.partial(detect_halo_body, taps),
        in_specs=[smem, vmem, vmem, vmem, vmem],
        out_specs=vmem,
        out_shape=jax.ShapeDtypeStruct((scales, rows, cols), f32),
        scratch_shapes=edge_scratch(taps, cols // lanes, scales * 256)
        + [pltpu.VMEM((scales, cols // lanes, rows, lanes), f32)],
        compiler_params=pltpu.CompilerParams(vmem_limit_bytes=vmem_bytes),
        name="detect_halo",
    )(odd, profile, first, second, acc)


def trade(first, second):
    count = lax.axis_size("section")
    out = []
    for start, rows in ((0, first), (1, second)):
        pairs = [(i, i + 1) for i in range(start, count - 1, 2)]
        out.append(lax.ppermute(rows, "section", pairs + [(b, a) for a, b in pairs]))
    return out


def on_device(
    exposures,
    coef_code,
    coef_table,
    basis_rows,
    basis_cols,
    exposure_weight,
    intersection_patch,
    intersection_shift,
    psf_kernels,
):
    number, rows, cols = exposures.shape
    taps = basis_rows.shape[1]
    reach = taps // 2
    wide = psf_kernels.shape[-1]
    wide_reach = wide // 2
    across = ("sy", "sx")
    patches = lax.axis_size("sy") * lax.axis_size("sx") * 2
    core = lax.axis_index("core")
    odd = lax.axis_index("section") % 2

    low, high = exposures[:, :reach, :], exposures[:, rows - reach :, :]
    first, second = trade(jnp.where(odd == 1, low, high), jnp.where(odd == 1, high, low))
    odd = odd[None]

    labels = jnp.concatenate(
        [exposure_weight[:, None], intersection_patch, intersection_shift], axis=1
    )
    swap = [(0, 1), (1, 0)]
    other_labels = lax.ppermute(labels, "core", swap)

    table = slot_table(labels, other_labels, patches)
    cols_a, cols_b = profile_rows(basis_cols, taps)
    rows_a = jnp.pad(basis_rows, ((0, 0), (0, 1)))
    rows_b = jnp.pad(basis_rows, ((0, 0), (1, 0)))
    g = rows_a[:, :, None] * cols_a[:, None, :] + rows_b[:, :, None] * cols_b[:, None, :]
    matched = match(odd, coef_code, coef_table, g, exposures, first, second, taps)
    other = lax.ppermute(matched, "core", swap)
    partial = pile(core[None], table, matched, other)
    parts = lax.all_to_all(partial, across, split_axis=0, concat_axis=0, tiled=True)
    coadd, first, second = coadd_of(odd, parts, rows, cols, wide_reach)
    first, second = trade(first, second)
    acc, profile = detect_own(psf_kernels, coadd)
    detect = detect_halo(odd, profile, first, second, acc, rows, wide)
    return (coadd[None], detect[None])


def solution(mesh):
    sections, sky = mesh.devices.shape
    grid = Mesh(mesh.devices.reshape(sections, 4, sky // 8, 2), ("section", "sy", "sx", "core"))
    sky = ("sy", "sx", "core")
    return jax.shard_map(
        on_device,
        mesh=grid,
        in_specs=(
            P(sky, "section", None),
            P(sky, None),
            P(),
            P(),
            P(),
            P(sky),
            P(sky, None),
            P(sky, None),
            P(),
        ),
        out_specs=(P(sky, "section", None), P(sky, None, "section", None)),
        check_vma=False,
    )
```

```python
import functools

import jax
import jax.numpy as jnp
from jax import lax
from jax.experimental import pallas as pl
from jax.experimental.pallas import tpu as pltpu
from jax.sharding import Mesh, PartitionSpec as P

f32 = jnp.float32
bf16 = jnp.bfloat16

lanes = 128
half = 64
group = 4
mib = 1024 * 1024


def one_hot(rows, cols, at):
    row = lax.broadcasted_iota(jnp.int32, (rows, cols), 0)
    col = lax.broadcasted_iota(jnp.int32, (rows, cols), 1)
    return (col == at(row)).astype(f32)


def lane_places(taps):
    first = one_hot(taps, lanes, lambda j: (lanes - j) % lanes)
    second = one_hot(taps, lanes, lambda j: half - j)
    return first, second


def row_places(rows, taps):
    return one_hot(rows, taps, lambda t: t), one_hot(rows, taps, lambda t: t - 1)


def lane_ids(rows):
    return lax.broadcasted_iota(jnp.int32, (rows, lanes), 1)


def band_mask(depth, taps):
    k = lax.broadcasted_iota(jnp.int32, (depth, lanes), 0)
    gap = k - lane_ids(depth) % half
    return (gap >= 0) & (gap < taps)


def band_tile(row, mask):
    depth = mask.shape[0]
    wide = jnp.broadcast_to(row, (depth, lanes))
    turned = pltpu.roll(wide, 0, 1, stride=1, stride_axis=0)
    return jnp.where(mask, turned, 0.0).astype(bf16)


def put_frame(frame, tiles, row, reach):
    count = len(tiles)
    rows = tiles[0].shape[0]
    lane = lane_ids(rows)
    zero = jnp.zeros((rows, lanes), f32)
    right = [pltpu.roll(t, reach, 1).astype(f32) for t in tiles]
    left = [pltpu.roll(t, half + reach, 1).astype(f32) for t in tiles]
    for m in range(count):
        before = right[m - 1] if m else zero
        frame[0, m, row : row + rows, :] = jnp.where(lane < reach, before, right[m])
        after = left[m + 1] if m + 1 < count else zero
        frame[1, m, row : row + rows, :] = jnp.where(lane < half + reach, left[m], after)


def put_lhs(lhs, frame, spans, row):
    tiles = frame.shape[1]
    for t in range(spans):
        for par in range(2):
            for m in range(tiles):
                at = (par * tiles + m) * 16
                piece = frame[par, m, pl.ds(row + t, 16, stride=group), :]
                lhs[at : at + 16, t * lanes : (t + 1) * lanes] = piece.astype(bf16)


def split_rows(even, odd, lane):
    first = jnp.where(lane < half, even, pltpu.roll(odd, half, 1))
    second = jnp.where(lane < half, pltpu.roll(even, half, 1), odd)
    return first, second


def columns(rows):
    return [rows[:, m * lanes : (m + 1) * lanes] for m in range(rows.shape[1] // lanes)]


def put_band(w, profile, taps, mask, first, last, at):
    depth = mask.shape[0]
    for u in range(max(first - 2, 0), min(last, taps + 1)):
        tile = band_tile(profile[u : u + 1, :], mask)
        if u >= first:
            row = (u - first) * lanes
            w[row : row + depth, at : at + lanes] = tile
        if first <= u + 2 < last:
            row = (u + 2 - first) * lanes
            w[row : row + depth, at + lanes : at + 2 * lanes] = tile


def clear_band(w, taps, depth, first, last):
    width = w.shape[1]
    for t in range(first, last):
        row = (t - first) * lanes
        w[row + depth : row + lanes, :] = jnp.zeros((lanes - depth, width), bf16)
        for u, at in ((t, 0), (t - 2, lanes)):
            if not 0 <= u <= taps:
                for n in range(at, width, 2 * lanes):
                    w[row : row + depth, n : n + lanes] = jnp.zeros((depth, lanes), bf16)


def edge_spans(taps):
    return (taps // 2 + 1) // 2 * 2


def put_edge_lhs(lhs, frame, spans):
    tiles = frame.shape[1]
    for t in range(spans):
        for par in range(2):
            for m in range(0, tiles, 2):
                pair = [frame[par, m + i, pl.ds(t, 8, stride=group), :] for i in range(2)]
                at = (par * tiles + m) * 8
                lhs[at : at + 16, t * lanes : (t + 1) * lanes] = jnp.concatenate(pair, axis=0).astype(bf16)


def edge_scratch(taps, tiles, width):
    spans = edge_spans(taps)
    return [
        pltpu.VMEM((2, 2, tiles, 48, lanes), f32),
        pltpu.VMEM((2, 128, spans * lanes), bf16),
        pltpu.VMEM((2, spans * lanes, width), bf16),
    ]


def put_edges(taps, frame, lhs, lo, hi):
    reach = taps // 2
    spans = edge_spans(taps)
    put_frame(frame.at[0], columns(lo), 0, reach)
    put_frame(frame.at[1], columns(hi), 28 - reach + spans, reach)
    for side in range(2):
        put_edge_lhs(lhs.at[side], frame.at[side], spans)


def halo_pair(odd, first, second):
    return jnp.where(odd, first, second), jnp.where(odd, second, first)


ways = 4


def match_body(taps, odd, code, table, base_rows, base_cols, x, first, second, out, g, frame, lhs, w):
    number, _, cols = x.shape
    reach = taps // 2
    exact = lax.Precision.HIGHEST
    rows_ab = [
        jnp.dot(places, base_rows[...], precision=exact, preferred_element_type=f32)
        for places in row_places(taps + 1, taps)
    ]
    cols_ab = [
        lax.dot_general(
            base_cols[...], places, (((0,), (0,)), ((), ())), precision=exact, preferred_element_type=f32
        )
        for places in lane_places(taps)
    ]
    for b in range(g.shape[0]):
        g[b] = sum(r[:, b : b + 1] * c[b : b + 1, :] for r, c in zip(rows_ab, cols_ab))
    spans = taps + 3
    count = cols // lanes
    depth = 96
    mask = band_mask(depth, taps)
    lane = lane_ids(16)
    for way in range(ways):
        clear_band(w.at[way], taps, depth, 0, spans)

    def one(e, way):
        total = jnp.zeros(g.shape[1:], f32)
        for b in range(g.shape[0]):
            total = total + table[b, code[e, b]] * g[b]
        total = total.astype(bf16).astype(f32)
        put_band(w.at[way], total, taps, mask, 0, spans, 0)
        lo, hi = halo_pair(odd[0] == 1, first[e], second[e])
        for piece, row in ((lo, 16 - reach), (x[e], 16), (hi, 80)):
            put_frame(frame.at[way], columns(piece), row, reach)
        put_lhs(lhs.at[way], frame.at[way], spans, 16 - reach)
        acc = jnp.dot(lhs[way], w[way], preferred_element_type=f32)
        for m in range(count):
            for h in range(2):
                cut = slice(h * lanes, (h + 1) * lanes)
                blocks = [acc[n * 16 : n * 16 + 16, cut] for n in (m, count + m)]
                for b, part in enumerate(split_rows(*blocks, lane)):
                    at = (2 * h + b) * 16
                    out[e, at : at + 16, m * lanes : (m + 1) * lanes] = part.astype(bf16)

    def some(i, _):
        for way in range(ways):
            one(ways * i + way, way)
        return 0

    lax.fori_loop(0, number // ways, some, 0)


def match(odd, code, table, base_rows, base_cols, x, first, second):
    number, rows, cols = x.shape
    taps, basis = base_rows.shape
    smem = pl.BlockSpec(memory_space=pltpu.SMEM)
    vmem = pl.BlockSpec(memory_space=pltpu.VMEM)
    spans = taps + 3
    return pl.pallas_call(
        functools.partial(match_body, taps),
        in_specs=[smem, smem, smem] + [vmem] * 5,
        out_specs=vmem,
        out_shape=jax.ShapeDtypeStruct((number, rows, cols), bf16),
        scratch_shapes=[
            pltpu.VMEM((basis, taps + 1, lanes), f32),
            pltpu.VMEM((ways, 2, cols // lanes, 96, lanes), f32),
            pltpu.VMEM((ways, 256, spans * lanes), bf16),
            pltpu.VMEM((ways, spans * lanes, 256), bf16),
        ],
        compiler_params=pltpu.CompilerParams(vmem_limit_bytes=24 * mib),
        cost_estimate=pl.CostEstimate(
            flops=number * 2 * 256 * 256 * spans * lanes, bytes_accessed=4 * x.size, transcendentals=0
        ),
        name="match",
    )(odd, code, table, base_rows, base_cols, x, first, second)


slots = 8


def slot_body(mine, other, out):
    number = mine.shape[0]
    per = (mine.shape[1] - 1) // 2
    patches = out.shape[0] // (slots + 1)

    def clear(p, _):
        out[p] = 0
        for s in range(slots):
            out[patches + p * slots + s] = 0
        return 0

    lax.fori_loop(0, patches, clear, 0)
    for base, labels in ((0, mine), (number, other)):

        def one(e, _):
            plane = (labels[e, 0] * 2 * number + base + e) * 256
            for k in range(per):
                p = labels[e, 1 + k]
                at = out[p]
                out[patches + p * slots + at] = plane + labels[e, 1 + per + k]
                out[p] = at + 1
            return 0

        lax.fori_loop(0, number, one, 0)


def slot_table(mine, other, patches):
    smem = pl.BlockSpec(memory_space=pltpu.SMEM)
    return pl.pallas_call(
        slot_body,
        in_specs=[smem, smem],
        out_specs=smem,
        out_shape=jax.ShapeDtypeStruct((patches * (slots + 1),), jnp.int32),
        name="slot_table",
    )(mine, other)


def pile_body(core, table, mine, other, out, planes, done, arrive, leave):
    number, rows, cols = mine.shape
    tiles = cols // lanes
    patches = table.shape[0] // (slots + 1)
    come = [
        pltpu.make_async_copy(ref, planes.at[pl.ds(i * number, number)], arrive.at[i])
        for i, ref in enumerate((mine, other))
    ]
    for copy in come:
        copy.start()
    for copy in come:
        copy.wait()
    lane = lane_ids(16)

    def patch(i, _):
        p = 2 * i + core[0]

        def some(used):
            entries = []
            for s in range(used):
                word = table[patches + p * slots + s]
                plane = word // 256
                entries.append(
                    (plane % (2 * number), word % 256, (plane // (2 * number)).astype(f32))
                )
            for c in range(rows // 16):
                total = [jnp.zeros((16, lanes), f32)] * tiles
                for e, o, weight in entries:
                    keep = lane < o
                    before = jnp.zeros((16, lanes), f32)
                    for m in range(tiles):
                        piece = planes[e, c * 16 : c * 16 + 16, m * lanes : (m + 1) * lanes]
                        turned = pltpu.roll(piece, o, 1).astype(f32)
                        total[m] = total[m] + weight * jnp.where(keep, before, turned)
                        before = turned
                for m in range(tiles):
                    at = m * rows + c * 16
                    done[i, at : at + 16, :] = total[m].astype(bf16)
            cover = jnp.zeros((16, lanes), f32)
            whole = jnp.zeros((16, lanes), f32)
            for e, o, weight in entries:
                cover = cover + jnp.where(lane < o, 0.0, weight)
                whole = whole + weight
            row = lax.broadcasted_iota(jnp.int32, (16, lanes), 0)
            done[i, tiles * rows : tiles * rows + 16, :] = jnp.where(row == 0, cover, whole).astype(bf16)

        used = table[p]
        for top in range(2, slots + 1, 2):
            low = top - 2 if top > 2 else -1

            @pl.when((used > low) & (used <= top))
            def _():
                some(top)

        pltpu.make_async_copy(done.at[i], out.at[i], leave.at[i]).start()
        return 0

    lax.fori_loop(0, patches // 2, patch, 0)

    def wait(i, _):
        pltpu.make_async_copy(done.at[i], out.at[i], leave.at[i]).wait()
        return 0

    lax.fori_loop(0, patches // 2, wait, 0)


def pile(core, table, mine, other):
    number, rows, cols = mine.shape
    patches = table.shape[0] // (slots + 1)
    smem = pl.BlockSpec(memory_space=pltpu.SMEM)
    far = pl.BlockSpec(memory_space=pl.ANY)
    shape = (patches // 2, cols // lanes * rows + 16, lanes)
    return pl.pallas_call(
        pile_body,
        in_specs=[smem, smem, far, far],
        out_specs=far,
        out_shape=jax.ShapeDtypeStruct(shape, bf16),
        scratch_shapes=[
            pltpu.VMEM((2 * number, rows, cols), bf16),
            pltpu.VMEM(shape, bf16),
            pltpu.SemaphoreType.DMA((2,)),
            pltpu.SemaphoreType.DMA((patches // 2,)),
        ],
        compiler_params=pltpu.CompilerParams(vmem_limit_bytes=8 * mib),
        name="pile",
    )(core, table, mine, other)


def coadd_body(reach, odd, far, coadd, first, second, parts, stage, arrive):
    count = parts.shape[0]
    rows, cols = coadd.shape
    tiles = cols // lanes
    starts = [tiles * rows] + [m * rows for m in range(tiles)]
    ends = [tiles * rows + 16] + [m * rows + rows for m in range(tiles)]
    come = []
    for i, (start, end) in enumerate(zip(starts, ends)):
        span = pl.ds(start, end - start)
        come.append(pltpu.make_async_copy(far.at[:, span, :], parts.at[:, span, :], arrive.at[i]))
        come[i].start()

    def add(at):
        total = parts[0, at : at + 16, :].astype(f32)
        for n in range(1, count):
            total = total + parts[n, at : at + 16, :].astype(f32)
        return total

    come[0].wait()
    cover = add(tiles * rows)
    scales = [1.0 / jnp.maximum(cover[r : r + 1, :], 1.0) for r in (0, 1)]
    for m in range(tiles):
        come[m + 1].wait()
        for b in range(group):
            value = add(m * rows + b * 16) * scales[min(m, 1)]
            stage[m, pl.ds(b, 16, stride=group), :] = value
        cut = slice(m * lanes, (m + 1) * lanes)
        coadd[:, cut] = stage[m]
        low = stage[m, 0:reach, :]
        high = stage[m, rows - reach : rows, :]
        first[:, cut] = jnp.where(odd[0] == 1, low, high).astype(bf16)
        second[:, cut] = jnp.where(odd[0] == 1, high, low).astype(bf16)


def coadd_of(odd, parts, rows, cols, reach):
    edge = jax.ShapeDtypeStruct((reach, cols), bf16)
    smem = pl.BlockSpec(memory_space=pltpu.SMEM)
    vmem = pl.BlockSpec(memory_space=pltpu.VMEM)
    return pl.pallas_call(
        functools.partial(coadd_body, reach),
        in_specs=[smem, pl.BlockSpec(memory_space=pl.ANY)],
        out_specs=(vmem, vmem, vmem),
        out_shape=(jax.ShapeDtypeStruct((rows, cols), f32), edge, edge),
        scratch_shapes=[
            pltpu.VMEM(parts.shape, bf16),
            pltpu.VMEM((cols // lanes, rows, lanes), f32),
            pltpu.SemaphoreType.DMA((cols // lanes + 1,)),
        ],
        compiler_params=pltpu.CompilerParams(vmem_limit_bytes=8 * mib),
        name="coadd",
    )(odd, parts)


def detect_own_body(taps, psf, x, acc, profile, frame, lhs, w):
    reach = taps // 2
    rows, cols = x.shape
    spans = taps + 3
    mask = band_mask(112, taps)
    for row in (0, 24 + rows):
        frame[:, :, row : row + 24, :] = jnp.zeros((2, cols // lanes, 24, lanes), f32)
    put_frame(frame, columns(x[...].astype(bf16)), 24, reach)
    put_lhs(lhs, frame, spans, 24 - reach)
    clear_band(w, taps, 112, 0, spans)
    for s in range(psf.shape[0]):
        total = 0.0
        for rows_at, cols_at in zip(row_places(profile.shape[1], taps), lane_places(taps)):
            moved = jnp.dot(rows_at.astype(bf16), psf[s], preferred_element_type=f32)
            total = total + jnp.dot(
                moved.astype(bf16), cols_at.astype(bf16), preferred_element_type=f32
            )
        profile[s] = total
        put_band(w, total, taps, mask, 0, spans, 256 * s)
        cut = slice(256 * s, 256 * s + 256)
        acc[:, cut] = jnp.dot(lhs[...], w[:, cut], preferred_element_type=f32)


def detect_own(psf, x):
    rows, cols = x.shape
    scales, _, taps = psf.shape
    spans = taps + 3
    return pl.pallas_call(
        functools.partial(detect_own_body, taps),
        out_shape=(
            jax.ShapeDtypeStruct((256, scales * 256), f32),
            jax.ShapeDtypeStruct((scales, 48, lanes), f32),
        ),
        scratch_shapes=[
            pltpu.VMEM((2, cols // lanes, 24 + rows + 24, lanes), f32),
            pltpu.VMEM((256, spans * lanes), bf16),
            pltpu.VMEM((spans * lanes, scales * 256), bf16),
        ],
        compiler_params=pltpu.CompilerParams(vmem_limit_bytes=20 * mib),
        cost_estimate=pl.CostEstimate(
            flops=scales * 2 * 256 * 256 * spans * lanes, bytes_accessed=4 * x.size, transcendentals=0
        ),
        name="detect_own",
    )(psf, x)


def detect_halo_body(taps, odd, profile, first, second, acc, out, frame, lhs, w, stage):
    scales, rows, cols = out.shape
    count = cols // lanes
    spans = edge_spans(taps)
    frame[...] = jnp.zeros_like(frame)
    clear_band(w.at[0], taps, 112, 0, spans)
    clear_band(w.at[1], taps, 112, taps + 3 - spans, taps + 3)
    mask = band_mask(112, taps)
    lane = lane_ids(16)
    lo, hi = halo_pair(odd[0] == 1, first[...], second[...])
    put_edges(taps, frame, lhs, lo, hi)
    for s in range(scales):
        at = 256 * s
        put_band(w.at[0], profile[s], taps, mask, 0, spans, at)
        put_band(w.at[1], profile[s], taps, mask, taps + 3 - spans, taps + 3, at)
        ends = [
            jnp.dot(lhs[side], w[side, :, at : at + 256], preferred_element_type=f32)
            for side in range(2)
        ]
        for m in range(count):
            for h in range(2):
                cut = slice(h * lanes, (h + 1) * lanes)
                blocks = []
                for n in (m, count + m):
                    more = jnp.concatenate([end[n * 8 : n * 8 + 8, cut] for end in ends], axis=0)
                    own = acc[n * 16 : n * 16 + 16, at + h * lanes : at + (h + 1) * lanes]
                    blocks.append(own + more)
                for b, part in enumerate(split_rows(*blocks, lane)):
                    stage[s, m, pl.ds(2 * h + b, 16, stride=group), :] = part
            out[s, :, m * lanes : (m + 1) * lanes] = stage[s, m]


def detect_halo(odd, profile, first, second, acc, rows, taps):
    cols = first.shape[1]
    scales = profile.shape[0]
    smem = pl.BlockSpec(memory_space=pltpu.SMEM)
    vmem = pl.BlockSpec(memory_space=pltpu.VMEM)
    return pl.pallas_call(
        functools.partial(detect_halo_body, taps),
        in_specs=[smem, vmem, vmem, vmem, vmem],
        out_specs=vmem,
        out_shape=jax.ShapeDtypeStruct((scales, rows, cols), f32),
        scratch_shapes=edge_scratch(taps, cols // lanes, scales * 256)
        + [pltpu.VMEM((scales, cols // lanes, rows, lanes), f32)],
        compiler_params=pltpu.CompilerParams(vmem_limit_bytes=20 * mib),
        name="detect_halo",
    )(odd, profile, first, second, acc)


def trade(first, second):
    count = lax.axis_size("section")
    out = []
    for start, rows in ((0, first), (1, second)):
        pairs = [(i, i + 1) for i in range(start, count - 1, 2)]
        out.append(lax.ppermute(rows, "section", pairs + [(b, a) for a, b in pairs]))
    return out


def on_device(
    exposures,
    coef_code,
    coef_table,
    basis_rows,
    basis_cols,
    exposure_weight,
    intersection_patch,
    intersection_shift,
    psf_kernels,
):
    number, rows, cols = exposures.shape
    taps = basis_rows.shape[1]
    reach = taps // 2
    wide = psf_kernels.shape[-1]
    wide_reach = wide // 2
    across = ("sy", "sx")
    patches = lax.axis_size("sy") * lax.axis_size("sx") * 2
    core = lax.axis_index("core")
    odd = lax.axis_index("section") % 2

    low, high = exposures[:, :reach, :], exposures[:, rows - reach :, :]
    first, second = trade(jnp.where(odd == 1, low, high), jnp.where(odd == 1, high, low))
    odd = odd[None]

    labels = jnp.concatenate(
        [exposure_weight[:, None], intersection_patch, intersection_shift], axis=1
    )
    swap = [(0, 1), (1, 0)]
    other_labels = lax.ppermute(labels, "core", swap)

    table = slot_table(labels, other_labels, patches)
    table, coef_code = lax.optimization_barrier((table, coef_code))
    matched = match(odd, coef_code, coef_table, basis_rows.T, basis_cols.T, exposures, first, second)
    other = lax.ppermute(matched, "core", swap)
    partial = pile(core[None], table, matched, other)
    parts = lax.all_to_all(partial, across, split_axis=0, concat_axis=0, tiled=True)
    coadd, first, second = coadd_of(odd, parts, rows, cols, wide_reach)
    first, second = trade(first, second)
    acc, profile = detect_own(psf_kernels, coadd)
    detect = detect_halo(odd, profile, first, second, acc, rows, wide)
    return (coadd[None], detect[None])


def solution(mesh):
    sections, sky = mesh.devices.shape
    grid = Mesh(mesh.devices.reshape(sections, 4, sky // 8, 2), ("section", "sy", "sx", "core"))
    sky = ("sy", "sx", "core")
    return jax.shard_map(
        on_device,
        mesh=grid,
        in_specs=(
            P(sky, "section", None),
            P(sky, None),
            P(),
            P(),
            P(),
            P(sky),
            P(sky, None),
            P(sky, None),
            P(),
        ),
        out_specs=(P(sky, "section", None), P(sky, None, "section", None)),
        check_vma=False,
    )
```

```python
import functools

import jax
import jax.numpy as jnp
from jax import lax
from jax.experimental import pallas as pl
from jax.experimental.pallas import tpu as pltpu
from jax.sharding import Mesh, PartitionSpec as P

f32 = jnp.float32
bf16 = jnp.bfloat16

lanes = 128
half = 64
group = 4
mib = 1024 * 1024


def one_hot(rows, cols, at):
    row = lax.broadcasted_iota(jnp.int32, (rows, cols), 0)
    col = lax.broadcasted_iota(jnp.int32, (rows, cols), 1)
    return (col == at(row)).astype(f32)


def lane_places(taps):
    first = one_hot(taps, lanes, lambda j: (lanes - j) % lanes)
    second = one_hot(taps, lanes, lambda j: half - j)
    return first, second


def row_places(rows, taps):
    return one_hot(rows, taps, lambda t: t), one_hot(rows, taps, lambda t: t - 1)


def lane_ids(rows):
    return lax.broadcasted_iota(jnp.int32, (rows, lanes), 1)


def band_mask(depth, taps):
    k = lax.broadcasted_iota(jnp.int32, (depth, lanes), 0)
    gap = k - lane_ids(depth) % half
    return (gap >= 0) & (gap < taps)


def band_tile(row, mask):
    depth = mask.shape[0]
    wide = jnp.broadcast_to(row, (depth, lanes))
    turned = pltpu.roll(wide, 0, 1, stride=1, stride_axis=0)
    return jnp.where(mask, turned, 0.0).astype(bf16)


def put_frame(frame, tiles, row, reach):
    count = len(tiles)
    rows = tiles[0].shape[0]
    lane = lane_ids(rows)
    zero = jnp.zeros((rows, lanes), f32)
    right = [pltpu.roll(t, reach, 1).astype(f32) for t in tiles]
    left = [pltpu.roll(t, half + reach, 1).astype(f32) for t in tiles]
    for m in range(count):
        before = right[m - 1] if m else zero
        frame[0, m, row : row + rows, :] = jnp.where(lane < reach, before, right[m])
        after = left[m + 1] if m + 1 < count else zero
        frame[1, m, row : row + rows, :] = jnp.where(lane < half + reach, left[m], after)


def put_lhs(lhs, frame, spans, row):
    tiles = frame.shape[1]
    for t in range(spans):
        for par in range(2):
            for m in range(tiles):
                at = (par * tiles + m) * 16
                piece = frame[par, m, pl.ds(row + t, 16, stride=group), :]
                lhs[at : at + 16, t * lanes : (t + 1) * lanes] = piece.astype(bf16)


def split_rows(even, odd, lane):
    first = jnp.where(lane < half, even, pltpu.roll(odd, half, 1))
    second = jnp.where(lane < half, pltpu.roll(even, half, 1), odd)
    return first, second


def columns(rows):
    return [rows[:, m * lanes : (m + 1) * lanes] for m in range(rows.shape[1] // lanes)]


def put_band(w, profile, taps, mask, first, last, at):
    depth = mask.shape[0]
    for u in range(max(first - 2, 0), min(last, taps + 1)):
        tile = band_tile(profile[u : u + 1, :], mask)
        if u >= first:
            row = (u - first) * lanes
            w[row : row + depth, at : at + lanes] = tile
        if first <= u + 2 < last:
            row = (u + 2 - first) * lanes
            w[row : row + depth, at + lanes : at + 2 * lanes] = tile


def clear_band(w, taps, depth, first, last):
    width = w.shape[1]
    for t in range(first, last):
        row = (t - first) * lanes
        w[row + depth : row + lanes, :] = jnp.zeros((lanes - depth, width), bf16)
        for u, at in ((t, 0), (t - 2, lanes)):
            if not 0 <= u <= taps:
                for n in range(at, width, 2 * lanes):
                    w[row : row + depth, n : n + lanes] = jnp.zeros((depth, lanes), bf16)


def edge_spans(taps):
    return (taps // 2 + 1) // 2 * 2


def put_edge_lhs(lhs, frame, spans):
    tiles = frame.shape[1]
    for t in range(spans):
        for par in range(2):
            for m in range(0, tiles, 2):
                pair = [frame[par, m + i, pl.ds(t, 8, stride=group), :] for i in range(2)]
                at = (par * tiles + m) * 8
                lhs[at : at + 16, t * lanes : (t + 1) * lanes] = jnp.concatenate(pair, axis=0).astype(bf16)


def edge_scratch(taps, tiles, width):
    spans = edge_spans(taps)
    return [
        pltpu.VMEM((2, 2, tiles, 48, lanes), f32),
        pltpu.VMEM((2, 128, spans * lanes), bf16),
        pltpu.VMEM((2, spans * lanes, width), bf16),
    ]


def put_edges(taps, frame, lhs, lo, hi):
    reach = taps // 2
    spans = edge_spans(taps)
    put_frame(frame.at[0], columns(lo), 0, reach)
    put_frame(frame.at[1], columns(hi), 28 - reach + spans, reach)
    for side in range(2):
        put_edge_lhs(lhs.at[side], frame.at[side], spans)


def halo_pair(odd, first, second):
    return jnp.where(odd, first, second), jnp.where(odd, second, first)


ways = 4


def profile_body(code, table, base_rows, base_cols, out, g):
    number, spans, _ = out.shape
    taps = base_rows.shape[0]
    exact = lax.Precision.HIGHEST
    rows_ab = [
        jnp.dot(places, base_rows[...], precision=exact, preferred_element_type=f32)
        for places in row_places(spans, taps)
    ]
    cols_ab = [
        lax.dot_general(
            base_cols[...], places, (((0,), (0,)), ((), ())), precision=exact, preferred_element_type=f32
        )
        for places in lane_places(taps)
    ]
    for b in range(g.shape[0]):
        g[b] = sum(r[:, b : b + 1] * c[b : b + 1, :] for r, c in zip(rows_ab, cols_ab))

    def one(e, _):
        total = jnp.zeros((spans, lanes), f32)
        for b in range(g.shape[0]):
            total = total + table[b, code[e, b]] * g[b]
        out[e] = total.astype(bf16).astype(f32)
        return 0

    lax.fori_loop(0, number, one, 0)


def profiles(code, table, base_rows, base_cols):
    number, basis = code.shape
    taps = base_rows.shape[0]
    smem = pl.BlockSpec(memory_space=pltpu.SMEM)
    vmem = pl.BlockSpec(memory_space=pltpu.VMEM)
    return pl.pallas_call(
        profile_body,
        in_specs=[smem, smem, vmem, vmem],
        out_specs=vmem,
        out_shape=jax.ShapeDtypeStruct((number, taps + 1, lanes), f32),
        scratch_shapes=[pltpu.VMEM((basis, taps + 1, lanes), f32)],
        compiler_params=pltpu.CompilerParams(vmem_limit_bytes=56 * mib),
        name="profiles",
    )(code, table, base_rows, base_cols)


def match_body(taps, odd, profile, far, first, second, out, x, frame, lhs, w, arrive):
    number, _, cols = x.shape
    reach = taps // 2
    spans = taps + 3
    count = cols // lanes
    depth = 96
    come = [pltpu.make_async_copy(far.at[e], x.at[e], arrive.at[e]) for e in range(number)]
    for copy in come:
        copy.start()
    mask = band_mask(depth, taps)
    lane = lane_ids(16)
    for way in range(ways):
        clear_band(w.at[way], taps, depth, 0, spans)

    def one(e, way):
        put_band(w.at[way], profile[e], taps, mask, 0, spans, 0)
        lo, hi = halo_pair(odd[0] == 1, first[e], second[e])
        for piece, row in ((lo, 16 - reach), (x[e], 16), (hi, 80)):
            put_frame(frame.at[way], columns(piece), row, reach)
        put_lhs(lhs.at[way], frame.at[way], spans, 16 - reach)
        acc = jnp.dot(lhs[way], w[way], preferred_element_type=f32)
        for m in range(count):
            for h in range(2):
                cut = slice(h * lanes, (h + 1) * lanes)
                blocks = [acc[n * 16 : n * 16 + 16, cut] for n in (m, count + m)]
                for b, part in enumerate(split_rows(*blocks, lane)):
                    at = (2 * h + b) * 16
                    out[e, at : at + 16, m * lanes : (m + 1) * lanes] = part.astype(bf16)

    for copy in come:
        copy.wait()

    def some(i, _):
        for way in range(ways):
            one(ways * i + way, way)
        return 0

    lax.fori_loop(0, number // ways, some, 0)


def match(odd, profile, x, first, second):
    number, rows, cols = x.shape
    taps = profile.shape[1] - 1
    smem = pl.BlockSpec(memory_space=pltpu.SMEM)
    vmem = pl.BlockSpec(memory_space=pltpu.VMEM)
    far = pl.BlockSpec(memory_space=pltpu.HBM)
    spans = taps + 3
    return pl.pallas_call(
        functools.partial(match_body, taps),
        in_specs=[smem, vmem, far, vmem, vmem],
        out_specs=vmem,
        out_shape=jax.ShapeDtypeStruct((number, rows, cols), bf16),
        scratch_shapes=[
            pltpu.VMEM(x.shape, bf16),
            pltpu.VMEM((ways, 2, cols // lanes, 96, lanes), f32),
            pltpu.VMEM((ways, 256, spans * lanes), bf16),
            pltpu.VMEM((ways, spans * lanes, 256), bf16),
            pltpu.SemaphoreType.DMA((number,)),
        ],
        compiler_params=pltpu.CompilerParams(vmem_limit_bytes=24 * mib),
        cost_estimate=pl.CostEstimate(
            flops=number * 2 * 256 * 256 * spans * lanes, bytes_accessed=4 * x.size, transcendentals=0
        ),
        name="match",
    )(odd, profile, x, first, second)


slots = 8


def slot_body(mine, other, out):
    number = mine.shape[0]
    per = (mine.shape[1] - 1) // 2
    patches = out.shape[0] // (slots + 1)

    def clear(p, _):
        out[p] = 0
        for s in range(slots):
            out[patches + p * slots + s] = 0
        return 0

    lax.fori_loop(0, patches, clear, 0)
    for base, labels in ((0, mine), (number, other)):

        def one(e, _):
            plane = (labels[e, 0] * 2 * number + base + e) * 256
            for k in range(per):
                p = labels[e, 1 + k]
                at = out[p]
                out[patches + p * slots + at] = plane + labels[e, 1 + per + k]
                out[p] = at + 1
            return 0

        lax.fori_loop(0, number, one, 0)


def slot_table(mine, other, patches):
    smem = pl.BlockSpec(memory_space=pltpu.SMEM)
    return pl.pallas_call(
        slot_body,
        in_specs=[smem, smem],
        out_specs=smem,
        out_shape=jax.ShapeDtypeStruct((patches * (slots + 1),), jnp.int32),
        name="slot_table",
    )(mine, other)


def pile_body(core, table, mine, other, out, planes):
    number, rows, cols = mine.shape
    tiles = cols // lanes
    patches = table.shape[0] // (slots + 1)
    planes[0:number] = mine[...]
    planes[number:] = other[...]
    lane = lane_ids(16)

    def patch(i, _):
        p = 2 * i + core[0]

        def some(used):
            entries = []
            for s in range(used):
                word = table[patches + p * slots + s]
                plane = word // 256
                entries.append(
                    (plane % (2 * number), word % 256, (plane // (2 * number)).astype(f32))
                )
            for c in range(rows // 16):
                total = [jnp.zeros((16, lanes), f32)] * tiles
                for e, o, weight in entries:
                    keep = lane < o
                    before = jnp.zeros((16, lanes), f32)
                    for m in range(tiles):
                        piece = planes[e, c * 16 : c * 16 + 16, m * lanes : (m + 1) * lanes]
                        turned = pltpu.roll(piece, o, 1).astype(f32)
                        total[m] = total[m] + weight * jnp.where(keep, before, turned)
                        before = turned
                for m in range(tiles):
                    at = m * rows + c * 16
                    out[i, at : at + 16, :] = total[m].astype(bf16)
            cover = jnp.zeros((16, lanes), f32)
            whole = jnp.zeros((16, lanes), f32)
            for e, o, weight in entries:
                cover = cover + jnp.where(lane < o, 0.0, weight)
                whole = whole + weight
            row = lax.broadcasted_iota(jnp.int32, (16, lanes), 0)
            out[i, tiles * rows : tiles * rows + 16, :] = jnp.where(row == 0, cover, whole).astype(bf16)

        used = table[p]
        for top in range(2, slots + 1, 2):
            low = top - 2 if top > 2 else -1

            @pl.when((used > low) & (used <= top))
            def _():
                some(top)

        return 0

    lax.fori_loop(0, patches // 2, patch, 0)


def pile(core, table, mine, other):
    number, rows, cols = mine.shape
    patches = table.shape[0] // (slots + 1)
    smem = pl.BlockSpec(memory_space=pltpu.SMEM)
    vmem = pl.BlockSpec(memory_space=pltpu.VMEM)
    shape = (patches // 2, cols // lanes * rows + 16, lanes)
    return pl.pallas_call(
        pile_body,
        in_specs=[smem, smem, vmem, vmem],
        out_specs=vmem,
        out_shape=jax.ShapeDtypeStruct(shape, bf16),
        scratch_shapes=[pltpu.VMEM((2 * number, rows, cols), bf16)],
        compiler_params=pltpu.CompilerParams(vmem_limit_bytes=12 * mib),
        name="pile",
    )(core, table, mine, other)


def coadd_body(reach, odd, parts, coadd, first, second, stage):
    count = parts.shape[0]
    rows, cols = coadd.shape
    tiles = cols // lanes
    def add(at):
        total = parts[0, at : at + 16, :].astype(f32)
        for n in range(1, count):
            total = total + parts[n, at : at + 16, :].astype(f32)
        return total

    cover = add(tiles * rows)
    scales = [1.0 / jnp.maximum(cover[r : r + 1, :], 1.0) for r in (0, 1)]
    for m in range(tiles):
        for b in range(group):
            value = add(m * rows + b * 16) * scales[min(m, 1)]
            stage[m, pl.ds(b, 16, stride=group), :] = value
        cut = slice(m * lanes, (m + 1) * lanes)
        coadd[:, cut] = stage[m]
        low = stage[m, 0:reach, :]
        high = stage[m, rows - reach : rows, :]
        first[:, cut] = jnp.where(odd[0] == 1, low, high).astype(bf16)
        second[:, cut] = jnp.where(odd[0] == 1, high, low).astype(bf16)


def coadd_of(odd, parts, rows, cols, reach):
    edge = jax.ShapeDtypeStruct((reach, cols), bf16)
    smem = pl.BlockSpec(memory_space=pltpu.SMEM)
    vmem = pl.BlockSpec(memory_space=pltpu.VMEM)
    return pl.pallas_call(
        functools.partial(coadd_body, reach),
        in_specs=[smem, vmem],
        out_specs=(vmem, vmem, vmem),
        out_shape=(jax.ShapeDtypeStruct((rows, cols), f32), edge, edge),
        scratch_shapes=[
            pltpu.VMEM((cols // lanes, rows, lanes), f32),
        ],
        compiler_params=pltpu.CompilerParams(vmem_limit_bytes=8 * mib),
        name="coadd",
    )(odd, parts)


def detect_own_body(taps, psf, x, acc, profile, frame, lhs, w):
    reach = taps // 2
    rows, cols = x.shape
    spans = taps + 3
    mask = band_mask(112, taps)
    for row in (0, 24 + rows):
        frame[:, :, row : row + 24, :] = jnp.zeros((2, cols // lanes, 24, lanes), f32)
    put_frame(frame, columns(x[...].astype(bf16)), 24, reach)
    put_lhs(lhs, frame, spans, 24 - reach)
    clear_band(w, taps, 112, 0, spans)
    for s in range(psf.shape[0]):
        total = 0.0
        for rows_at, cols_at in zip(row_places(profile.shape[1], taps), lane_places(taps)):
            moved = jnp.dot(rows_at.astype(bf16), psf[s], preferred_element_type=f32)
            total = total + jnp.dot(
                moved.astype(bf16), cols_at.astype(bf16), preferred_element_type=f32
            )
        profile[s] = total
        put_band(w, total, taps, mask, 0, spans, 256 * s)
        cut = slice(256 * s, 256 * s + 256)
        acc[:, cut] = jnp.dot(lhs[...], w[:, cut], preferred_element_type=f32)


def detect_own(psf, x):
    rows, cols = x.shape
    scales, _, taps = psf.shape
    spans = taps + 3
    return pl.pallas_call(
        functools.partial(detect_own_body, taps),
        out_shape=(
            jax.ShapeDtypeStruct((256, scales * 256), f32),
            jax.ShapeDtypeStruct((scales, 48, lanes), f32),
        ),
        scratch_shapes=[
            pltpu.VMEM((2, cols // lanes, 24 + rows + 24, lanes), f32),
            pltpu.VMEM((256, spans * lanes), bf16),
            pltpu.VMEM((spans * lanes, scales * 256), bf16),
        ],
        compiler_params=pltpu.CompilerParams(vmem_limit_bytes=20 * mib),
        cost_estimate=pl.CostEstimate(
            flops=scales * 2 * 256 * 256 * spans * lanes, bytes_accessed=4 * x.size, transcendentals=0
        ),
        name="detect_own",
    )(psf, x)


def detect_halo_body(taps, odd, profile, first, second, acc, out, frame, lhs, w, stage):
    scales, rows, cols = out.shape
    count = cols // lanes
    spans = edge_spans(taps)
    frame[...] = jnp.zeros_like(frame)
    clear_band(w.at[0], taps, 112, 0, spans)
    clear_band(w.at[1], taps, 112, taps + 3 - spans, taps + 3)
    mask = band_mask(112, taps)
    lane = lane_ids(16)
    lo, hi = halo_pair(odd[0] == 1, first[...], second[...])
    put_edges(taps, frame, lhs, lo, hi)
    for s in range(scales):
        at = 256 * s
        put_band(w.at[0], profile[s], taps, mask, 0, spans, at)
        put_band(w.at[1], profile[s], taps, mask, taps + 3 - spans, taps + 3, at)
        ends = [
            jnp.dot(lhs[side], w[side, :, at : at + 256], preferred_element_type=f32)
            for side in range(2)
        ]
        for m in range(count):
            for h in range(2):
                cut = slice(h * lanes, (h + 1) * lanes)
                blocks = []
                for n in (m, count + m):
                    more = jnp.concatenate([end[n * 8 : n * 8 + 8, cut] for end in ends], axis=0)
                    own = acc[n * 16 : n * 16 + 16, at + h * lanes : at + (h + 1) * lanes]
                    blocks.append(own + more)
                for b, part in enumerate(split_rows(*blocks, lane)):
                    stage[s, m, pl.ds(2 * h + b, 16, stride=group), :] = part
            out[s, :, m * lanes : (m + 1) * lanes] = stage[s, m]


def detect_halo(odd, profile, first, second, acc, rows, taps):
    cols = first.shape[1]
    scales = profile.shape[0]
    smem = pl.BlockSpec(memory_space=pltpu.SMEM)
    vmem = pl.BlockSpec(memory_space=pltpu.VMEM)
    return pl.pallas_call(
        functools.partial(detect_halo_body, taps),
        in_specs=[smem, vmem, vmem, vmem, vmem],
        out_specs=vmem,
        out_shape=jax.ShapeDtypeStruct((scales, rows, cols), f32),
        scratch_shapes=edge_scratch(taps, cols // lanes, scales * 256)
        + [pltpu.VMEM((scales, cols // lanes, rows, lanes), f32)],
        compiler_params=pltpu.CompilerParams(vmem_limit_bytes=20 * mib),
        name="detect_halo",
    )(odd, profile, first, second, acc)


def trade(first, second):
    count = lax.axis_size("section")
    out = []
    for start, rows in ((0, first), (1, second)):
        pairs = [(i, i + 1) for i in range(start, count - 1, 2)]
        out.append(lax.ppermute(rows, "section", pairs + [(b, a) for a, b in pairs]))
    return out


def on_device(
    exposures,
    coef_code,
    coef_table,
    basis_rows,
    basis_cols,
    exposure_weight,
    intersection_patch,
    intersection_shift,
    psf_kernels,
):
    number, rows, cols = exposures.shape
    taps = basis_rows.shape[1]
    reach = taps // 2
    wide = psf_kernels.shape[-1]
    wide_reach = wide // 2
    across = ("sy", "sx")
    patches = lax.axis_size("sy") * lax.axis_size("sx") * 2
    core = lax.axis_index("core")
    odd = lax.axis_index("section") % 2

    low, high = exposures[:, :reach, :], exposures[:, rows - reach :, :]
    first, second = trade(jnp.where(odd == 1, low, high), jnp.where(odd == 1, high, low))
    odd = odd[None]

    labels = jnp.concatenate(
        [exposure_weight[:, None], intersection_patch, intersection_shift], axis=1
    )
    swap = [(0, 1), (1, 0)]
    other_labels = lax.ppermute(labels, "core", swap)

    profile = profiles(coef_code, coef_table, basis_rows.T, basis_cols.T)
    table = slot_table(labels, other_labels, patches)
    table, profile = lax.optimization_barrier((table, profile))
    matched = match(odd, profile, exposures, first, second)
    other = lax.ppermute(matched, "core", swap)
    partial = pile(core[None], table, matched, other)
    parts = lax.all_to_all(partial, across, split_axis=0, concat_axis=0, tiled=True)
    coadd, first, second = coadd_of(odd, parts, rows, cols, wide_reach)
    first, second = trade(first, second)
    acc, profile = detect_own(psf_kernels, coadd)
    detect = detect_halo(odd, profile, first, second, acc, rows, wide)
    return (coadd[None], detect[None])


def solution(mesh):
    sections, sky = mesh.devices.shape
    grid = Mesh(mesh.devices.reshape(sections, 4, sky // 8, 2), ("section", "sy", "sx", "core"))
    sky = ("sy", "sx", "core")
    return jax.shard_map(
        on_device,
        mesh=grid,
        in_specs=(
            P(sky, "section", None),
            P(sky, None),
            P(),
            P(),
            P(),
            P(sky),
            P(sky, None),
            P(sky, None),
            P(),
        ),
        out_specs=(P(sky, "section", None), P(sky, None, "section", None)),
        check_vma=False,
    )
```

```python
import functools

import jax
import jax.numpy as jnp
from jax import lax
from jax.experimental import pallas as pl
from jax.experimental.pallas import tpu as pltpu
from jax.sharding import Mesh, PartitionSpec as P

f32 = jnp.float32
bf16 = jnp.bfloat16

lanes = 128
half = 64
group = 4
mib = 1024 * 1024


def one_hot(rows, cols, at):
    row = lax.broadcasted_iota(jnp.int32, (rows, cols), 0)
    col = lax.broadcasted_iota(jnp.int32, (rows, cols), 1)
    return (col == at(row)).astype(f32)


def lane_places(taps):
    first = one_hot(taps, lanes, lambda j: (lanes - j) % lanes)
    second = one_hot(taps, lanes, lambda j: half - j)
    return first, second


def row_places(rows, taps):
    return one_hot(rows, taps, lambda t: t), one_hot(rows, taps, lambda t: t - 1)


def lane_ids(rows):
    return lax.broadcasted_iota(jnp.int32, (rows, lanes), 1)


def band_mask(depth, taps):
    k = lax.broadcasted_iota(jnp.int32, (depth, lanes), 0)
    gap = k - lane_ids(depth) % half
    return (gap >= 0) & (gap < taps)


def band_tile(row, mask):
    depth = mask.shape[0]
    wide = jnp.broadcast_to(row, (depth, lanes))
    turned = pltpu.roll(wide, 0, 1, stride=1, stride_axis=0)
    return jnp.where(mask, turned, 0.0).astype(bf16)


def put_frame(frame, tiles, row, reach):
    count = len(tiles)
    rows = tiles[0].shape[0]
    lane = lane_ids(rows)
    zero = jnp.zeros((rows, lanes), f32)
    right = [pltpu.roll(t, reach, 1).astype(f32) for t in tiles]
    left = [pltpu.roll(t, half + reach, 1).astype(f32) for t in tiles]
    for m in range(count):
        before = right[m - 1] if m else zero
        frame[0, m, row : row + rows, :] = jnp.where(lane < reach, before, right[m])
        after = left[m + 1] if m + 1 < count else zero
        frame[1, m, row : row + rows, :] = jnp.where(lane < half + reach, left[m], after)


def put_lhs(lhs, frame, spans, row):
    tiles = frame.shape[1]
    for t in range(spans):
        for par in range(2):
            for m in range(tiles):
                at = (par * tiles + m) * 16
                piece = frame[par, m, pl.ds(row + t, 16, stride=group), :]
                lhs[at : at + 16, t * lanes : (t + 1) * lanes] = piece.astype(bf16)


def split_rows(even, odd, lane):
    first = jnp.where(lane < half, even, pltpu.roll(odd, half, 1))
    second = jnp.where(lane < half, pltpu.roll(even, half, 1), odd)
    return first, second


def columns(rows):
    return [rows[:, m * lanes : (m + 1) * lanes] for m in range(rows.shape[1] // lanes)]


def put_band(w, profile, taps, mask, first, last, at):
    depth = mask.shape[0]
    for u in range(max(first - 2, 0), min(last, taps + 1)):
        tile = band_tile(profile[u : u + 1, :], mask)
        if u >= first:
            row = (u - first) * lanes
            w[row : row + depth, at : at + lanes] = tile
        if first <= u + 2 < last:
            row = (u + 2 - first) * lanes
            w[row : row + depth, at + lanes : at + 2 * lanes] = tile


def clear_band(w, taps, depth, first, last):
    width = w.shape[1]
    for t in range(first, last):
        row = (t - first) * lanes
        w[row + depth : row + lanes, :] = jnp.zeros((lanes - depth, width), bf16)
        for u, at in ((t, 0), (t - 2, lanes)):
            if not 0 <= u <= taps:
                for n in range(at, width, 2 * lanes):
                    w[row : row + depth, n : n + lanes] = jnp.zeros((depth, lanes), bf16)


def edge_spans(taps):
    return (taps // 2 + 1) // 2 * 2


def put_edge_lhs(lhs, frame, spans):
    tiles = frame.shape[1]
    for t in range(spans):
        for par in range(2):
            for m in range(0, tiles, 2):
                pair = [frame[par, m + i, pl.ds(t, 8, stride=group), :] for i in range(2)]
                at = (par * tiles + m) * 8
                lhs[at : at + 16, t * lanes : (t + 1) * lanes] = jnp.concatenate(pair, axis=0).astype(bf16)


def edge_scratch(taps, tiles, width):
    spans = edge_spans(taps)
    return [
        pltpu.VMEM((2, 2, tiles, 48, lanes), f32),
        pltpu.VMEM((2, 128, spans * lanes), bf16),
        pltpu.VMEM((2, spans * lanes, width), bf16),
    ]


def put_edges(taps, frame, lhs, lo, hi):
    reach = taps // 2
    spans = edge_spans(taps)
    put_frame(frame.at[0], columns(lo), 0, reach)
    put_frame(frame.at[1], columns(hi), 28 - reach + spans, reach)
    for side in range(2):
        put_edge_lhs(lhs.at[side], frame.at[side], spans)


def halo_pair(odd, first, second):
    return jnp.where(odd, first, second), jnp.where(odd, second, first)


ways = 4


def profile_body(code, table, base_rows, base_cols, out, g):
    number, spans, _ = out.shape
    taps = base_rows.shape[0]
    exact = lax.Precision.HIGHEST
    rows_ab = [
        jnp.dot(places, base_rows[...], precision=exact, preferred_element_type=f32)
        for places in row_places(spans, taps)
    ]
    cols_ab = [
        lax.dot_general(
            base_cols[...], places, (((0,), (0,)), ((), ())), precision=exact, preferred_element_type=f32
        )
        for places in lane_places(taps)
    ]
    for b in range(g.shape[0]):
        g[b] = sum(r[:, b : b + 1] * c[b : b + 1, :] for r, c in zip(rows_ab, cols_ab))

    def one(e, _):
        total = jnp.zeros((spans, lanes), f32)
        for b in range(g.shape[0]):
            total = total + table[b, code[e, b]] * g[b]
        out[e] = total.astype(bf16).astype(f32)
        return 0

    lax.fori_loop(0, number, one, 0)


def profiles(code, table, base_rows, base_cols):
    number, basis = code.shape
    taps = base_rows.shape[0]
    smem = pl.BlockSpec(memory_space=pltpu.SMEM)
    vmem = pl.BlockSpec(memory_space=pltpu.VMEM)
    return pl.pallas_call(
        profile_body,
        in_specs=[smem, smem, vmem, vmem],
        out_specs=vmem,
        out_shape=jax.ShapeDtypeStruct((number, taps + 1, lanes), f32),
        scratch_shapes=[pltpu.VMEM((basis, taps + 1, lanes), f32)],
        compiler_params=pltpu.CompilerParams(vmem_limit_bytes=4 * mib),
        name="profiles",
    )(code, table, base_rows, base_cols)


def match_body(taps, odd, place, profile, far, first, second, keep, send, x, frame, lhs, w, arrive):
    number, _, cols = x.shape
    reach = taps // 2
    spans = taps + 3
    count = cols // lanes
    depth = 96
    come = [pltpu.make_async_copy(far.at[e], x.at[e], arrive.at[e]) for e in range(number)]
    for copy in come:
        copy.start()
    mask = band_mask(depth, taps)
    lane = lane_ids(16)
    for way in range(ways):
        clear_band(w.at[way], taps, depth, 0, spans)

    def one(e, way):
        put_band(w.at[way], profile[e], taps, mask, 0, spans, 0)
        lo, hi = halo_pair(odd[0] == 1, first[e], second[e])
        for piece, row in ((lo, 16 - reach), (x[e], 16), (hi, 80)):
            put_frame(frame.at[way], columns(piece), row, reach)
        put_lhs(lhs.at[way], frame.at[way], spans, 16 - reach)
        acc = jnp.dot(lhs[way], w[way], preferred_element_type=f32)
        for h in range(2):
            cut = slice(h * lanes, (h + 1) * lanes)
            parts = []
            for m in range(count):
                blocks = [acc[n * 16 : n * 16 + 16, cut] for n in (m, count + m)]
                parts.append([part.astype(bf16) for part in split_rows(*blocks, lane)])
            for b in range(2):
                rows = slice((2 * h + b) * 16, (2 * h + b) * 16 + 16)
                tiles = [part[b] for part in parts]
                low = [jnp.zeros((16, lanes), bf16)] + tiles[: count // 2]
                high = tiles[count // 2 - 1 :]
                for k in range(count // 2 + 1):
                    at = slice(k * lanes, (k + 1) * lanes)
                    keep[e, rows, at] = jnp.where(place[0] == 0, low[k], high[k])
                    send[e, rows, at] = jnp.where(place[0] == 0, high[k], low[k])

    for copy in come:
        copy.wait()

    def some(i, _):
        for way in range(ways):
            one(ways * i + way, way)
        return 0

    lax.fori_loop(0, number // ways, some, 0)


def match(odd, place, profile, x, first, second):
    number, rows, cols = x.shape
    taps = profile.shape[1] - 1
    smem = pl.BlockSpec(memory_space=pltpu.SMEM)
    vmem = pl.BlockSpec(memory_space=pltpu.VMEM)
    far = pl.BlockSpec(memory_space=pltpu.HBM)
    spans = taps + 3
    return pl.pallas_call(
        functools.partial(match_body, taps),
        in_specs=[smem, smem, vmem, far, vmem, vmem],
        out_specs=(vmem, vmem),
        out_shape=(jax.ShapeDtypeStruct((number, rows, cols // 2 + lanes), bf16),) * 2,
        scratch_shapes=[
            pltpu.VMEM(x.shape, bf16),
            pltpu.VMEM((ways, 2, cols // lanes, 96, lanes), f32),
            pltpu.VMEM((ways, 256, spans * lanes), bf16),
            pltpu.VMEM((ways, spans * lanes, 256), bf16),
            pltpu.SemaphoreType.DMA((number,)),
        ],
        compiler_params=pltpu.CompilerParams(vmem_limit_bytes=24 * mib),
        cost_estimate=pl.CostEstimate(
            flops=number * 2 * 256 * 256 * spans * lanes, bytes_accessed=4 * x.size, transcendentals=0
        ),
        name="match",
    )(odd, place, profile, x, first, second)


slots = 8


def slot_body(mine, other, out):
    number = mine.shape[0]
    per = (mine.shape[1] - 1) // 2
    patches = out.shape[0] // (slots + 1)

    def clear(p, _):
        out[p] = 0
        for s in range(slots):
            out[patches + p * slots + s] = 0
        return 0

    lax.fori_loop(0, patches, clear, 0)
    for base, labels in ((0, mine), (number, other)):

        def one(e, _):
            plane = (labels[e, 0] * 2 * number + base + e) * 256
            for k in range(per):
                p = labels[e, 1 + k]
                at = out[p]
                out[patches + p * slots + at] = plane + labels[e, 1 + per + k]
                out[p] = at + 1
            return 0

        lax.fori_loop(0, number, one, 0)


def slot_table(mine, other, patches):
    smem = pl.BlockSpec(memory_space=pltpu.SMEM)
    return pl.pallas_call(
        slot_body,
        in_specs=[smem, smem],
        out_specs=smem,
        out_shape=jax.ShapeDtypeStruct((patches * (slots + 1),), jnp.int32),
        compiler_params=pltpu.CompilerParams(vmem_limit_bytes=mib),
        name="slot_table",
    )(mine, other)


def role_pairs(step, size, shift):
    index = lambda y, x, core: ((y % size) * size + x % size) * 2 + core
    pairs = []
    for y in range(size):
        for x in range(size):
            for core in range(2):
                to = (y, x + shift) if core == step else (y + shift, x)
                pairs.append((index(y, x, core), index(*to, core)))
    return pairs


def pile_body(chunks, size, place, table, mine, other, *rest):
    outs, planes = rest[:-1], rest[-1]
    number, rows, cols = mine.shape
    tiles = cols // lanes - 1
    patches = table.shape[0] // (slots + 1)
    core = place[0]
    planes[0:number] = mine[...]
    planes[number:] = other[...]
    lane = lane_ids(16)
    tail = lax.broadcasted_iota(jnp.int32, (16, lanes), 0)

    for chunk, out in zip(chunks, outs):

        def patch(i, _):
            u = (place[1] + chunk) % size
            v = (place[2] + i // 2) % size
            p = jnp.where(core == 0, v * size + u, u * size + v) * 2 + i % 2

            def some(used):
                entries = []
                for s in range(used):
                    word = table[patches + p * slots + s]
                    plane = word // 256
                    entries.append(
                        (plane % (2 * number), word % 256, (plane // (2 * number)).astype(f32))
                    )
                for c in range(rows // 16):
                    total = [jnp.zeros((16, lanes), f32)] * tiles
                    for e, o, weight in entries:
                        early = lane < o
                        before = None
                        for k in range(tiles + 1):
                            piece = planes[e, c * 16 : c * 16 + 16, k * lanes : (k + 1) * lanes]
                            turned = pltpu.roll(piece, o, 1).astype(f32)
                            if k:
                                part = jnp.where(early, before, turned)
                                total[k - 1] = total[k - 1] + weight * part
                            before = turned
                    for k in range(tiles):
                        at = k * rows + c * 16
                        out[i, at : at + 16, :] = total[k].astype(out.dtype)
                cover = jnp.zeros((16, lanes), f32)
                whole = jnp.zeros((16, lanes), f32)
                for e, o, weight in entries:
                    cover = cover + jnp.where(lane < o, 0.0, weight)
                    whole = whole + weight
                out[i, tiles * rows :, :] = jnp.where(tail == 0, cover, whole).astype(out.dtype)

            used = table[p]
            for top in range(2, slots + 1, 2):
                low = top - 2 if top > 2 else -1

                @pl.when((used > low) & (used <= top))
                def _():
                    some(top)

            return 0

        lax.fori_loop(0, 2 * size, patch, 0)


def pile(chunks, kinds, size, place, table, mine, other):
    number, rows, cols = mine.shape
    smem = pl.BlockSpec(memory_space=pltpu.SMEM)
    vmem = pl.BlockSpec(memory_space=pltpu.VMEM)
    shape = (2 * size, (cols // lanes - 1) * rows + 16, lanes)
    return pl.pallas_call(
        functools.partial(pile_body, chunks, size),
        in_specs=[smem, smem, vmem, vmem],
        out_specs=[vmem] * len(chunks),
        out_shape=[jax.ShapeDtypeStruct(shape, kind) for kind in kinds],
        scratch_shapes=[pltpu.VMEM((2 * number, rows, cols), bf16)],
        compiler_params=pltpu.CompilerParams(vmem_limit_bytes=8 * mib),
        cost_estimate=pl.CostEstimate(
            flops=len(chunks) * 1000000000, bytes_accessed=4 * mine.size, transcendentals=0
        ),
        name="pile_" + "_".join(str(chunk) for chunk in chunks),
    )(place, table, mine, other)


def fold_body(own, *rest):
    came, keep, sends = rest[: len(rest) // 2], rest[len(rest) // 2], rest[len(rest) // 2 + 1 :]
    rows = own.shape[1]
    for i in range(own.shape[0]):
        for at in range(0, rows, 16):
            total = own[i, at : at + 16, :]
            for ref in came:
                total = total + ref[i, at : at + 16, :].astype(f32)
            if i < 2:
                keep[i, at : at + 16, :] = total
            else:
                sends[i // 2 - 1][i % 2, at : at + 16, :] = total.astype(bf16)


def fold(own, came):
    vmem = pl.BlockSpec(memory_space=pltpu.VMEM)
    shape = (2,) + own.shape[1:]
    return pl.pallas_call(
        fold_body,
        in_specs=[vmem] * (1 + len(came)),
        out_specs=[vmem] * (1 + len(came)),
        out_shape=[jax.ShapeDtypeStruct(shape, f32)] + [jax.ShapeDtypeStruct(shape, bf16)] * len(came),
        compiler_params=pltpu.CompilerParams(vmem_limit_bytes=4 * mib),
        name="fold",
    )(own, *came)


def meet_body(place, own, *rest):
    came, mine, send = rest[:-2], rest[-2], rest[-1]
    core = place[0]
    for at in range(0, own.shape[1], 16):
        for out, i in ((mine, core), (send, 1 - core)):
            total = own[i, at : at + 16, :]
            for ref in came:
                total = total + ref[i, at : at + 16, :].astype(f32)
            out[at : at + 16, :] = total


def meet(place, own, came):
    smem = pl.BlockSpec(memory_space=pltpu.SMEM)
    vmem = pl.BlockSpec(memory_space=pltpu.VMEM)
    return pl.pallas_call(
        meet_body,
        in_specs=[smem] + [vmem] * (1 + len(came)),
        out_specs=[vmem] * 2,
        out_shape=[jax.ShapeDtypeStruct(own.shape[1:], f32)] * 2,
        compiler_params=pltpu.CompilerParams(vmem_limit_bytes=4 * mib),
        name="meet",
    )(place, own, *came)


def coadd_body(reach, odd, place, mine, other, coadd, rounded, first, second, stage):
    rows, cols = coadd.shape
    tiles = cols // lanes
    near = place[0] == 0

    def pick(low, at):
        a, b = mine[at : at + 16, :], other[at : at + 16, :]
        return jnp.where(near, a, b) if low else jnp.where(near, b, a)

    cover = pick(True, tiles // 2 * rows)
    scales = [1.0 / jnp.maximum(cover[r : r + 1, :], 1.0) for r in (0, 1)]
    for m in range(tiles):
        for b in range(group):
            at = m % (tiles // 2) * rows + b * 16
            stage[m, pl.ds(b, 16, stride=group), :] = pick(m < tiles // 2, at) * scales[min(m, 1)]
        cut = slice(m * lanes, (m + 1) * lanes)
        coadd[:, cut] = stage[m]
        rounded[:, cut] = stage[m].astype(bf16)
        low = stage[m, 0:reach, :]
        high = stage[m, rows - reach : rows, :]
        first[:, cut] = jnp.where(odd[0] == 1, low, high).astype(bf16)
        second[:, cut] = jnp.where(odd[0] == 1, high, low).astype(bf16)


def coadd_of(odd, place, mine, other, rows, cols, reach):
    edge = jax.ShapeDtypeStruct((reach, cols), bf16)
    smem = pl.BlockSpec(memory_space=pltpu.SMEM)
    vmem = pl.BlockSpec(memory_space=pltpu.VMEM)
    return pl.pallas_call(
        functools.partial(coadd_body, reach),
        in_specs=[smem, smem, vmem, vmem],
        out_specs=(vmem,) * 4,
        out_shape=(
            jax.ShapeDtypeStruct((rows, cols), f32),
            jax.ShapeDtypeStruct((rows, cols), bf16),
            edge,
            edge,
        ),
        scratch_shapes=[pltpu.VMEM((cols // lanes, rows, lanes), f32)],
        compiler_params=pltpu.CompilerParams(vmem_limit_bytes=8 * mib),
        name="coadd",
    )(odd, place, mine, other)


def detect_own_body(taps, psf, x, acc, profile, frame, lhs, w):
    reach = taps // 2
    rows, cols = x.shape
    spans = taps + 3
    mask = band_mask(112, taps)
    for row in (0, 24 + rows):
        frame[:, :, row : row + 24, :] = jnp.zeros((2, cols // lanes, 24, lanes), f32)
    put_frame(frame, columns(x[...]), 24, reach)
    put_lhs(lhs, frame, spans, 24 - reach)
    clear_band(w, taps, 112, 0, spans)
    for s in range(psf.shape[0]):
        total = 0.0
        for rows_at, cols_at in zip(row_places(profile.shape[1], taps), lane_places(taps)):
            moved = jnp.dot(rows_at.astype(bf16), psf[s], preferred_element_type=f32)
            total = total + jnp.dot(
                moved.astype(bf16), cols_at.astype(bf16), preferred_element_type=f32
            )
        profile[s] = total
        put_band(w, total, taps, mask, 0, spans, 256 * s)
        cut = slice(256 * s, 256 * s + 256)
        acc[:, cut] = jnp.dot(lhs[...], w[:, cut], preferred_element_type=f32)


def detect_own(psf, x):
    rows, cols = x.shape
    scales, _, taps = psf.shape
    spans = taps + 3
    return pl.pallas_call(
        functools.partial(detect_own_body, taps),
        out_shape=(
            jax.ShapeDtypeStruct((256, scales * 256), f32),
            jax.ShapeDtypeStruct((scales, 48, lanes), f32),
        ),
        scratch_shapes=[
            pltpu.VMEM((2, cols // lanes, 24 + rows + 24, lanes), f32),
            pltpu.VMEM((256, spans * lanes), bf16),
            pltpu.VMEM((spans * lanes, scales * 256), bf16),
        ],
        compiler_params=pltpu.CompilerParams(vmem_limit_bytes=20 * mib),
        cost_estimate=pl.CostEstimate(
            flops=scales * 2 * 256 * 256 * spans * lanes, bytes_accessed=4 * x.size, transcendentals=0
        ),
        name="detect_own",
    )(psf, x)


def detect_halo_body(taps, odd, profile, first, second, acc, out, frame, lhs, w, stage):
    scales, rows, cols = out.shape
    count = cols // lanes
    spans = edge_spans(taps)
    frame[...] = jnp.zeros_like(frame)
    clear_band(w.at[0], taps, 112, 0, spans)
    clear_band(w.at[1], taps, 112, taps + 3 - spans, taps + 3)
    mask = band_mask(112, taps)
    lane = lane_ids(16)
    lo, hi = halo_pair(odd[0] == 1, first[...], second[...])
    put_edges(taps, frame, lhs, lo, hi)
    for s in range(scales):
        at = 256 * s
        put_band(w.at[0], profile[s], taps, mask, 0, spans, at)
        put_band(w.at[1], profile[s], taps, mask, taps + 3 - spans, taps + 3, at)
        ends = [
            jnp.dot(lhs[side], w[side, :, at : at + 256], preferred_element_type=f32)
            for side in range(2)
        ]
        for m in range(count):
            for h in range(2):
                cut = slice(h * lanes, (h + 1) * lanes)
                blocks = []
                for n in (m, count + m):
                    more = jnp.concatenate([end[n * 8 : n * 8 + 8, cut] for end in ends], axis=0)
                    own = acc[n * 16 : n * 16 + 16, at + h * lanes : at + (h + 1) * lanes]
                    blocks.append(own + more)
                for b, part in enumerate(split_rows(*blocks, lane)):
                    stage[s, m, pl.ds(2 * h + b, 16, stride=group), :] = part
            out[s, :, m * lanes : (m + 1) * lanes] = stage[s, m]


def detect_halo(odd, profile, first, second, acc, rows, taps):
    cols = first.shape[1]
    scales = profile.shape[0]
    smem = pl.BlockSpec(memory_space=pltpu.SMEM)
    vmem = pl.BlockSpec(memory_space=pltpu.VMEM)
    return pl.pallas_call(
        functools.partial(detect_halo_body, taps),
        in_specs=[smem, vmem, vmem, vmem, vmem],
        out_specs=vmem,
        out_shape=jax.ShapeDtypeStruct((scales, rows, cols), f32),
        scratch_shapes=edge_scratch(taps, cols // lanes, scales * 256)
        + [pltpu.VMEM((scales, cols // lanes, rows, lanes), f32)],
        compiler_params=pltpu.CompilerParams(vmem_limit_bytes=20 * mib),
        name="detect_halo",
    )(odd, profile, first, second, acc)


def trade(first, second):
    count = lax.axis_size("section")
    out = []
    for start, rows in ((0, first), (1, second)):
        pairs = [(i, i + 1) for i in range(start, count - 1, 2)]
        out.append(lax.ppermute(rows, "section", pairs + [(b, a) for a, b in pairs]))
    return out


def on_device(
    exposures,
    coef_code,
    coef_table,
    basis_rows,
    basis_cols,
    exposure_weight,
    intersection_patch,
    intersection_shift,
    psf_kernels,
):
    number, rows, cols = exposures.shape
    taps = basis_rows.shape[1]
    reach = taps // 2
    wide = psf_kernels.shape[-1]
    wide_reach = wide // 2
    sky = ("sy", "sx", "core")
    size = lax.axis_size("sx")
    patches = size * size * 2
    core, at_x, at_y = (lax.axis_index(name) for name in ("core", "sx", "sy"))
    place = jnp.stack([core, jnp.where(core == 0, at_x, at_y), jnp.where(core == 0, at_y, at_x)])
    odd = lax.axis_index("section") % 2

    low, high = exposures[:, :reach, :], exposures[:, rows - reach :, :]
    first, second = trade(jnp.where(odd == 1, low, high), jnp.where(odd == 1, high, low))
    odd = odd[None]

    labels = jnp.concatenate(
        [exposure_weight[:, None], intersection_patch, intersection_shift], axis=1
    )
    swap = [(0, 1), (1, 0)]
    other_labels = lax.ppermute(labels, "core", swap)

    profile = profiles(coef_code, coef_table, basis_rows.T, basis_cols.T)
    table = slot_table(labels, other_labels, patches)
    table, profile = lax.optimization_barrier((table, profile))
    mine, send = match(odd, place, profile, exposures, first, second)
    other = lax.ppermute(send, "core", swap)

    steps = (2, 1, 3)
    move = lambda rows, step, by: lax.ppermute(rows, sky, role_pairs(step, size, by))
    (far,) = pile((2,), (bf16,), size, place, table, mine, other)
    came = [move(far, 0, 2)]
    far, table = lax.optimization_barrier((far, table))
    ahead, behind, own = pile((1, 3, 0), (bf16, bf16, f32), size, place, table, mine, other)
    came += [move(ahead, 0, 1), move(behind, 0, 3)]
    keep, *sends = fold(own, came)
    came = [move(sends[by - 1], 1, by) for by in steps]
    mine, send = meet(place, keep, came)
    other = lax.ppermute(send, "core", swap)
    coadd, rounded, first, second = coadd_of(odd, place, mine, other, rows, cols, wide_reach)
    first, second = trade(first, second)
    acc, profile = detect_own(psf_kernels, rounded)
    detect = detect_halo(odd, profile, first, second, acc, rows, wide)
    return (coadd[None], detect[None])


def solution(mesh):
    sections, sky = mesh.devices.shape
    grid = Mesh(mesh.devices.reshape(sections, 4, sky // 8, 2), ("section", "sy", "sx", "core"))
    sky = ("sy", "sx", "core")
    return jax.shard_map(
        on_device,
        mesh=grid,
        in_specs=(
            P(sky, "section", None),
            P(sky, None),
            P(),
            P(),
            P(),
            P(sky),
            P(sky, None),
            P(sky, None),
            P(),
        ),
        out_specs=(P(sky, "section", None), P(sky, None, "section", None)),
        check_vma=False,
    )
```

```python
import functools

import jax
import jax.numpy as jnp
from jax import lax
from jax.experimental import pallas as pl
from jax.experimental.pallas import tpu as pltpu
from jax.sharding import Mesh, PartitionSpec as P

f32 = jnp.float32
bf16 = jnp.bfloat16

lanes = 128
half = 64
group = 4
mib = 1024 * 1024


def one_hot(rows, cols, at):
    row = lax.broadcasted_iota(jnp.int32, (rows, cols), 0)
    col = lax.broadcasted_iota(jnp.int32, (rows, cols), 1)
    return (col == at(row)).astype(f32)


def lane_places(taps):
    first = one_hot(taps, lanes, lambda j: (lanes - j) % lanes)
    second = one_hot(taps, lanes, lambda j: half - j)
    return first, second


def row_places(rows, taps):
    return one_hot(rows, taps, lambda t: t), one_hot(rows, taps, lambda t: t - 1)


def lane_ids(rows):
    return lax.broadcasted_iota(jnp.int32, (rows, lanes), 1)


def band_mask(depth, taps):
    k = lax.broadcasted_iota(jnp.int32, (depth, lanes), 0)
    gap = k - lane_ids(depth) % half
    return (gap >= 0) & (gap < taps)


def band_tile(row, mask):
    depth = mask.shape[0]
    wide = jnp.broadcast_to(row, (depth, lanes))
    turned = pltpu.roll(wide, 0, 1, stride=1, stride_axis=0)
    return jnp.where(mask, turned, 0.0).astype(bf16)


def put_frame(frame, tiles, row, reach):
    count = len(tiles)
    rows = tiles[0].shape[0]
    lane = lane_ids(rows)
    zero = jnp.zeros((rows, lanes), f32)
    right = [pltpu.roll(t, reach, 1).astype(f32) for t in tiles]
    left = [pltpu.roll(t, half + reach, 1).astype(f32) for t in tiles]
    for m in range(count):
        before = right[m - 1] if m else zero
        frame[0, m, row : row + rows, :] = jnp.where(lane < reach, before, right[m])
        after = left[m + 1] if m + 1 < count else zero
        frame[1, m, row : row + rows, :] = jnp.where(lane < half + reach, left[m], after)


def put_lhs(lhs, frame, spans, row):
    tiles = frame.shape[1]
    for t in range(spans):
        for par in range(2):
            for m in range(tiles):
                at = (par * tiles + m) * 16
                piece = frame[par, m, pl.ds(row + t, 16, stride=group), :]
                lhs[at : at + 16, t * lanes : (t + 1) * lanes] = piece.astype(bf16)


def split_rows(even, odd, lane):
    first = jnp.where(lane < half, even, pltpu.roll(odd, half, 1))
    second = jnp.where(lane < half, pltpu.roll(even, half, 1), odd)
    return first, second


def columns(rows):
    return [rows[:, m * lanes : (m + 1) * lanes] for m in range(rows.shape[1] // lanes)]


def put_band(w, profile, taps, mask, first, last, at):
    depth = mask.shape[0]
    for u in range(max(first - 2, 0), min(last, taps + 1)):
        tile = band_tile(profile[u : u + 1, :], mask)
        if u >= first:
            row = (u - first) * lanes
            w[row : row + depth, at : at + lanes] = tile
        if first <= u + 2 < last:
            row = (u + 2 - first) * lanes
            w[row : row + depth, at + lanes : at + 2 * lanes] = tile


def clear_band(w, taps, depth, first, last):
    width = w.shape[1]
    for t in range(first, last):
        row = (t - first) * lanes
        w[row + depth : row + lanes, :] = jnp.zeros((lanes - depth, width), bf16)
        for u, at in ((t, 0), (t - 2, lanes)):
            if not 0 <= u <= taps:
                for n in range(at, width, 2 * lanes):
                    w[row : row + depth, n : n + lanes] = jnp.zeros((depth, lanes), bf16)


def edge_spans(taps):
    return (taps // 2 + 1) // 2 * 2


def put_edge_lhs(lhs, frame, spans):
    tiles = frame.shape[1]
    for t in range(spans):
        for par in range(2):
            for m in range(0, tiles, 2):
                pair = [frame[par, m + i, pl.ds(t, 8, stride=group), :] for i in range(2)]
                at = (par * tiles + m) * 8
                lhs[at : at + 16, t * lanes : (t + 1) * lanes] = jnp.concatenate(pair, axis=0).astype(bf16)


def edge_scratch(taps, tiles):
    spans = edge_spans(taps)
    return [
        pltpu.VMEM((2, 2, tiles, 48, lanes), f32),
        pltpu.VMEM((2, 128, spans * lanes), bf16),
    ]


def put_edges(taps, frame, lhs, lo, hi):
    reach = taps // 2
    spans = edge_spans(taps)
    put_frame(frame.at[0], columns(lo), 0, reach)
    put_frame(frame.at[1], columns(hi), 28 - reach + spans, reach)
    for side in range(2):
        put_edge_lhs(lhs.at[side], frame.at[side], spans)


def halo_pair(odd, first, second):
    return jnp.where(odd, first, second), jnp.where(odd, second, first)


ways = 4


def profile_body(code, table, base_rows, base_cols, out, g):
    number, spans, _ = out.shape
    taps = base_rows.shape[0]
    exact = lax.Precision.HIGHEST
    rows_ab = [
        jnp.dot(places, base_rows[...], precision=exact, preferred_element_type=f32)
        for places in row_places(spans, taps)
    ]
    cols_ab = [
        lax.dot_general(
            base_cols[...], places, (((0,), (0,)), ((), ())), precision=exact, preferred_element_type=f32
        )
        for places in lane_places(taps)
    ]
    for b in range(g.shape[0]):
        g[b] = sum(r[:, b : b + 1] * c[b : b + 1, :] for r, c in zip(rows_ab, cols_ab))

    def one(e, _):
        total = jnp.zeros((spans, lanes), f32)
        for b in range(g.shape[0]):
            total = total + table[b, code[e, b]] * g[b]
        out[e] = total.astype(bf16).astype(f32)
        return 0

    lax.fori_loop(0, number, one, 0)


def profiles(code, table, base_rows, base_cols):
    number, basis = code.shape
    taps = base_rows.shape[0]
    smem = pl.BlockSpec(memory_space=pltpu.SMEM)
    vmem = pl.BlockSpec(memory_space=pltpu.VMEM)
    return pl.pallas_call(
        profile_body,
        in_specs=[smem, smem, vmem, vmem],
        out_specs=vmem,
        out_shape=jax.ShapeDtypeStruct((number, taps + 1, lanes), f32),
        scratch_shapes=[pltpu.VMEM((basis, taps + 1, lanes), f32)],
        compiler_params=pltpu.CompilerParams(vmem_limit_bytes=4 * mib),
        name="profiles",
    )(code, table, base_rows, base_cols)


def match_body(taps, odd, place, profile, far, first, second, keep, send, x, frame, lhs, w, arrive):
    number, _, cols = x.shape
    reach = taps // 2
    spans = taps + 3
    count = cols // lanes
    depth = 96
    come = [pltpu.make_async_copy(far.at[e], x.at[e], arrive.at[e]) for e in range(number)]
    for copy in come:
        copy.start()
    mask = band_mask(depth, taps)
    lane = lane_ids(16)
    for way in range(ways):
        clear_band(w.at[way], taps, depth, 0, spans)

    def one(e, way):
        put_band(w.at[way], profile[e], taps, mask, 0, spans, 0)
        lo, hi = halo_pair(odd[0] == 1, first[e], second[e])
        for piece, row in ((lo, 16 - reach), (x[e], 16), (hi, 80)):
            put_frame(frame.at[way], columns(piece), row, reach)
        put_lhs(lhs.at[way], frame.at[way], spans, 16 - reach)
        acc = jnp.dot(lhs[way], w[way], preferred_element_type=f32)
        for h in range(2):
            cut = slice(h * lanes, (h + 1) * lanes)
            parts = []
            for m in range(count):
                blocks = [acc[n * 16 : n * 16 + 16, cut] for n in (m, count + m)]
                parts.append([part.astype(bf16) for part in split_rows(*blocks, lane)])
            for b in range(2):
                rows = slice((2 * h + b) * 16, (2 * h + b) * 16 + 16)
                tiles = [part[b] for part in parts]
                low = [jnp.zeros((16, lanes), bf16)] + tiles[: count // 2]
                high = tiles[count // 2 - 1 :]
                for k in range(count // 2 + 1):
                    at = slice(k * lanes, (k + 1) * lanes)
                    keep[e, rows, at] = jnp.where(place[0] == 0, low[k], high[k])
                    send[e, rows, at] = jnp.where(place[0] == 0, high[k], low[k])

    for copy in come:
        copy.wait()

    def some(i, _):
        for way in range(ways):
            one(ways * i + way, way)
        return 0

    lax.fori_loop(0, number // ways, some, 0)


def match(odd, place, profile, x, first, second):
    number, rows, cols = x.shape
    taps = profile.shape[1] - 1
    smem = pl.BlockSpec(memory_space=pltpu.SMEM)
    vmem = pl.BlockSpec(memory_space=pltpu.VMEM)
    far = pl.BlockSpec(memory_space=pltpu.HBM)
    spans = taps + 3
    return pl.pallas_call(
        functools.partial(match_body, taps),
        in_specs=[smem, smem, vmem, far, vmem, vmem],
        out_specs=(vmem, vmem),
        out_shape=(jax.ShapeDtypeStruct((number, rows, cols // 2 + lanes), bf16),) * 2,
        scratch_shapes=[
            pltpu.VMEM(x.shape, bf16),
            pltpu.VMEM((ways, 2, cols // lanes, 96, lanes), f32),
            pltpu.VMEM((ways, 256, spans * lanes), bf16),
            pltpu.VMEM((ways, spans * lanes, 256), bf16),
            pltpu.SemaphoreType.DMA((number,)),
        ],
        compiler_params=pltpu.CompilerParams(vmem_limit_bytes=24 * mib),
        cost_estimate=pl.CostEstimate(
            flops=number * 2 * 256 * 256 * spans * lanes, bytes_accessed=4 * x.size, transcendentals=0
        ),
        name="match",
    )(odd, place, profile, x, first, second)


slots = 8


def slot_body(mine, other, out):
    number = mine.shape[0]
    per = (mine.shape[1] - 1) // 2
    patches = out.shape[0] // (slots + 1)

    def clear(p, _):
        out[p] = 0
        for s in range(slots):
            out[patches + p * slots + s] = 0
        return 0

    lax.fori_loop(0, patches, clear, 0)
    for base, labels in ((0, mine), (number, other)):

        def one(e, _):
            plane = (labels[e, 0] * 2 * number + base + e) * 256
            for k in range(per):
                p = labels[e, 1 + k]
                at = out[p]
                out[patches + p * slots + at] = plane + labels[e, 1 + per + k]
                out[p] = at + 1
            return 0

        lax.fori_loop(0, number, one, 0)


def slot_table(mine, other, patches):
    smem = pl.BlockSpec(memory_space=pltpu.SMEM)
    return pl.pallas_call(
        slot_body,
        in_specs=[smem, smem],
        out_specs=smem,
        out_shape=jax.ShapeDtypeStruct((patches * (slots + 1),), jnp.int32),
        compiler_params=pltpu.CompilerParams(vmem_limit_bytes=mib),
        name="slot_table",
    )(mine, other)


def role_pairs(step, size, shift):
    index = lambda y, x, core: ((y % size) * size + x % size) * 2 + core
    pairs = []
    for y in range(size):
        for x in range(size):
            for core in range(2):
                to = (y, x + shift) if core == step else (y + shift, x)
                pairs.append((index(y, x, core), index(*to, core)))
    return pairs


def pile_body(chunks, size, place, table, mine, other, *rest):
    outs, planes = rest[:-1], rest[-1]
    number, rows, cols = mine.shape
    tiles = cols // lanes - 1
    patches = table.shape[0] // (slots + 1)
    core = place[0]
    planes[0:number] = mine[...]
    planes[number:] = other[...]
    lane = lane_ids(16)
    tail = lax.broadcasted_iota(jnp.int32, (16, lanes), 0)

    for chunk, out in zip(chunks, outs):

        def patch(i, _):
            u = (place[1] + chunk) % size
            v = (place[2] + i) % size
            p = jnp.where(core == 0, v * size + u, u * size + v) * 2

            def some(used):
                entries = []
                for c in range(2):
                    words = [table[patches + (p + c) * slots + s] for s in range(used)]
                    entries.append(
                        [
                            ((word >> 8) & (2 * number - 1), word & 255, (word >> 12).astype(f32))
                            for word in words
                        ]
                    )
                for r in range(rows // 16):
                    for c in range(2):
                        total = [jnp.zeros((16, lanes), f32)] * tiles
                        for e, o, weight in entries[c]:
                            early = lane < o
                            before = None
                            for k in range(tiles + 1):
                                piece = planes[e, r * 16 : r * 16 + 16, k * lanes : (k + 1) * lanes]
                                turned = pltpu.roll(piece, o, 1).astype(f32)
                                if k:
                                    part = jnp.where(early, before, turned)
                                    total[k - 1] = total[k - 1] + weight * part
                                before = turned
                        for k in range(tiles):
                            at = k * rows + r * 16
                            out[2 * i + c, at : at + 16, :] = total[k].astype(out.dtype)
                for c in range(2):
                    cover = jnp.zeros((16, lanes), f32)
                    whole = jnp.zeros((16, lanes), f32)
                    for e, o, weight in entries[c]:
                        cover = cover + jnp.where(lane < o, 0.0, weight)
                        whole = whole + weight
                    last = jnp.where(tail == 0, cover, whole)
                    out[2 * i + c, tiles * rows :, :] = last.astype(out.dtype)

            used = jnp.maximum(table[p], table[p + 1])
            for top in range(2, slots + 1, 2):
                low = top - 2 if top > 2 else -1

                @pl.when((used > low) & (used <= top))
                def _():
                    some(top)

            return 0

        lax.fori_loop(0, size, patch, 0)


def pile(chunks, kinds, size, place, table, mine, other):
    number, rows, cols = mine.shape
    smem = pl.BlockSpec(memory_space=pltpu.SMEM)
    vmem = pl.BlockSpec(memory_space=pltpu.VMEM)
    shape = (2 * size, (cols // lanes - 1) * rows + 16, lanes)
    return pl.pallas_call(
        functools.partial(pile_body, chunks, size),
        in_specs=[smem, smem, vmem, vmem],
        out_specs=[vmem] * len(chunks),
        out_shape=[jax.ShapeDtypeStruct(shape, kind) for kind in kinds],
        scratch_shapes=[pltpu.VMEM((2 * number, rows, cols), bf16)],
        compiler_params=pltpu.CompilerParams(vmem_limit_bytes=8 * mib),
        cost_estimate=pl.CostEstimate(
            flops=len(chunks) * 1000000000, bytes_accessed=4 * mine.size, transcendentals=0
        ),
        name="pile_" + "_".join(str(chunk) for chunk in chunks),
    )(place, table, mine, other)


def fold_body(own, *rest):
    came, keep, sends = rest[: len(rest) // 2], rest[len(rest) // 2], rest[len(rest) // 2 + 1 :]
    rows = own.shape[1]
    for i in range(own.shape[0]):
        for at in range(0, rows, 16):
            total = own[i, at : at + 16, :]
            for ref in came:
                total = total + ref[i, at : at + 16, :].astype(f32)
            if i < 2:
                keep[i, at : at + 16, :] = total
            else:
                sends[i // 2 - 1][i % 2, at : at + 16, :] = total.astype(bf16)


def fold(own, came):
    vmem = pl.BlockSpec(memory_space=pltpu.VMEM)
    shape = (2,) + own.shape[1:]
    return pl.pallas_call(
        fold_body,
        in_specs=[vmem] * (1 + len(came)),
        out_specs=[vmem] * (1 + len(came)),
        out_shape=[jax.ShapeDtypeStruct(shape, f32)] + [jax.ShapeDtypeStruct(shape, bf16)] * len(came),
        compiler_params=pltpu.CompilerParams(vmem_limit_bytes=4 * mib),
        name="fold",
    )(own, *came)


def meet_body(place, own, *rest):
    came, mine, send = rest[:-2], rest[-2], rest[-1]
    core = place[0]
    for at in range(0, own.shape[1], 16):
        for out, i in ((mine, core), (send, 1 - core)):
            total = own[i, at : at + 16, :]
            for ref in came:
                total = total + ref[i, at : at + 16, :].astype(f32)
            out[at : at + 16, :] = total


def meet(place, own, came):
    smem = pl.BlockSpec(memory_space=pltpu.SMEM)
    vmem = pl.BlockSpec(memory_space=pltpu.VMEM)
    return pl.pallas_call(
        meet_body,
        in_specs=[smem] + [vmem] * (1 + len(came)),
        out_specs=[vmem] * 2,
        out_shape=[jax.ShapeDtypeStruct(own.shape[1:], f32)] * 2,
        compiler_params=pltpu.CompilerParams(vmem_limit_bytes=4 * mib),
        name="meet",
    )(place, own, *came)


def coadd_body(reach, odd, place, mine, other, coadd, rounded, first, second, stage):
    rows, cols = coadd.shape
    tiles = cols // lanes
    near = place[0] == 0

    def pick(low, at):
        a, b = mine[at : at + 16, :], other[at : at + 16, :]
        return jnp.where(near, a, b) if low else jnp.where(near, b, a)

    cover = pick(True, tiles // 2 * rows)
    scales = [1.0 / jnp.maximum(cover[r : r + 1, :], 1.0) for r in (0, 1)]
    for m in range(tiles):
        for b in range(group):
            at = m % (tiles // 2) * rows + b * 16
            stage[m, pl.ds(b, 16, stride=group), :] = pick(m < tiles // 2, at) * scales[min(m, 1)]
        cut = slice(m * lanes, (m + 1) * lanes)
        coadd[:, cut] = stage[m]
        rounded[:, cut] = stage[m].astype(bf16)
        low = stage[m, 0:reach, :]
        high = stage[m, rows - reach : rows, :]
        first[:, cut] = jnp.where(odd[0] == 1, low, high).astype(bf16)
        second[:, cut] = jnp.where(odd[0] == 1, high, low).astype(bf16)


def coadd_of(odd, place, mine, other, rows, cols, reach):
    edge = jax.ShapeDtypeStruct((reach, cols), bf16)
    smem = pl.BlockSpec(memory_space=pltpu.SMEM)
    vmem = pl.BlockSpec(memory_space=pltpu.VMEM)
    return pl.pallas_call(
        functools.partial(coadd_body, reach),
        in_specs=[smem, smem, vmem, vmem],
        out_specs=(vmem,) * 4,
        out_shape=(
            jax.ShapeDtypeStruct((rows, cols), f32),
            jax.ShapeDtypeStruct((rows, cols), bf16),
            edge,
            edge,
        ),
        scratch_shapes=[pltpu.VMEM((cols // lanes, rows, lanes), f32)],
        compiler_params=pltpu.CompilerParams(vmem_limit_bytes=8 * mib),
        name="coadd",
    )(odd, place, mine, other)


def bands_body(taps, psf, w):
    spans = taps + 3
    mask = band_mask(112, taps)
    clear_band(w, taps, 112, 0, spans)
    for s in range(psf.shape[0]):
        total = 0.0
        for rows_at, cols_at in zip(row_places(48, taps), lane_places(taps)):
            moved = jnp.dot(rows_at.astype(bf16), psf[s], preferred_element_type=f32)
            total = total + jnp.dot(
                moved.astype(bf16), cols_at.astype(bf16), preferred_element_type=f32
            )
        put_band(w, total, taps, mask, 0, spans, 256 * s)


def detect_bands(psf):
    scales, _, taps = psf.shape
    return pl.pallas_call(
        functools.partial(bands_body, taps),
        out_shape=jax.ShapeDtypeStruct(((taps + 3) * lanes, scales * 256), bf16),
        compiler_params=pltpu.CompilerParams(vmem_limit_bytes=12 * mib),
        name="bands",
    )(psf)


def detect_own_body(taps, w, x, acc, frame, lhs):
    reach = taps // 2
    rows, cols = x.shape
    spans = taps + 3
    for row in (0, 24 + rows):
        frame[:, :, row : row + 24, :] = jnp.zeros((2, cols // lanes, 24, lanes), f32)
    put_frame(frame, columns(x[...]), 24, reach)
    put_lhs(lhs, frame, spans, 24 - reach)
    for at in range(0, w.shape[1], 256):
        cut = slice(at, at + 256)
        acc[:, cut] = jnp.dot(lhs[...], w[:, cut], preferred_element_type=f32)


def detect_own(w, x, taps):
    rows, cols = x.shape
    spans = taps + 3
    return pl.pallas_call(
        functools.partial(detect_own_body, taps),
        out_shape=jax.ShapeDtypeStruct((256, w.shape[1]), f32),
        scratch_shapes=[
            pltpu.VMEM((2, cols // lanes, 24 + rows + 24, lanes), f32),
            pltpu.VMEM((256, spans * lanes), bf16),
        ],
        compiler_params=pltpu.CompilerParams(vmem_limit_bytes=16 * mib),
        cost_estimate=pl.CostEstimate(
            flops=2 * 256 * w.size, bytes_accessed=2 * w.size, transcendentals=0
        ),
        name="detect_own",
    )(w, x)


def detect_halo_body(taps, odd, w, first, second, acc, out, frame, lhs, stage):
    scales, rows, cols = out.shape
    count = cols // lanes
    spans = edge_spans(taps)
    frame[...] = jnp.zeros_like(frame)
    ends_at = (0, (taps + 3 - spans) * lanes)
    lane = lane_ids(16)
    lo, hi = halo_pair(odd[0] == 1, first[...], second[...])
    put_edges(taps, frame, lhs, lo, hi)
    for s in range(scales):
        at = 256 * s
        ends = [
            jnp.dot(
                lhs[side], w[row : row + spans * lanes, at : at + 256], preferred_element_type=f32
            )
            for side, row in enumerate(ends_at)
        ]
        for m in range(count):
            for h in range(2):
                cut = slice(h * lanes, (h + 1) * lanes)
                blocks = []
                for n in (m, count + m):
                    more = jnp.concatenate([end[n * 8 : n * 8 + 8, cut] for end in ends], axis=0)
                    own = acc[n * 16 : n * 16 + 16, at + h * lanes : at + (h + 1) * lanes]
                    blocks.append(own + more)
                for b, part in enumerate(split_rows(*blocks, lane)):
                    stage[s, m, pl.ds(2 * h + b, 16, stride=group), :] = part
            out[s, :, m * lanes : (m + 1) * lanes] = stage[s, m]


def detect_halo(odd, w, first, second, acc, rows, taps):
    cols = first.shape[1]
    scales = w.shape[1] // 256
    smem = pl.BlockSpec(memory_space=pltpu.SMEM)
    vmem = pl.BlockSpec(memory_space=pltpu.VMEM)
    return pl.pallas_call(
        functools.partial(detect_halo_body, taps),
        in_specs=[smem, vmem, vmem, vmem, vmem],
        out_specs=vmem,
        out_shape=jax.ShapeDtypeStruct((scales, rows, cols), f32),
        scratch_shapes=edge_scratch(taps, cols // lanes)
        + [pltpu.VMEM((scales, cols // lanes, rows, lanes), f32)],
        compiler_params=pltpu.CompilerParams(vmem_limit_bytes=16 * mib),
        name="detect_halo",
    )(odd, w, first, second, acc)


def trade(first, second):
    count = lax.axis_size("section")
    out = []
    for start, rows in ((0, first), (1, second)):
        pairs = [(i, i + 1) for i in range(start, count - 1, 2)]
        out.append(lax.ppermute(rows, "section", pairs + [(b, a) for a, b in pairs]))
    return out


def on_device(
    exposures,
    coef_code,
    coef_table,
    basis_rows,
    basis_cols,
    exposure_weight,
    intersection_patch,
    intersection_shift,
    psf_kernels,
):
    number, rows, cols = exposures.shape
    taps = basis_rows.shape[1]
    reach = taps // 2
    wide = psf_kernels.shape[-1]
    wide_reach = wide // 2
    sky = ("sy", "sx", "core")
    size = lax.axis_size("sx")
    patches = size * size * 2
    core, at_x, at_y = (lax.axis_index(name) for name in ("core", "sx", "sy"))
    place = jnp.stack([core, jnp.where(core == 0, at_x, at_y), jnp.where(core == 0, at_y, at_x)])
    odd = lax.axis_index("section") % 2

    low, high = exposures[:, :reach, :], exposures[:, rows - reach :, :]
    first, second = trade(jnp.where(odd == 1, low, high), jnp.where(odd == 1, high, low))
    odd = odd[None]

    labels = jnp.concatenate(
        [exposure_weight[:, None], intersection_patch, intersection_shift], axis=1
    )
    swap = [(0, 1), (1, 0)]
    other_labels = lax.ppermute(labels, "core", swap)

    profile = profiles(coef_code, coef_table, basis_rows.T, basis_cols.T)
    table = slot_table(labels, other_labels, patches)
    table, profile = lax.optimization_barrier((table, profile))
    mine, send = match(odd, place, profile, exposures, first, second)
    other = lax.ppermute(send, "core", swap)

    steps = (2, 3, 1)
    move = lambda rows, step, by: lax.ppermute(rows, sky, role_pairs(step, size, by))
    (far,) = pile((2,), (bf16,), size, place, table, mine, other)
    came = [move(far, 0, 2)]
    far, table = lax.optimization_barrier((far, table))
    behind, ahead = pile((3, 1), (bf16, bf16), size, place, table, mine, other)
    came += [move(behind, 0, 3), move(ahead, 0, 1)]
    ahead, table = lax.optimization_barrier((ahead, table))
    (own,) = pile((0,), (f32,), size, place, table, mine, other)
    own, psf_kernels = lax.optimization_barrier((own, psf_kernels))
    bands = detect_bands(psf_kernels)
    own, bands = lax.optimization_barrier((own, bands))
    keep, *sends = fold(own, came)
    came = [move(sends[by - 1], 1, by) for by in steps]
    mine, send = meet(place, keep, came)
    other = lax.ppermute(send, "core", swap)
    coadd, rounded, first, second = coadd_of(odd, place, mine, other, rows, cols, wide_reach)
    first, second = trade(first, second)
    acc = detect_own(bands, rounded, wide)
    detect = detect_halo(odd, bands, first, second, acc, rows, wide)
    return (coadd[None], detect[None])


def solution(mesh):
    sections, sky = mesh.devices.shape
    grid = Mesh(mesh.devices.reshape(sections, 4, sky // 8, 2), ("section", "sy", "sx", "core"))
    sky = ("sy", "sx", "core")
    return jax.shard_map(
        on_device,
        mesh=grid,
        in_specs=(
            P(sky, "section", None),
            P(sky, None),
            P(),
            P(),
            P(),
            P(sky),
            P(sky, None),
            P(sky, None),
            P(),
        ),
        out_specs=(P(sky, "section", None), P(sky, None, "section", None)),
        check_vma=False,
    )
```

```python
import functools

import jax
import jax.numpy as jnp
from jax import lax
from jax.experimental import pallas as pl
from jax.experimental.pallas import tpu as pltpu
from jax.sharding import Mesh, PartitionSpec as P

f32 = jnp.float32
bf16 = jnp.bfloat16

lanes = 128
half = 64
group = 4
mib = 1024 * 1024


def one_hot(rows, cols, at):
    row = lax.broadcasted_iota(jnp.int32, (rows, cols), 0)
    col = lax.broadcasted_iota(jnp.int32, (rows, cols), 1)
    return (col == at(row)).astype(f32)


def lane_places(taps):
    first = one_hot(taps, lanes, lambda j: (lanes - j) % lanes)
    second = one_hot(taps, lanes, lambda j: half - j)
    return first, second


def row_places(rows, taps):
    return one_hot(rows, taps, lambda t: t), one_hot(rows, taps, lambda t: t - 1)


def lane_ids(rows):
    return lax.broadcasted_iota(jnp.int32, (rows, lanes), 1)


def band_mask(depth, taps):
    k = lax.broadcasted_iota(jnp.int32, (depth, lanes), 0)
    gap = k - lane_ids(depth) % half
    return (gap >= 0) & (gap < taps)


def band_tile(row, mask):
    depth = mask.shape[0]
    wide = jnp.broadcast_to(row, (depth, lanes))
    turned = pltpu.roll(wide, 0, 1, stride=1, stride_axis=0)
    return jnp.where(mask, turned, 0.0).astype(bf16)


def put_frame(frame, tiles, row, reach):
    count = len(tiles)
    rows = tiles[0].shape[0]
    lane = lane_ids(rows)
    zero = jnp.zeros((rows, lanes), f32)
    right = [pltpu.roll(t, reach, 1).astype(f32) for t in tiles]
    left = [pltpu.roll(t, half + reach, 1).astype(f32) for t in tiles]
    for m in range(count):
        before = right[m - 1] if m else zero
        frame[0, m, row : row + rows, :] = jnp.where(lane < reach, before, right[m])
        after = left[m + 1] if m + 1 < count else zero
        frame[1, m, row : row + rows, :] = jnp.where(lane < half + reach, left[m], after)


def put_lhs(lhs, frame, spans, row):
    tiles = frame.shape[1]
    for t in range(spans):
        for par in range(2):
            for m in range(tiles):
                at = (par * tiles + m) * 16
                piece = frame[par, m, pl.ds(row + t, 16, stride=group), :]
                lhs[at : at + 16, t * lanes : (t + 1) * lanes] = piece.astype(bf16)


def split_rows(even, odd, lane):
    first = jnp.where(lane < half, even, pltpu.roll(odd, half, 1))
    second = jnp.where(lane < half, pltpu.roll(even, half, 1), odd)
    return first, second


def columns(rows):
    return [rows[:, m * lanes : (m + 1) * lanes] for m in range(rows.shape[1] // lanes)]


def put_band(w, profile, taps, mask, first, last, at):
    depth = mask.shape[0]
    for u in range(max(first - 2, 0), min(last, taps + 1)):
        tile = band_tile(profile[u : u + 1, :], mask)
        if u >= first:
            row = (u - first) * lanes
            w[row : row + depth, at : at + lanes] = tile
        if first <= u + 2 < last:
            row = (u + 2 - first) * lanes
            w[row : row + depth, at + lanes : at + 2 * lanes] = tile


def clear_band(w, taps, depth, first, last):
    width = w.shape[1]
    for t in range(first, last):
        row = (t - first) * lanes
        w[row + depth : row + lanes, :] = jnp.zeros((lanes - depth, width), bf16)
        for u, at in ((t, 0), (t - 2, lanes)):
            if not 0 <= u <= taps:
                for n in range(at, width, 2 * lanes):
                    w[row : row + depth, n : n + lanes] = jnp.zeros((depth, lanes), bf16)


def edge_spans(taps):
    return (taps // 2 + 1) // 2 * 2


def put_edge_lhs(lhs, frame, spans):
    tiles = frame.shape[1]
    for t in range(spans):
        for par in range(2):
            for m in range(0, tiles, 2):
                pair = [frame[par, m + i, pl.ds(t, 8, stride=group), :] for i in range(2)]
                at = (par * tiles + m) * 8
                lhs[at : at + 16, t * lanes : (t + 1) * lanes] = jnp.concatenate(pair, axis=0).astype(bf16)


def edge_scratch(taps, tiles, width):
    spans = edge_spans(taps)
    return [
        pltpu.VMEM((2, 2, tiles, 48, lanes), f32),
        pltpu.VMEM((2, 128, spans * lanes), bf16),
        pltpu.VMEM((2, spans * lanes, width), bf16),
    ]


def put_edges(taps, frame, lhs, lo, hi):
    reach = taps // 2
    spans = edge_spans(taps)
    put_frame(frame.at[0], columns(lo), 0, reach)
    put_frame(frame.at[1], columns(hi), 28 - reach + spans, reach)
    for side in range(2):
        put_edge_lhs(lhs.at[side], frame.at[side], spans)


def halo_pair(odd, first, second):
    return jnp.where(odd, first, second), jnp.where(odd, second, first)


ways = 4


def profile_body(code, table, base_rows, base_cols, out, g):
    number, spans, _ = out.shape
    taps = base_rows.shape[0]
    exact = lax.Precision.HIGHEST
    rows_ab = [
        jnp.dot(places, base_rows[...], precision=exact, preferred_element_type=f32)
        for places in row_places(spans, taps)
    ]
    cols_ab = [
        lax.dot_general(
            base_cols[...], places, (((0,), (0,)), ((), ())), precision=exact, preferred_element_type=f32
        )
        for places in lane_places(taps)
    ]
    for b in range(g.shape[0]):
        g[b] = sum(r[:, b : b + 1] * c[b : b + 1, :] for r, c in zip(rows_ab, cols_ab))

    def one(e, _):
        total = jnp.zeros((spans, lanes), f32)
        for b in range(g.shape[0]):
            total = total + table[b, code[e, b]] * g[b]
        out[e] = total.astype(bf16).astype(f32)
        return 0

    lax.fori_loop(0, number, one, 0)


def profiles(code, table, base_rows, base_cols):
    number, basis = code.shape
    taps = base_rows.shape[0]
    smem = pl.BlockSpec(memory_space=pltpu.SMEM)
    vmem = pl.BlockSpec(memory_space=pltpu.VMEM)
    return pl.pallas_call(
        profile_body,
        in_specs=[smem, smem, vmem, vmem],
        out_specs=vmem,
        out_shape=jax.ShapeDtypeStruct((number, taps + 1, lanes), f32),
        scratch_shapes=[pltpu.VMEM((basis, taps + 1, lanes), f32)],
        compiler_params=pltpu.CompilerParams(vmem_limit_bytes=4 * mib),
        name="profiles",
    )(code, table, base_rows, base_cols)


def match_body(taps, odd, place, profile, far, first, second, keep, send, x, frame, lhs, w, arrive):
    number, _, cols = x.shape
    reach = taps // 2
    spans = taps + 3
    count = cols // lanes
    depth = 96
    come = [pltpu.make_async_copy(far.at[e], x.at[e], arrive.at[e]) for e in range(number)]
    for copy in come:
        copy.start()
    mask = band_mask(depth, taps)
    lane = lane_ids(16)
    for way in range(ways):
        clear_band(w.at[way], taps, depth, 0, spans)

    def one(e, way):
        put_band(w.at[way], profile[e], taps, mask, 0, spans, 0)
        lo, hi = halo_pair(odd[0] == 1, first[e], second[e])
        for piece, row in ((lo, 16 - reach), (x[e], 16), (hi, 80)):
            put_frame(frame.at[way], columns(piece), row, reach)
        put_lhs(lhs.at[way], frame.at[way], spans, 16 - reach)
        acc = jnp.dot(lhs[way], w[way], preferred_element_type=f32)
        for h in range(2):
            cut = slice(h * lanes, (h + 1) * lanes)
            parts = []
            for m in range(count):
                blocks = [acc[n * 16 : n * 16 + 16, cut] for n in (m, count + m)]
                parts.append([part.astype(bf16) for part in split_rows(*blocks, lane)])
            for b in range(2):
                rows = slice((2 * h + b) * 16, (2 * h + b) * 16 + 16)
                tiles = [part[b] for part in parts]
                low = [jnp.zeros((16, lanes), bf16)] + tiles[: count // 2]
                high = tiles[count // 2 - 1 :]
                for k in range(count // 2 + 1):
                    at = slice(k * lanes, (k + 1) * lanes)
                    keep[e, rows, at] = jnp.where(place[0] == 0, low[k], high[k])
                    send[e, rows, at] = jnp.where(place[0] == 0, high[k], low[k])

    for copy in come:
        copy.wait()

    def some(i, _):
        for way in range(ways):
            one(ways * i + way, way)
        return 0

    lax.fori_loop(0, number // ways, some, 0)


def match(odd, place, profile, x, first, second):
    number, rows, cols = x.shape
    taps = profile.shape[1] - 1
    smem = pl.BlockSpec(memory_space=pltpu.SMEM)
    vmem = pl.BlockSpec(memory_space=pltpu.VMEM)
    far = pl.BlockSpec(memory_space=pltpu.HBM)
    spans = taps + 3
    return pl.pallas_call(
        functools.partial(match_body, taps),
        in_specs=[smem, smem, vmem, far, vmem, vmem],
        out_specs=(vmem, vmem),
        out_shape=(jax.ShapeDtypeStruct((number, rows, cols // 2 + lanes), bf16),) * 2,
        scratch_shapes=[
            pltpu.VMEM(x.shape, bf16),
            pltpu.VMEM((ways, 2, cols // lanes, 96, lanes), f32),
            pltpu.VMEM((ways, 256, spans * lanes), bf16),
            pltpu.VMEM((ways, spans * lanes, 256), bf16),
            pltpu.SemaphoreType.DMA((number,)),
        ],
        compiler_params=pltpu.CompilerParams(vmem_limit_bytes=24 * mib),
        cost_estimate=pl.CostEstimate(
            flops=number * 2 * 256 * 256 * spans * lanes, bytes_accessed=4 * x.size, transcendentals=0
        ),
        name="match",
    )(odd, place, profile, x, first, second)


slots = 8


def slot_body(mine, other, out):
    number = mine.shape[0]
    per = (mine.shape[1] - 1) // 2
    patches = out.shape[0] // (slots + 1)

    def clear(p, _):
        out[p] = 0
        for s in range(slots):
            out[patches + p * slots + s] = 0
        return 0

    lax.fori_loop(0, patches, clear, 0)
    for base, labels in ((0, mine), (number, other)):

        def one(e, _):
            plane = (labels[e, 0] * 2 * number + base + e) * 256
            for k in range(per):
                p = labels[e, 1 + k]
                at = out[p]
                out[patches + p * slots + at] = plane + labels[e, 1 + per + k]
                out[p] = at + 1
            return 0

        lax.fori_loop(0, number, one, 0)


def slot_table(mine, other, patches):
    smem = pl.BlockSpec(memory_space=pltpu.SMEM)
    return pl.pallas_call(
        slot_body,
        in_specs=[smem, smem],
        out_specs=smem,
        out_shape=jax.ShapeDtypeStruct((patches * (slots + 1),), jnp.int32),
        compiler_params=pltpu.CompilerParams(vmem_limit_bytes=mib),
        name="slot_table",
    )(mine, other)


def role_pairs(step, size, shift):
    index = lambda y, x, core: ((y % size) * size + x % size) * 2 + core
    pairs = []
    for y in range(size):
        for x in range(size):
            for core in range(2):
                to = (y, x + shift) if core == step else (y + shift, x)
                pairs.append((index(y, x, core), index(*to, core)))
    return pairs


def pile_body(chunks, size, place, table, mine, other, *rest):
    outs, planes = rest[:-1], rest[-1]
    number, rows, cols = mine.shape
    tiles = cols // lanes - 1
    patches = table.shape[0] // (slots + 1)
    core = place[0]
    planes[0:number] = mine[...]
    planes[number:] = other[...]
    lane = lane_ids(16)
    tail = lax.broadcasted_iota(jnp.int32, (16, lanes), 0)

    for chunk, out in zip(chunks, outs):

        def patch(i, _):
            u = (place[1] + chunk) % size
            v = (place[2] + i) % size
            p = jnp.where(core == 0, v * size + u, u * size + v) * 2

            def some(used):
                entries = []
                for c in range(2):
                    words = [table[patches + (p + c) * slots + s] for s in range(used)]
                    entries.append(
                        [
                            ((word >> 8) & (2 * number - 1), word & 255, (word >> 12).astype(f32))
                            for word in words
                        ]
                    )
                for r in range(rows // 16):
                    for c in range(2):
                        total = [jnp.zeros((16, lanes), f32)] * tiles
                        for e, o, weight in entries[c]:
                            early = lane < o
                            before = None
                            for k in range(tiles + 1):
                                piece = planes[e, r * 16 : r * 16 + 16, k * lanes : (k + 1) * lanes]
                                turned = pltpu.roll(piece, o, 1).astype(f32)
                                if k:
                                    part = jnp.where(early, before, turned)
                                    total[k - 1] = total[k - 1] + weight * part
                                before = turned
                        for k in range(tiles):
                            at = k * rows + r * 16
                            out[2 * i + c, at : at + 16, :] = total[k].astype(out.dtype)
                for c in range(2):
                    cover = jnp.zeros((16, lanes), f32)
                    whole = jnp.zeros((16, lanes), f32)
                    for e, o, weight in entries[c]:
                        cover = cover + jnp.where(lane < o, 0.0, weight)
                        whole = whole + weight
                    last = jnp.where(tail == 0, cover, whole)
                    out[2 * i + c, tiles * rows :, :] = last.astype(out.dtype)

            used = jnp.maximum(table[p], table[p + 1])
            for top in range(2, slots + 1, 2):
                low = top - 2 if top > 2 else -1

                @pl.when((used > low) & (used <= top))
                def _():
                    some(top)

            return 0

        lax.fori_loop(0, size, patch, 0)


def pile(chunks, kinds, size, place, table, mine, other):
    number, rows, cols = mine.shape
    smem = pl.BlockSpec(memory_space=pltpu.SMEM)
    vmem = pl.BlockSpec(memory_space=pltpu.VMEM)
    shape = (2 * size, (cols // lanes - 1) * rows + 16, lanes)
    return pl.pallas_call(
        functools.partial(pile_body, chunks, size),
        in_specs=[smem, smem, vmem, vmem],
        out_specs=[vmem] * len(chunks),
        out_shape=[jax.ShapeDtypeStruct(shape, kind) for kind in kinds],
        scratch_shapes=[pltpu.VMEM((2 * number, rows, cols), bf16)],
        compiler_params=pltpu.CompilerParams(vmem_limit_bytes=8 * mib),
        cost_estimate=pl.CostEstimate(
            flops=len(chunks) * 1000000000, bytes_accessed=4 * mine.size, transcendentals=0
        ),
        name="pile_" + "_".join(str(chunk) for chunk in chunks),
    )(place, table, mine, other)


def fold_body(own, *rest):
    came, keep, sends = rest[: len(rest) // 2], rest[len(rest) // 2], rest[len(rest) // 2 + 1 :]
    rows = own.shape[1]
    for i in range(own.shape[0]):
        for at in range(0, rows, 16):
            total = own[i, at : at + 16, :]
            for ref in came:
                total = total + ref[i, at : at + 16, :].astype(f32)
            if i < 2:
                keep[i, at : at + 16, :] = total
            else:
                sends[i // 2 - 1][i % 2, at : at + 16, :] = total.astype(bf16)


def fold(own, came):
    vmem = pl.BlockSpec(memory_space=pltpu.VMEM)
    shape = (2,) + own.shape[1:]
    return pl.pallas_call(
        fold_body,
        in_specs=[vmem] * (1 + len(came)),
        out_specs=[vmem] * (1 + len(came)),
        out_shape=[jax.ShapeDtypeStruct(shape, f32)] + [jax.ShapeDtypeStruct(shape, bf16)] * len(came),
        compiler_params=pltpu.CompilerParams(vmem_limit_bytes=4 * mib),
        name="fold",
    )(own, *came)


def meet_body(place, own, *rest):
    came, mine, send = rest[:-2], rest[-2], rest[-1]
    core = place[0]
    for at in range(0, own.shape[1], 16):
        for out, i in ((mine, core), (send, 1 - core)):
            total = own[i, at : at + 16, :]
            for ref in came:
                total = total + ref[i, at : at + 16, :].astype(f32)
            out[at : at + 16, :] = total


def meet(place, own, came):
    smem = pl.BlockSpec(memory_space=pltpu.SMEM)
    vmem = pl.BlockSpec(memory_space=pltpu.VMEM)
    return pl.pallas_call(
        meet_body,
        in_specs=[smem] + [vmem] * (1 + len(came)),
        out_specs=[vmem] * 2,
        out_shape=[jax.ShapeDtypeStruct(own.shape[1:], f32)] * 2,
        compiler_params=pltpu.CompilerParams(vmem_limit_bytes=4 * mib),
        name="meet",
    )(place, own, *came)


def coadd_body(reach, odd, place, mine, other, coadd, rounded, first, second, stage):
    rows, cols = coadd.shape
    tiles = cols // lanes
    near = place[0] == 0

    def pick(low, at):
        a, b = mine[at : at + 16, :], other[at : at + 16, :]
        return jnp.where(near, a, b) if low else jnp.where(near, b, a)

    cover = pick(True, tiles // 2 * rows)
    scales = [1.0 / jnp.maximum(cover[r : r + 1, :], 1.0) for r in (0, 1)]
    for m in range(tiles):
        for b in range(group):
            at = m % (tiles // 2) * rows + b * 16
            stage[m, pl.ds(b, 16, stride=group), :] = pick(m < tiles // 2, at) * scales[min(m, 1)]
        cut = slice(m * lanes, (m + 1) * lanes)
        coadd[:, cut] = stage[m]
        rounded[:, cut] = stage[m].astype(bf16)
        low = stage[m, 0:reach, :]
        high = stage[m, rows - reach : rows, :]
        first[:, cut] = jnp.where(odd[0] == 1, low, high).astype(bf16)
        second[:, cut] = jnp.where(odd[0] == 1, high, low).astype(bf16)


def coadd_of(odd, place, mine, other, rows, cols, reach):
    edge = jax.ShapeDtypeStruct((reach, cols), bf16)
    smem = pl.BlockSpec(memory_space=pltpu.SMEM)
    vmem = pl.BlockSpec(memory_space=pltpu.VMEM)
    return pl.pallas_call(
        functools.partial(coadd_body, reach),
        in_specs=[smem, smem, vmem, vmem],
        out_specs=(vmem,) * 4,
        out_shape=(
            jax.ShapeDtypeStruct((rows, cols), f32),
            jax.ShapeDtypeStruct((rows, cols), bf16),
            edge,
            edge,
        ),
        scratch_shapes=[pltpu.VMEM((cols // lanes, rows, lanes), f32)],
        compiler_params=pltpu.CompilerParams(vmem_limit_bytes=8 * mib),
        name="coadd",
    )(odd, place, mine, other)


def detect_own_body(taps, psf, x, acc, profile, frame, lhs, w):
    reach = taps // 2
    rows, cols = x.shape
    spans = taps + 3
    mask = band_mask(112, taps)
    for row in (0, 24 + rows):
        frame[:, :, row : row + 24, :] = jnp.zeros((2, cols // lanes, 24, lanes), f32)
    put_frame(frame, columns(x[...]), 24, reach)
    put_lhs(lhs, frame, spans, 24 - reach)
    clear_band(w, taps, 112, 0, spans)
    for s in range(psf.shape[0]):
        total = 0.0
        for rows_at, cols_at in zip(row_places(profile.shape[1], taps), lane_places(taps)):
            moved = jnp.dot(rows_at.astype(bf16), psf[s], preferred_element_type=f32)
            total = total + jnp.dot(
                moved.astype(bf16), cols_at.astype(bf16), preferred_element_type=f32
            )
        profile[s] = total
        put_band(w, total, taps, mask, 0, spans, 256 * s)
        cut = slice(256 * s, 256 * s + 256)
        acc[:, cut] = jnp.dot(lhs[...], w[:, cut], preferred_element_type=f32)


def detect_own(psf, x):
    rows, cols = x.shape
    scales, _, taps = psf.shape
    spans = taps + 3
    return pl.pallas_call(
        functools.partial(detect_own_body, taps),
        out_shape=(
            jax.ShapeDtypeStruct((256, scales * 256), f32),
            jax.ShapeDtypeStruct((scales, 48, lanes), f32),
        ),
        scratch_shapes=[
            pltpu.VMEM((2, cols // lanes, 24 + rows + 24, lanes), f32),
            pltpu.VMEM((256, spans * lanes), bf16),
            pltpu.VMEM((spans * lanes, scales * 256), bf16),
        ],
        compiler_params=pltpu.CompilerParams(vmem_limit_bytes=20 * mib),
        cost_estimate=pl.CostEstimate(
            flops=scales * 2 * 256 * 256 * spans * lanes, bytes_accessed=4 * x.size, transcendentals=0
        ),
        name="detect_own",
    )(psf, x)


def detect_halo_body(taps, odd, profile, first, second, acc, out, frame, lhs, w, stage):
    scales, rows, cols = out.shape
    count = cols // lanes
    spans = edge_spans(taps)
    frame[...] = jnp.zeros_like(frame)
    clear_band(w.at[0], taps, 112, 0, spans)
    clear_band(w.at[1], taps, 112, taps + 3 - spans, taps + 3)
    mask = band_mask(112, taps)
    lane = lane_ids(16)
    lo, hi = halo_pair(odd[0] == 1, first[...], second[...])
    put_edges(taps, frame, lhs, lo, hi)
    for s in range(scales):
        at = 256 * s
        put_band(w.at[0], profile[s], taps, mask, 0, spans, at)
        put_band(w.at[1], profile[s], taps, mask, taps + 3 - spans, taps + 3, at)
        ends = [
            jnp.dot(lhs[side], w[side, :, at : at + 256], preferred_element_type=f32)
            for side in range(2)
        ]
        for m in range(count):
            for h in range(2):
                cut = slice(h * lanes, (h + 1) * lanes)
                blocks = []
                for n in (m, count + m):
                    more = jnp.concatenate([end[n * 8 : n * 8 + 8, cut] for end in ends], axis=0)
                    own = acc[n * 16 : n * 16 + 16, at + h * lanes : at + (h + 1) * lanes]
                    blocks.append(own + more)
                for b, part in enumerate(split_rows(*blocks, lane)):
                    stage[s, m, pl.ds(2 * h + b, 16, stride=group), :] = part
            out[s, :, m * lanes : (m + 1) * lanes] = stage[s, m]


def detect_halo(odd, profile, first, second, acc, rows, taps):
    cols = first.shape[1]
    scales = profile.shape[0]
    smem = pl.BlockSpec(memory_space=pltpu.SMEM)
    vmem = pl.BlockSpec(memory_space=pltpu.VMEM)
    return pl.pallas_call(
        functools.partial(detect_halo_body, taps),
        in_specs=[smem, vmem, vmem, vmem, vmem],
        out_specs=vmem,
        out_shape=jax.ShapeDtypeStruct((scales, rows, cols), f32),
        scratch_shapes=edge_scratch(taps, cols // lanes, scales * 256)
        + [pltpu.VMEM((scales, cols // lanes, rows, lanes), f32)],
        compiler_params=pltpu.CompilerParams(vmem_limit_bytes=20 * mib),
        name="detect_halo",
    )(odd, profile, first, second, acc)


def trade(first, second):
    count = lax.axis_size("section")
    out = []
    for start, rows in ((0, first), (1, second)):
        pairs = [(i, i + 1) for i in range(start, count - 1, 2)]
        out.append(lax.ppermute(rows, "section", pairs + [(b, a) for a, b in pairs]))
    return out


def on_device(
    exposures,
    coef_code,
    coef_table,
    basis_rows,
    basis_cols,
    exposure_weight,
    intersection_patch,
    intersection_shift,
    psf_kernels,
):
    number, rows, cols = exposures.shape
    taps = basis_rows.shape[1]
    reach = taps // 2
    wide = psf_kernels.shape[-1]
    wide_reach = wide // 2
    sky = ("sy", "sx", "core")
    size = lax.axis_size("sx")
    patches = size * size * 2
    core, at_x, at_y = (lax.axis_index(name) for name in ("core", "sx", "sy"))
    place = jnp.stack([core, jnp.where(core == 0, at_x, at_y), jnp.where(core == 0, at_y, at_x)])
    odd = lax.axis_index("section") % 2

    low, high = exposures[:, :reach, :], exposures[:, rows - reach :, :]
    first, second = trade(jnp.where(odd == 1, low, high), jnp.where(odd == 1, high, low))
    odd = odd[None]

    labels = jnp.concatenate(
        [exposure_weight[:, None], intersection_patch, intersection_shift], axis=1
    )
    swap = [(0, 1), (1, 0)]
    other_labels = lax.ppermute(labels, "core", swap)

    profile = profiles(coef_code, coef_table, basis_rows.T, basis_cols.T)
    table = slot_table(labels, other_labels, patches)
    table, profile = lax.optimization_barrier((table, profile))
    mine, send = match(odd, place, profile, exposures, first, second)
    other = lax.ppermute(send, "core", swap)

    steps = (2, 3, 1)
    move = lambda rows, step, by: lax.ppermute(rows, sky, role_pairs(step, size, by))
    (far,) = pile((2,), (bf16,), size, place, table, mine, other)
    came = [move(far, 0, 2)]
    far, table = lax.optimization_barrier((far, table))
    behind, ahead = pile((3, 1), (bf16, bf16), size, place, table, mine, other)
    came += [move(behind, 0, 3), move(ahead, 0, 1)]
    ahead, table = lax.optimization_barrier((ahead, table))
    (own,) = pile((0,), (f32,), size, place, table, mine, other)
    keep, *sends = fold(own, came)
    came = [move(sends[by - 1], 1, by) for by in steps]
    mine, send = meet(place, keep, came)
    other = lax.ppermute(send, "core", swap)
    coadd, rounded, first, second = coadd_of(odd, place, mine, other, rows, cols, wide_reach)
    first, second = trade(first, second)
    acc, profile = detect_own(psf_kernels, rounded)
    detect = detect_halo(odd, profile, first, second, acc, rows, wide)
    return (coadd[None], detect[None])


def solution(mesh):
    sections, sky = mesh.devices.shape
    grid = Mesh(mesh.devices.reshape(sections, 4, sky // 8, 2), ("section", "sy", "sx", "core"))
    sky = ("sy", "sx", "core")
    return jax.shard_map(
        on_device,
        mesh=grid,
        in_specs=(
            P(sky, "section", None),
            P(sky, None),
            P(),
            P(),
            P(),
            P(sky),
            P(sky, None),
            P(sky, None),
            P(),
        ),
        out_specs=(P(sky, "section", None), P(sky, None, "section", None)),
        check_vma=False,
    )
```

```python
import functools

import jax
import jax.numpy as jnp
from jax import lax
from jax.experimental import pallas as pl
from jax.experimental.pallas import tpu as pltpu
from jax.sharding import Mesh, PartitionSpec as P

f32 = jnp.float32
bf16 = jnp.bfloat16

lanes = 128
half = 64
group = 4
mib = 1024 * 1024


def one_hot(rows, cols, at):
    row = lax.broadcasted_iota(jnp.int32, (rows, cols), 0)
    col = lax.broadcasted_iota(jnp.int32, (rows, cols), 1)
    return (col == at(row)).astype(f32)


def lane_places(taps):
    first = one_hot(taps, lanes, lambda j: (lanes - j) % lanes)
    second = one_hot(taps, lanes, lambda j: half - j)
    return first, second


def row_places(rows, taps):
    return one_hot(rows, taps, lambda t: t), one_hot(rows, taps, lambda t: t - 1)


def lane_ids(rows):
    return lax.broadcasted_iota(jnp.int32, (rows, lanes), 1)


def band_mask(depth, taps):
    k = lax.broadcasted_iota(jnp.int32, (depth, lanes), 0)
    gap = k - lane_ids(depth) % half
    return (gap >= 0) & (gap < taps)


def band_tile(row, mask):
    depth = mask.shape[0]
    wide = jnp.broadcast_to(row, (depth, lanes))
    turned = pltpu.roll(wide, 0, 1, stride=1, stride_axis=0)
    return jnp.where(mask, turned, 0.0).astype(bf16)


def put_frame(frame, tiles, row, reach):
    count = len(tiles)
    rows = tiles[0].shape[0]
    lane = lane_ids(rows)
    zero = jnp.zeros((rows, lanes), f32)
    right = [pltpu.roll(t, reach, 1).astype(f32) for t in tiles]
    left = [pltpu.roll(t, half + reach, 1).astype(f32) for t in tiles]
    for m in range(count):
        before = right[m - 1] if m else zero
        frame[0, m, row : row + rows, :] = jnp.where(lane < reach, before, right[m])
        after = left[m + 1] if m + 1 < count else zero
        frame[1, m, row : row + rows, :] = jnp.where(lane < half + reach, left[m], after)


def put_lhs(lhs, frame, spans, row):
    tiles = frame.shape[1]
    for t in range(spans):
        for par in range(2):
            for m in range(tiles):
                at = (par * tiles + m) * 16
                piece = frame[par, m, pl.ds(row + t, 16, stride=group), :]
                lhs[at : at + 16, t * lanes : (t + 1) * lanes] = piece.astype(bf16)


def split_rows(even, odd, lane):
    first = jnp.where(lane < half, even, pltpu.roll(odd, half, 1))
    second = jnp.where(lane < half, pltpu.roll(even, half, 1), odd)
    return first, second


def columns(rows):
    return [rows[:, m * lanes : (m + 1) * lanes] for m in range(rows.shape[1] // lanes)]


def put_band(w, profile, taps, mask, first, last, at):
    depth = mask.shape[0]
    for u in range(max(first - 2, 0), min(last, taps + 1)):
        tile = band_tile(profile[u : u + 1, :], mask)
        if u >= first:
            row = (u - first) * lanes
            w[row : row + depth, at : at + lanes] = tile
        if first <= u + 2 < last:
            row = (u + 2 - first) * lanes
            w[row : row + depth, at + lanes : at + 2 * lanes] = tile


def clear_band(w, taps, depth, first, last):
    width = w.shape[1]
    for t in range(first, last):
        row = (t - first) * lanes
        w[row + depth : row + lanes, :] = jnp.zeros((lanes - depth, width), bf16)
        for u, at in ((t, 0), (t - 2, lanes)):
            if not 0 <= u <= taps:
                for n in range(at, width, 2 * lanes):
                    w[row : row + depth, n : n + lanes] = jnp.zeros((depth, lanes), bf16)


def edge_spans(taps):
    return (taps // 2 + 1) // 2 * 2


def put_edge_lhs(lhs, frame, spans):
    tiles = frame.shape[1]
    for t in range(spans):
        for par in range(2):
            for m in range(0, tiles, 2):
                pair = [frame[par, m + i, pl.ds(t, 8, stride=group), :] for i in range(2)]
                at = (par * tiles + m) * 8
                lhs[at : at + 16, t * lanes : (t + 1) * lanes] = jnp.concatenate(pair, axis=0).astype(bf16)


def edge_scratch(taps, tiles, width):
    spans = edge_spans(taps)
    return [
        pltpu.VMEM((2, 2, tiles, 48, lanes), f32),
        pltpu.VMEM((2, 128, spans * lanes), bf16),
        pltpu.VMEM((2, spans * lanes, width), bf16),
    ]


def put_edges(taps, frame, lhs, lo, hi):
    reach = taps // 2
    spans = edge_spans(taps)
    put_frame(frame.at[0], columns(lo), 0, reach)
    put_frame(frame.at[1], columns(hi), 28 - reach + spans, reach)
    for side in range(2):
        put_edge_lhs(lhs.at[side], frame.at[side], spans)


def halo_pair(odd, first, second):
    return jnp.where(odd, first, second), jnp.where(odd, second, first)


ways = 8


def profile_body(code, table, base_rows, base_cols, out, g):
    number, spans, _ = out.shape
    taps = base_rows.shape[0]
    exact = lax.Precision.HIGHEST
    rows_ab = [
        jnp.dot(places, base_rows[...], precision=exact, preferred_element_type=f32)
        for places in row_places(spans, taps)
    ]
    cols_ab = [
        lax.dot_general(
            base_cols[...], places, (((0,), (0,)), ((), ())), precision=exact, preferred_element_type=f32
        )
        for places in lane_places(taps)
    ]
    for b in range(g.shape[0]):
        g[b] = sum(r[:, b : b + 1] * c[b : b + 1, :] for r, c in zip(rows_ab, cols_ab))

    def one(e, _):
        total = jnp.zeros((spans, lanes), f32)
        for b in range(g.shape[0]):
            total = total + table[b, code[e, b]] * g[b]
        out[e] = total.astype(bf16).astype(f32)
        return 0

    lax.fori_loop(0, number, one, 0)


def profiles(code, table, base_rows, base_cols):
    number, basis = code.shape
    taps = base_rows.shape[0]
    smem = pl.BlockSpec(memory_space=pltpu.SMEM)
    vmem = pl.BlockSpec(memory_space=pltpu.VMEM)
    return pl.pallas_call(
        profile_body,
        in_specs=[smem, smem, vmem, vmem],
        out_specs=vmem,
        out_shape=jax.ShapeDtypeStruct((number, taps + 1, lanes), f32),
        scratch_shapes=[pltpu.VMEM((basis, taps + 1, lanes), f32)],
        compiler_params=pltpu.CompilerParams(vmem_limit_bytes=4 * mib),
        name="profiles",
    )(code, table, base_rows, base_cols)


def match_body(taps, odd, place, profile, x, first, second, keep, send, frame, lhs, w):
    number, _, cols = x.shape
    reach = taps // 2
    spans = taps + 3
    count = cols // lanes
    depth = 96
    mask = band_mask(depth, taps)
    lane = lane_ids(16)
    for way in range(ways):
        clear_band(w.at[way], taps, depth, 0, spans)

    def one(e, way):
        put_band(w.at[way], profile[e], taps, mask, 0, spans, 0)
        lo, hi = halo_pair(odd[0] == 1, first[e], second[e])
        for piece, row in ((lo, 16 - reach), (x[e], 16), (hi, 80)):
            put_frame(frame.at[way], columns(piece), row, reach)
        put_lhs(lhs.at[way], frame.at[way], spans, 16 - reach)
        acc = jnp.dot(lhs[way], w[way], preferred_element_type=f32)
        for h in range(2):
            cut = slice(h * lanes, (h + 1) * lanes)
            parts = []
            for m in range(count):
                blocks = [acc[n * 16 : n * 16 + 16, cut] for n in (m, count + m)]
                parts.append([part.astype(bf16) for part in split_rows(*blocks, lane)])
            for b in range(2):
                rows = slice((2 * h + b) * 16, (2 * h + b) * 16 + 16)
                tiles = [part[b] for part in parts]
                low = [jnp.zeros((16, lanes), bf16)] + tiles[: count // 2]
                high = tiles[count // 2 - 1 :]
                for k in range(count // 2 + 1):
                    at = slice(k * lanes, (k + 1) * lanes)
                    keep[e, rows, at] = jnp.where(place[0] == 0, low[k], high[k])
                    send[e, rows, at] = jnp.where(place[0] == 0, high[k], low[k])

    def some(i, _):
        for way in range(ways):
            one(ways * i + way, way)
        return 0

    lax.fori_loop(0, number // ways, some, 0)


def match(odd, place, profile, x, first, second):
    number, rows, cols = x.shape
    taps = profile.shape[1] - 1
    smem = pl.BlockSpec(memory_space=pltpu.SMEM)
    vmem = pl.BlockSpec(memory_space=pltpu.VMEM)
    spans = taps + 3
    return pl.pallas_call(
        functools.partial(match_body, taps),
        in_specs=[smem, smem] + [vmem] * 4,
        out_specs=(vmem, vmem),
        out_shape=(jax.ShapeDtypeStruct((number, rows, cols // 2 + lanes), bf16),) * 2,
        scratch_shapes=[
            pltpu.VMEM((ways, 2, cols // lanes, 96, lanes), f32),
            pltpu.VMEM((ways, 256, spans * lanes), bf16),
            pltpu.VMEM((ways, spans * lanes, 256), bf16),
        ],
        compiler_params=pltpu.CompilerParams(vmem_limit_bytes=40 * mib),
        cost_estimate=pl.CostEstimate(
            flops=number * 2 * 256 * 256 * spans * lanes, bytes_accessed=4 * x.size, transcendentals=0
        ),
        name="match",
    )(odd, place, profile, x, first, second)


slots = 8


def slot_body(mine, other, out):
    number = mine.shape[0]
    per = (mine.shape[1] - 1) // 2
    patches = out.shape[0] // (slots + 1)

    def clear(p, _):
        out[p] = 0
        for s in range(slots):
            out[patches + p * slots + s] = 0
        return 0

    lax.fori_loop(0, patches, clear, 0)
    for base, labels in ((0, mine), (number, other)):

        def one(e, _):
            plane = (labels[e, 0] * 2 * number + base + e) * 256
            for k in range(per):
                p = labels[e, 1 + k]
                at = out[p]
                out[patches + p * slots + at] = plane + labels[e, 1 + per + k]
                out[p] = at + 1
            return 0

        lax.fori_loop(0, number, one, 0)


def slot_table(mine, other, patches):
    smem = pl.BlockSpec(memory_space=pltpu.SMEM)
    return pl.pallas_call(
        slot_body,
        in_specs=[smem, smem],
        out_specs=smem,
        out_shape=jax.ShapeDtypeStruct((patches * (slots + 1),), jnp.int32),
        compiler_params=pltpu.CompilerParams(vmem_limit_bytes=mib),
        name="slot_table",
    )(mine, other)


def role_pairs(step, size, shift):
    index = lambda y, x, core: ((y % size) * size + x % size) * 2 + core
    pairs = []
    for y in range(size):
        for x in range(size):
            for core in range(2):
                to = (y, x + shift) if core == step else (y + shift, x)
                pairs.append((index(y, x, core), index(*to, core)))
    return pairs


def pile_body(chunks, size, place, table, mine, other, *rest):
    outs, planes = rest[:-1], rest[-1]
    number, rows, cols = mine.shape
    tiles = cols // lanes - 1
    patches = table.shape[0] // (slots + 1)
    core = place[0]
    planes[0:number] = mine[...]
    planes[number:] = other[...]
    lane = lane_ids(16)
    tail = lax.broadcasted_iota(jnp.int32, (16, lanes), 0)

    for chunk, out in zip(chunks, outs):

        def patch(i, _):
            u = (place[1] + chunk) % size
            v = (place[2] + i) % size
            p = jnp.where(core == 0, v * size + u, u * size + v) * 2

            def some(used):
                entries = []
                for c in range(2):
                    words = [table[patches + (p + c) * slots + s] for s in range(used)]
                    entries.append(
                        [
                            ((word >> 8) & (2 * number - 1), word & 255, (word >> 12).astype(f32))
                            for word in words
                        ]
                    )
                for r in range(rows // 16):
                    for c in range(2):
                        total = [jnp.zeros((16, lanes), f32)] * tiles
                        for e, o, weight in entries[c]:
                            early = lane < o
                            before = None
                            for k in range(tiles + 1):
                                piece = planes[e, r * 16 : r * 16 + 16, k * lanes : (k + 1) * lanes]
                                turned = pltpu.roll(piece, o, 1).astype(f32)
                                if k:
                                    part = jnp.where(early, before, turned)
                                    total[k - 1] = total[k - 1] + weight * part
                                before = turned
                        for k in range(tiles):
                            at = k * rows + r * 16
                            out[2 * i + c, at : at + 16, :] = total[k].astype(out.dtype)
                for c in range(2):
                    cover = jnp.zeros((16, lanes), f32)
                    whole = jnp.zeros((16, lanes), f32)
                    for e, o, weight in entries[c]:
                        cover = cover + jnp.where(lane < o, 0.0, weight)
                        whole = whole + weight
                    last = jnp.where(tail == 0, cover, whole)
                    out[2 * i + c, tiles * rows :, :] = last.astype(out.dtype)

            used = jnp.maximum(table[p], table[p + 1])
            for top in range(2, slots + 1, 2):
                low = top - 2 if top > 2 else -1

                @pl.when((used > low) & (used <= top))
                def _():
                    some(top)

            return 0

        lax.fori_loop(0, size, patch, 0)


def pile(chunks, kinds, size, place, table, mine, other):
    number, rows, cols = mine.shape
    smem = pl.BlockSpec(memory_space=pltpu.SMEM)
    vmem = pl.BlockSpec(memory_space=pltpu.VMEM)
    shape = (2 * size, (cols // lanes - 1) * rows + 16, lanes)
    return pl.pallas_call(
        functools.partial(pile_body, chunks, size),
        in_specs=[smem, smem, vmem, vmem],
        out_specs=[vmem] * len(chunks),
        out_shape=[jax.ShapeDtypeStruct(shape, kind) for kind in kinds],
        scratch_shapes=[pltpu.VMEM((2 * number, rows, cols), bf16)],
        compiler_params=pltpu.CompilerParams(vmem_limit_bytes=8 * mib),
        cost_estimate=pl.CostEstimate(
            flops=len(chunks) * 1000000000, bytes_accessed=4 * mine.size, transcendentals=0
        ),
        name="pile_" + "_".join(str(chunk) for chunk in chunks),
    )(place, table, mine, other)


def fold_body(own, *rest):
    came, keep, sends = rest[: len(rest) // 2], rest[len(rest) // 2], rest[len(rest) // 2 + 1 :]
    rows = own.shape[1]
    for i in range(own.shape[0]):
        for at in range(0, rows, 16):
            total = own[i, at : at + 16, :]
            for ref in came:
                total = total + ref[i, at : at + 16, :].astype(f32)
            if i < 2:
                keep[i, at : at + 16, :] = total
            else:
                sends[i // 2 - 1][i % 2, at : at + 16, :] = total.astype(bf16)


def fold(own, came):
    vmem = pl.BlockSpec(memory_space=pltpu.VMEM)
    shape = (2,) + own.shape[1:]
    return pl.pallas_call(
        fold_body,
        in_specs=[vmem] * (1 + len(came)),
        out_specs=[vmem] * (1 + len(came)),
        out_shape=[jax.ShapeDtypeStruct(shape, f32)] + [jax.ShapeDtypeStruct(shape, bf16)] * len(came),
        compiler_params=pltpu.CompilerParams(vmem_limit_bytes=4 * mib),
        name="fold",
    )(own, *came)


def meet_body(place, own, *rest):
    came, mine, send = rest[:-2], rest[-2], rest[-1]
    core = place[0]
    for at in range(0, own.shape[1], 16):
        for out, i in ((mine, core), (send, 1 - core)):
            total = own[i, at : at + 16, :]
            for ref in came:
                total = total + ref[i, at : at + 16, :].astype(f32)
            out[at : at + 16, :] = total


def meet(place, own, came):
    smem = pl.BlockSpec(memory_space=pltpu.SMEM)
    vmem = pl.BlockSpec(memory_space=pltpu.VMEM)
    return pl.pallas_call(
        meet_body,
        in_specs=[smem] + [vmem] * (1 + len(came)),
        out_specs=[vmem] * 2,
        out_shape=[jax.ShapeDtypeStruct(own.shape[1:], f32)] * 2,
        compiler_params=pltpu.CompilerParams(vmem_limit_bytes=4 * mib),
        name="meet",
    )(place, own, *came)


def coadd_body(reach, odd, place, mine, other, coadd, rounded, first, second, stage):
    rows, cols = coadd.shape
    tiles = cols // lanes
    near = place[0] == 0

    def pick(low, at):
        a, b = mine[at : at + 16, :], other[at : at + 16, :]
        return jnp.where(near, a, b) if low else jnp.where(near, b, a)

    cover = pick(True, tiles // 2 * rows)
    scales = [1.0 / jnp.maximum(cover[r : r + 1, :], 1.0) for r in (0, 1)]
    for m in range(tiles):
        for b in range(group):
            at = m % (tiles // 2) * rows + b * 16
            stage[m, pl.ds(b, 16, stride=group), :] = pick(m < tiles // 2, at) * scales[min(m, 1)]
        cut = slice(m * lanes, (m + 1) * lanes)
        coadd[:, cut] = stage[m]
        rounded[:, cut] = stage[m].astype(bf16)
        low = stage[m, 0:reach, :]
        high = stage[m, rows - reach : rows, :]
        first[:, cut] = jnp.where(odd[0] == 1, low, high).astype(bf16)
        second[:, cut] = jnp.where(odd[0] == 1, high, low).astype(bf16)


def coadd_of(odd, place, mine, other, rows, cols, reach):
    edge = jax.ShapeDtypeStruct((reach, cols), bf16)
    smem = pl.BlockSpec(memory_space=pltpu.SMEM)
    vmem = pl.BlockSpec(memory_space=pltpu.VMEM)
    return pl.pallas_call(
        functools.partial(coadd_body, reach),
        in_specs=[smem, smem, vmem, vmem],
        out_specs=(vmem,) * 4,
        out_shape=(
            jax.ShapeDtypeStruct((rows, cols), f32),
            jax.ShapeDtypeStruct((rows, cols), bf16),
            edge,
            edge,
        ),
        scratch_shapes=[pltpu.VMEM((cols // lanes, rows, lanes), f32)],
        compiler_params=pltpu.CompilerParams(vmem_limit_bytes=8 * mib),
        name="coadd",
    )(odd, place, mine, other)


def detect_own_body(taps, psf, x, acc, profile, frame, lhs, w):
    reach = taps // 2
    rows, cols = x.shape
    spans = taps + 3
    mask = band_mask(112, taps)
    for row in (0, 24 + rows):
        frame[:, :, row : row + 24, :] = jnp.zeros((2, cols // lanes, 24, lanes), f32)
    put_frame(frame, columns(x[...]), 24, reach)
    put_lhs(lhs, frame, spans, 24 - reach)
    clear_band(w, taps, 112, 0, spans)
    for s in range(psf.shape[0]):
        total = 0.0
        for rows_at, cols_at in zip(row_places(profile.shape[1], taps), lane_places(taps)):
            moved = jnp.dot(rows_at.astype(bf16), psf[s], preferred_element_type=f32)
            total = total + jnp.dot(
                moved.astype(bf16), cols_at.astype(bf16), preferred_element_type=f32
            )
        profile[s] = total
        put_band(w, total, taps, mask, 0, spans, 256 * s)
        cut = slice(256 * s, 256 * s + 256)
        acc[:, cut] = jnp.dot(lhs[...], w[:, cut], preferred_element_type=f32)


def detect_own(psf, x):
    rows, cols = x.shape
    scales, _, taps = psf.shape
    spans = taps + 3
    return pl.pallas_call(
        functools.partial(detect_own_body, taps),
        out_shape=(
            jax.ShapeDtypeStruct((256, scales * 256), f32),
            jax.ShapeDtypeStruct((scales, 48, lanes), f32),
        ),
        scratch_shapes=[
            pltpu.VMEM((2, cols // lanes, 24 + rows + 24, lanes), f32),
            pltpu.VMEM((256, spans * lanes), bf16),
            pltpu.VMEM((spans * lanes, scales * 256), bf16),
        ],
        compiler_params=pltpu.CompilerParams(vmem_limit_bytes=20 * mib),
        cost_estimate=pl.CostEstimate(
            flops=scales * 2 * 256 * 256 * spans * lanes, bytes_accessed=4 * x.size, transcendentals=0
        ),
        name="detect_own",
    )(psf, x)


def detect_halo_body(taps, odd, profile, first, second, acc, out, frame, lhs, w, stage):
    scales, rows, cols = out.shape
    count = cols // lanes
    spans = edge_spans(taps)
    frame[...] = jnp.zeros_like(frame)
    clear_band(w.at[0], taps, 112, 0, spans)
    clear_band(w.at[1], taps, 112, taps + 3 - spans, taps + 3)
    mask = band_mask(112, taps)
    lane = lane_ids(16)
    lo, hi = halo_pair(odd[0] == 1, first[...], second[...])
    put_edges(taps, frame, lhs, lo, hi)
    for s in range(scales):
        at = 256 * s
        put_band(w.at[0], profile[s], taps, mask, 0, spans, at)
        put_band(w.at[1], profile[s], taps, mask, taps + 3 - spans, taps + 3, at)
        ends = [
            jnp.dot(lhs[side], w[side, :, at : at + 256], preferred_element_type=f32)
            for side in range(2)
        ]
        for m in range(count):
            for h in range(2):
                cut = slice(h * lanes, (h + 1) * lanes)
                blocks = []
                for n in (m, count + m):
                    more = jnp.concatenate([end[n * 8 : n * 8 + 8, cut] for end in ends], axis=0)
                    own = acc[n * 16 : n * 16 + 16, at + h * lanes : at + (h + 1) * lanes]
                    blocks.append(own + more)
                for b, part in enumerate(split_rows(*blocks, lane)):
                    stage[s, m, pl.ds(2 * h + b, 16, stride=group), :] = part
            out[s, :, m * lanes : (m + 1) * lanes] = stage[s, m]


def detect_halo(odd, profile, first, second, acc, rows, taps):
    cols = first.shape[1]
    scales = profile.shape[0]
    smem = pl.BlockSpec(memory_space=pltpu.SMEM)
    vmem = pl.BlockSpec(memory_space=pltpu.VMEM)
    return pl.pallas_call(
        functools.partial(detect_halo_body, taps),
        in_specs=[smem, vmem, vmem, vmem, vmem],
        out_specs=vmem,
        out_shape=jax.ShapeDtypeStruct((scales, rows, cols), f32),
        scratch_shapes=edge_scratch(taps, cols // lanes, scales * 256)
        + [pltpu.VMEM((scales, cols // lanes, rows, lanes), f32)],
        compiler_params=pltpu.CompilerParams(vmem_limit_bytes=20 * mib),
        name="detect_halo",
    )(odd, profile, first, second, acc)


def trade(first, second):
    count = lax.axis_size("section")
    out = []
    for start, rows in ((0, first), (1, second)):
        pairs = [(i, i + 1) for i in range(start, count - 1, 2)]
        out.append(lax.ppermute(rows, "section", pairs + [(b, a) for a, b in pairs]))
    return out


def on_device(
    exposures,
    coef_code,
    coef_table,
    basis_rows,
    basis_cols,
    exposure_weight,
    intersection_patch,
    intersection_shift,
    psf_kernels,
):
    number, rows, cols = exposures.shape
    taps = basis_rows.shape[1]
    reach = taps // 2
    wide = psf_kernels.shape[-1]
    wide_reach = wide // 2
    sky = ("sy", "sx", "core")
    size = lax.axis_size("sx")
    patches = size * size * 2
    core, at_x, at_y = (lax.axis_index(name) for name in ("core", "sx", "sy"))
    place = jnp.stack([core, jnp.where(core == 0, at_x, at_y), jnp.where(core == 0, at_y, at_x)])
    odd = lax.axis_index("section") % 2

    low, high = exposures[:, :reach, :], exposures[:, rows - reach :, :]
    first, second = trade(jnp.where(odd == 1, low, high), jnp.where(odd == 1, high, low))
    odd = odd[None]

    labels = jnp.concatenate(
        [exposure_weight[:, None], intersection_patch, intersection_shift], axis=1
    )
    swap = [(0, 1), (1, 0)]
    other_labels = lax.ppermute(labels, "core", swap)

    profile = profiles(coef_code, coef_table, basis_rows.T, basis_cols.T)
    table = slot_table(labels, other_labels, patches)
    table, profile = lax.optimization_barrier((table, profile))
    mine, send = match(odd, place, profile, exposures, first, second)
    other = lax.ppermute(send, "core", swap)

    steps = (2, 3, 1)
    move = lambda rows, step, by: lax.ppermute(rows, sky, role_pairs(step, size, by))
    (far,) = pile((2,), (bf16,), size, place, table, mine, other)
    came = [move(far, 0, 2)]
    far, table = lax.optimization_barrier((far, table))
    behind, ahead = pile((3, 1), (bf16, bf16), size, place, table, mine, other)
    came += [move(behind, 0, 3), move(ahead, 0, 1)]
    ahead, table = lax.optimization_barrier((ahead, table))
    (own,) = pile((0,), (f32,), size, place, table, mine, other)
    keep, *sends = fold(own, came)
    came = [move(sends[by - 1], 1, by) for by in steps]
    mine, send = meet(place, keep, came)
    other = lax.ppermute(send, "core", swap)
    coadd, rounded, first, second = coadd_of(odd, place, mine, other, rows, cols, wide_reach)
    first, second = trade(first, second)
    acc, profile = detect_own(psf_kernels, rounded)
    detect = detect_halo(odd, profile, first, second, acc, rows, wide)
    return (coadd[None], detect[None])


def solution(mesh):
    sections, sky = mesh.devices.shape
    grid = Mesh(mesh.devices.reshape(sections, 4, sky // 8, 2), ("section", "sy", "sx", "core"))
    sky = ("sy", "sx", "core")
    return jax.shard_map(
        on_device,
        mesh=grid,
        in_specs=(
            P(sky, "section", None),
            P(sky, None),
            P(),
            P(),
            P(),
            P(sky),
            P(sky, None),
            P(sky, None),
            P(),
        ),
        out_specs=(P(sky, "section", None), P(sky, None, "section", None)),
        check_vma=False,
    )
```

```python
import functools

import jax
import jax.numpy as jnp
from jax import lax
from jax.experimental import pallas as pl
from jax.experimental.pallas import tpu as pltpu
from jax.sharding import Mesh, PartitionSpec as P

f32 = jnp.float32
bf16 = jnp.bfloat16

lanes = 128
half = 64
group = 4
mib = 1024 * 1024


def one_hot(rows, cols, at):
    row = lax.broadcasted_iota(jnp.int32, (rows, cols), 0)
    col = lax.broadcasted_iota(jnp.int32, (rows, cols), 1)
    return (col == at(row)).astype(f32)


def lane_places(taps):
    first = one_hot(taps, lanes, lambda j: (lanes - j) % lanes)
    second = one_hot(taps, lanes, lambda j: half - j)
    return first, second


def row_places(rows, taps):
    return one_hot(rows, taps, lambda t: t), one_hot(rows, taps, lambda t: t - 1)


def lane_ids(rows):
    return lax.broadcasted_iota(jnp.int32, (rows, lanes), 1)


def band_mask(depth, taps):
    k = lax.broadcasted_iota(jnp.int32, (depth, lanes), 0)
    gap = k - lane_ids(depth) % half
    return (gap >= 0) & (gap < taps)


def band_tile(row, mask):
    depth = mask.shape[0]
    wide = jnp.broadcast_to(row, (depth, lanes))
    turned = pltpu.roll(wide, 0, 1, stride=1, stride_axis=0)
    return jnp.where(mask, turned, 0.0).astype(bf16)


def put_frame(frame, tiles, row, reach):
    count = len(tiles)
    rows = tiles[0].shape[0]
    lane = lane_ids(rows)
    zero = jnp.zeros((rows, lanes), f32)
    right = [pltpu.roll(t, reach, 1).astype(f32) for t in tiles]
    left = [pltpu.roll(t, half + reach, 1).astype(f32) for t in tiles]
    for m in range(count):
        before = right[m - 1] if m else zero
        frame[0, m, row : row + rows, :] = jnp.where(lane < reach, before, right[m])
        after = left[m + 1] if m + 1 < count else zero
        frame[1, m, row : row + rows, :] = jnp.where(lane < half + reach, left[m], after)


def put_lhs(lhs, frame, spans, row):
    tiles = frame.shape[1]
    for t in range(spans):
        for par in range(2):
            for m in range(tiles):
                at = (par * tiles + m) * 16
                piece = frame[par, m, pl.ds(row + t, 16, stride=group), :]
                lhs[at : at + 16, t * lanes : (t + 1) * lanes] = piece.astype(bf16)


def split_rows(even, odd, lane):
    first = jnp.where(lane < half, even, pltpu.roll(odd, half, 1))
    second = jnp.where(lane < half, pltpu.roll(even, half, 1), odd)
    return first, second


def columns(rows):
    return [rows[:, m * lanes : (m + 1) * lanes] for m in range(rows.shape[1] // lanes)]


def put_band(w, profile, taps, mask, first, last, at):
    depth = mask.shape[0]
    for u in range(max(first - 2, 0), min(last, taps + 1)):
        tile = band_tile(profile[u : u + 1, :], mask)
        if u >= first:
            row = (u - first) * lanes
            w[row : row + depth, at : at + lanes] = tile
        if first <= u + 2 < last:
            row = (u + 2 - first) * lanes
            w[row : row + depth, at + lanes : at + 2 * lanes] = tile


def clear_band(w, taps, depth, first, last):
    width = w.shape[1]
    for t in range(first, last):
        row = (t - first) * lanes
        w[row + depth : row + lanes, :] = jnp.zeros((lanes - depth, width), bf16)
        for u, at in ((t, 0), (t - 2, lanes)):
            if not 0 <= u <= taps:
                for n in range(at, width, 2 * lanes):
                    w[row : row + depth, n : n + lanes] = jnp.zeros((depth, lanes), bf16)


def edge_spans(taps):
    return (taps // 2 + 1) // 2 * 2


def put_edge_lhs(lhs, frame, spans):
    tiles = frame.shape[1]
    for t in range(spans):
        for par in range(2):
            for m in range(0, tiles, 2):
                pair = [frame[par, m + i, pl.ds(t, 8, stride=group), :] for i in range(2)]
                at = (par * tiles + m) * 8
                lhs[at : at + 16, t * lanes : (t + 1) * lanes] = jnp.concatenate(pair, axis=0).astype(bf16)


def edge_scratch(taps, tiles, width):
    spans = edge_spans(taps)
    return [
        pltpu.VMEM((2, 2, tiles, 48, lanes), f32),
        pltpu.VMEM((2, 128, spans * lanes), bf16),
        pltpu.VMEM((2, spans * lanes, width), bf16),
    ]


def put_edges(taps, frame, lhs, lo, hi):
    reach = taps // 2
    spans = edge_spans(taps)
    put_frame(frame.at[0], columns(lo), 0, reach)
    put_frame(frame.at[1], columns(hi), 28 - reach + spans, reach)
    for side in range(2):
        put_edge_lhs(lhs.at[side], frame.at[side], spans)


def halo_pair(odd, first, second):
    return jnp.where(odd, first, second), jnp.where(odd, second, first)


ways = 8


def profile_body(code, table, base_rows, base_cols, out, g):
    number, spans, _ = out.shape
    taps = base_rows.shape[0]
    exact = lax.Precision.HIGHEST
    rows_ab = [
        jnp.dot(places, base_rows[...], precision=exact, preferred_element_type=f32)
        for places in row_places(spans, taps)
    ]
    cols_ab = [
        lax.dot_general(
            base_cols[...], places, (((0,), (0,)), ((), ())), precision=exact, preferred_element_type=f32
        )
        for places in lane_places(taps)
    ]
    for b in range(g.shape[0]):
        g[b] = sum(r[:, b : b + 1] * c[b : b + 1, :] for r, c in zip(rows_ab, cols_ab))

    def one(e, _):
        total = jnp.zeros((spans, lanes), f32)
        for b in range(g.shape[0]):
            total = total + table[b, code[e, b]] * g[b]
        out[e] = total.astype(bf16).astype(f32)
        return 0

    lax.fori_loop(0, number, one, 0)


def profiles(code, table, base_rows, base_cols):
    number, basis = code.shape
    taps = base_rows.shape[0]
    smem = pl.BlockSpec(memory_space=pltpu.SMEM)
    vmem = pl.BlockSpec(memory_space=pltpu.VMEM)
    return pl.pallas_call(
        profile_body,
        in_specs=[smem, smem, vmem, vmem],
        out_specs=vmem,
        out_shape=jax.ShapeDtypeStruct((number, taps + 1, lanes), f32),
        scratch_shapes=[pltpu.VMEM((basis, taps + 1, lanes), f32)],
        compiler_params=pltpu.CompilerParams(vmem_limit_bytes=4 * mib),
        name="profiles",
    )(code, table, base_rows, base_cols)


def match_body(taps, odd, place, profile, x, first, second, keep, send, frame, lhs, w):
    number, _, cols = x.shape
    reach = taps // 2
    spans = taps + 3
    count = cols // lanes
    depth = 96
    mask = band_mask(depth, taps)
    lane = lane_ids(16)
    for way in range(ways):
        clear_band(w.at[way], taps, depth, 0, spans)

    def one(e, way):
        put_band(w.at[way], profile[e], taps, mask, 0, spans, 0)
        lo, hi = halo_pair(odd[0] == 1, first[e], second[e])
        for piece, row in ((lo, 16 - reach), (x[e], 16), (hi, 80)):
            put_frame(frame.at[way], columns(piece), row, reach)
        put_lhs(lhs.at[way], frame.at[way], spans, 16 - reach)
        acc = jnp.dot(lhs[way], w[way], preferred_element_type=f32)
        for h in range(2):
            cut = slice(h * lanes, (h + 1) * lanes)
            parts = []
            for m in range(count):
                blocks = [acc[n * 16 : n * 16 + 16, cut] for n in (m, count + m)]
                parts.append([part.astype(bf16) for part in split_rows(*blocks, lane)])
            for b in range(2):
                rows = slice((2 * h + b) * 16, (2 * h + b) * 16 + 16)
                tiles = [part[b] for part in parts]
                low = [jnp.zeros((16, lanes), bf16)] + tiles[: count // 2]
                high = tiles[count // 2 - 1 :]
                for k in range(count // 2 + 1):
                    at = slice(k * lanes, (k + 1) * lanes)
                    keep[e, rows, at] = jnp.where(place[0] == 0, low[k], high[k])
                    send[e, rows, at] = jnp.where(place[0] == 0, high[k], low[k])

    def some(i, _):
        for way in range(ways):
            one(ways * i + way, way)
        return 0

    lax.fori_loop(0, number // ways, some, 0)


def match(odd, place, profile, x, first, second):
    number, rows, cols = x.shape
    taps = profile.shape[1] - 1
    smem = pl.BlockSpec(memory_space=pltpu.SMEM)
    vmem = pl.BlockSpec(memory_space=pltpu.VMEM)
    spans = taps + 3
    return pl.pallas_call(
        functools.partial(match_body, taps),
        in_specs=[smem, smem] + [vmem] * 4,
        out_specs=(vmem, vmem),
        out_shape=(jax.ShapeDtypeStruct((number, rows, cols // 2 + lanes), bf16),) * 2,
        scratch_shapes=[
            pltpu.VMEM((ways, 2, cols // lanes, 96, lanes), f32),
            pltpu.VMEM((ways, 256, spans * lanes), bf16),
            pltpu.VMEM((ways, spans * lanes, 256), bf16),
        ],
        compiler_params=pltpu.CompilerParams(vmem_limit_bytes=40 * mib),
        cost_estimate=pl.CostEstimate(
            flops=number * 2 * 256 * 256 * spans * lanes, bytes_accessed=4 * x.size, transcendentals=0
        ),
        name="match",
    )(odd, place, profile, x, first, second)


slots = 8


def slot_body(mine, other, out):
    number = mine.shape[0]
    per = (mine.shape[1] - 1) // 2
    patches = out.shape[0] // (slots + 1)

    def clear(p, _):
        out[p] = 0
        for s in range(slots):
            out[patches + p * slots + s] = 0
        return 0

    lax.fori_loop(0, patches, clear, 0)
    for base, labels in ((0, mine), (number, other)):

        def one(e, _):
            plane = (labels[e, 0] * 2 * number + base + e) * 256
            for k in range(per):
                p = labels[e, 1 + k]
                at = out[p]
                out[patches + p * slots + at] = plane + labels[e, 1 + per + k]
                out[p] = at + 1
            return 0

        lax.fori_loop(0, number, one, 0)


def slot_table(mine, other, patches):
    smem = pl.BlockSpec(memory_space=pltpu.SMEM)
    return pl.pallas_call(
        slot_body,
        in_specs=[smem, smem],
        out_specs=smem,
        out_shape=jax.ShapeDtypeStruct((patches * (slots + 1),), jnp.int32),
        compiler_params=pltpu.CompilerParams(vmem_limit_bytes=mib),
        name="slot_table",
    )(mine, other)


def role_pairs(step, size, shift):
    index = lambda y, x, core: ((y % size) * size + x % size) * 2 + core
    pairs = []
    for y in range(size):
        for x in range(size):
            for core in range(2):
                to = (y, x + shift) if core == step else (y + shift, x)
                pairs.append((index(y, x, core), index(*to, core)))
    return pairs


def pile_body(chunks, size, place, table, mine, other, *rest):
    outs, planes = rest[:-1], rest[-1]
    number, rows, cols = mine.shape
    tiles = cols // lanes - 1
    patches = table.shape[0] // (slots + 1)
    core = place[0]
    planes[0:number] = mine[...]
    planes[number:] = other[...]
    lane = lane_ids(16)
    tail = lax.broadcasted_iota(jnp.int32, (16, lanes), 0)

    for chunk, out in zip(chunks, outs):

        def patch(i, _):
            u = (place[1] + chunk) % size
            v = (place[2] + i) % size
            p = jnp.where(core == 0, v * size + u, u * size + v) * 2

            def some(used):
                entries = []
                for c in range(2):
                    words = [table[patches + (p + c) * slots + s] for s in range(used)]
                    entries.append(
                        [
                            ((word >> 8) & (2 * number - 1), word & 255, (word >> 12).astype(f32))
                            for word in words
                        ]
                    )
                for r in range(rows // 16):
                    for c in range(2):
                        total = [jnp.zeros((16, lanes), f32)] * tiles
                        for e, o, weight in entries[c]:
                            early = lane < o
                            before = None
                            for k in range(tiles + 1):
                                piece = planes[e, r * 16 : r * 16 + 16, k * lanes : (k + 1) * lanes]
                                turned = pltpu.roll(piece, o, 1).astype(f32)
                                if k:
                                    part = jnp.where(early, before, turned)
                                    total[k - 1] = total[k - 1] + weight * part
                                before = turned
                        for k in range(tiles):
                            at = k * rows + r * 16
                            out[2 * i + c, at : at + 16, :] = total[k].astype(out.dtype)
                for c in range(2):
                    cover = jnp.zeros((16, lanes), f32)
                    whole = jnp.zeros((16, lanes), f32)
                    for e, o, weight in entries[c]:
                        cover = cover + jnp.where(lane < o, 0.0, weight)
                        whole = whole + weight
                    last = jnp.where(tail == 0, cover, whole)
                    out[2 * i + c, tiles * rows :, :] = last.astype(out.dtype)

            used = jnp.maximum(table[p], table[p + 1])
            for top in range(2, slots + 1, 2):
                low = top - 2 if top > 2 else -1

                @pl.when((used > low) & (used <= top))
                def _():
                    some(top)

            return 0

        lax.fori_loop(0, size, patch, 0)


def pile(chunks, kinds, size, place, table, mine, other):
    number, rows, cols = mine.shape
    smem = pl.BlockSpec(memory_space=pltpu.SMEM)
    vmem = pl.BlockSpec(memory_space=pltpu.VMEM)
    shape = (2 * size, (cols // lanes - 1) * rows + 16, lanes)
    return pl.pallas_call(
        functools.partial(pile_body, chunks, size),
        in_specs=[smem, smem, vmem, vmem],
        out_specs=[vmem] * len(chunks),
        out_shape=[jax.ShapeDtypeStruct(shape, kind) for kind in kinds],
        scratch_shapes=[pltpu.VMEM((2 * number, rows, cols), bf16)],
        compiler_params=pltpu.CompilerParams(vmem_limit_bytes=8 * mib),
        cost_estimate=pl.CostEstimate(
            flops=len(chunks) * 1000000000, bytes_accessed=4 * mine.size, transcendentals=0
        ),
        name="pile_" + "_".join(str(chunk) for chunk in chunks),
    )(place, table, mine, other)


def fold_body(own, *rest):
    came, keep, sends = rest[: len(rest) // 2], rest[len(rest) // 2], rest[len(rest) // 2 + 1 :]
    rows = own.shape[1]
    for i in range(own.shape[0]):
        for at in range(0, rows, 16):
            total = own[i, at : at + 16, :]
            for ref in came:
                total = total + ref[i, at : at + 16, :].astype(f32)
            if i < 2:
                keep[i, at : at + 16, :] = total
            else:
                sends[i // 2 - 1][i % 2, at : at + 16, :] = total.astype(bf16)


def fold(own, came):
    vmem = pl.BlockSpec(memory_space=pltpu.VMEM)
    shape = (2,) + own.shape[1:]
    return pl.pallas_call(
        fold_body,
        in_specs=[vmem] * (1 + len(came)),
        out_specs=[vmem] * (1 + len(came)),
        out_shape=[jax.ShapeDtypeStruct(shape, f32)] + [jax.ShapeDtypeStruct(shape, bf16)] * len(came),
        compiler_params=pltpu.CompilerParams(vmem_limit_bytes=4 * mib),
        name="fold",
    )(own, *came)


def meet_body(place, own, *rest):
    came, mine, send = rest[:-2], rest[-2], rest[-1]
    core = place[0]
    for at in range(0, own.shape[1], 16):
        for out, i in ((mine, core), (send, 1 - core)):
            total = own[i, at : at + 16, :]
            for ref in came:
                total = total + ref[i, at : at + 16, :].astype(f32)
            out[at : at + 16, :] = total


def meet(place, own, came):
    smem = pl.BlockSpec(memory_space=pltpu.SMEM)
    vmem = pl.BlockSpec(memory_space=pltpu.VMEM)
    return pl.pallas_call(
        meet_body,
        in_specs=[smem] + [vmem] * (1 + len(came)),
        out_specs=[vmem] * 2,
        out_shape=[jax.ShapeDtypeStruct(own.shape[1:], f32)] * 2,
        compiler_params=pltpu.CompilerParams(vmem_limit_bytes=4 * mib),
        name="meet",
    )(place, own, *came)


def coadd_body(reach, odd, place, mine, other, coadd, rounded, first, second, stage):
    rows, cols = coadd.shape
    tiles = cols // lanes
    near = place[0] == 0

    def pick(low, at):
        a, b = mine[at : at + 16, :], other[at : at + 16, :]
        return jnp.where(near, a, b) if low else jnp.where(near, b, a)

    cover = pick(True, tiles // 2 * rows)
    scales = [1.0 / jnp.maximum(cover[r : r + 1, :], 1.0) for r in (0, 1)]
    for m in range(tiles):
        for b in range(group):
            at = m % (tiles // 2) * rows + b * 16
            stage[m, pl.ds(b, 16, stride=group), :] = pick(m < tiles // 2, at) * scales[min(m, 1)]
        cut = slice(m * lanes, (m + 1) * lanes)
        coadd[:, cut] = stage[m]
        rounded[:, cut] = stage[m].astype(bf16)
        low = stage[m, 0:reach, :]
        high = stage[m, rows - reach : rows, :]
        first[:, cut] = jnp.where(odd[0] == 1, low, high).astype(bf16)
        second[:, cut] = jnp.where(odd[0] == 1, high, low).astype(bf16)


def coadd_of(odd, place, mine, other, rows, cols, reach):
    edge = jax.ShapeDtypeStruct((reach, cols), bf16)
    smem = pl.BlockSpec(memory_space=pltpu.SMEM)
    vmem = pl.BlockSpec(memory_space=pltpu.VMEM)
    return pl.pallas_call(
        functools.partial(coadd_body, reach),
        in_specs=[smem, smem, vmem, vmem],
        out_specs=(vmem,) * 4,
        out_shape=(
            jax.ShapeDtypeStruct((rows, cols), f32),
            jax.ShapeDtypeStruct((rows, cols), bf16),
            edge,
            edge,
        ),
        scratch_shapes=[pltpu.VMEM((cols // lanes, rows, lanes), f32)],
        compiler_params=pltpu.CompilerParams(vmem_limit_bytes=8 * mib),
        name="coadd",
    )(odd, place, mine, other)


def detect_own_body(taps, psf, x, acc, profile, frame, lhs, w):
    reach = taps // 2
    rows, cols = x.shape
    spans = taps + 3
    mask = band_mask(112, taps)
    for row in (0, 24 + rows):
        frame[:, :, row : row + 24, :] = jnp.zeros((2, cols // lanes, 24, lanes), f32)
    put_frame(frame, columns(x[...]), 24, reach)
    put_lhs(lhs, frame, spans, 24 - reach)
    clear_band(w, taps, 112, 0, spans)
    for s in range(psf.shape[0]):
        total = 0.0
        for rows_at, cols_at in zip(row_places(profile.shape[1], taps), lane_places(taps)):
            moved = jnp.dot(rows_at.astype(bf16), psf[s], preferred_element_type=f32)
            total = total + jnp.dot(
                moved.astype(bf16), cols_at.astype(bf16), preferred_element_type=f32
            )
        profile[s] = total
        put_band(w, total, taps, mask, 0, spans, 256 * s)
        cut = slice(256 * s, 256 * s + 256)
        acc[:, cut] = jnp.dot(lhs[...], w[:, cut], preferred_element_type=f32)


def detect_own(psf, x):
    rows, cols = x.shape
    scales, _, taps = psf.shape
    spans = taps + 3
    return pl.pallas_call(
        functools.partial(detect_own_body, taps),
        out_shape=(
            jax.ShapeDtypeStruct((256, scales * 256), f32),
            jax.ShapeDtypeStruct((scales, 48, lanes), f32),
        ),
        scratch_shapes=[
            pltpu.VMEM((2, cols // lanes, 24 + rows + 24, lanes), f32),
            pltpu.VMEM((256, spans * lanes), bf16),
            pltpu.VMEM((spans * lanes, scales * 256), bf16),
        ],
        compiler_params=pltpu.CompilerParams(vmem_limit_bytes=20 * mib),
        cost_estimate=pl.CostEstimate(
            flops=scales * 2 * 256 * 256 * spans * lanes, bytes_accessed=4 * x.size, transcendentals=0
        ),
        name="detect_own",
    )(psf, x)


def detect_halo_body(
    taps, odd, profile, first, second, acc, coadd, out, again, frame, lhs, w, stage, ready, leave
):
    scales, rows, cols = out.shape
    go = [pltpu.make_async_copy(ready.at[s], out.at[s], leave.at[s]) for s in range(scales)]
    go.append(pltpu.make_async_copy(coadd, again, leave.at[scales]))
    go[scales].start()
    count = cols // lanes
    spans = edge_spans(taps)
    frame[...] = jnp.zeros_like(frame)
    clear_band(w.at[0], taps, 112, 0, spans)
    clear_band(w.at[1], taps, 112, taps + 3 - spans, taps + 3)
    mask = band_mask(112, taps)
    lane = lane_ids(16)
    lo, hi = halo_pair(odd[0] == 1, first[...], second[...])
    put_edges(taps, frame, lhs, lo, hi)
    for s in range(scales):
        at = 256 * s
        put_band(w.at[0], profile[s], taps, mask, 0, spans, at)
        put_band(w.at[1], profile[s], taps, mask, taps + 3 - spans, taps + 3, at)
        ends = [
            jnp.dot(lhs[side], w[side, :, at : at + 256], preferred_element_type=f32)
            for side in range(2)
        ]
        for m in range(count):
            for h in range(2):
                cut = slice(h * lanes, (h + 1) * lanes)
                blocks = []
                for n in (m, count + m):
                    more = jnp.concatenate([end[n * 8 : n * 8 + 8, cut] for end in ends], axis=0)
                    own = acc[n * 16 : n * 16 + 16, at + h * lanes : at + (h + 1) * lanes]
                    blocks.append(own + more)
                for b, part in enumerate(split_rows(*blocks, lane)):
                    stage[s, m, pl.ds(2 * h + b, 16, stride=group), :] = part
            ready[s, :, m * lanes : (m + 1) * lanes] = stage[s, m]
        go[s].start()
    for copy in go:
        copy.wait()


def detect_halo(odd, profile, first, second, acc, coadd, rows, taps):
    cols = first.shape[1]
    scales = profile.shape[0]
    smem = pl.BlockSpec(memory_space=pltpu.SMEM)
    vmem = pl.BlockSpec(memory_space=pltpu.VMEM)
    return pl.pallas_call(
        functools.partial(detect_halo_body, taps),
        in_specs=[smem] + [vmem] * 5,
        out_specs=(pl.BlockSpec(memory_space=pl.ANY),) * 2,
        out_shape=(
            jax.ShapeDtypeStruct((scales, rows, cols), f32),
            jax.ShapeDtypeStruct((rows, cols), f32),
        ),
        scratch_shapes=edge_scratch(taps, cols // lanes, scales * 256)
        + [
            pltpu.VMEM((scales, cols // lanes, rows, lanes), f32),
            pltpu.VMEM((scales, rows, cols), f32),
            pltpu.SemaphoreType.DMA((scales + 1,)),
        ],
        compiler_params=pltpu.CompilerParams(vmem_limit_bytes=20 * mib),
        name="detect_halo",
    )(odd, profile, first, second, acc, coadd)


def trade(first, second):
    count = lax.axis_size("section")
    out = []
    for start, rows in ((0, first), (1, second)):
        pairs = [(i, i + 1) for i in range(start, count - 1, 2)]
        out.append(lax.ppermute(rows, "section", pairs + [(b, a) for a, b in pairs]))
    return out


def on_device(
    exposures,
    coef_code,
    coef_table,
    basis_rows,
    basis_cols,
    exposure_weight,
    intersection_patch,
    intersection_shift,
    psf_kernels,
):
    number, rows, cols = exposures.shape
    taps = basis_rows.shape[1]
    reach = taps // 2
    wide = psf_kernels.shape[-1]
    wide_reach = wide // 2
    sky = ("sy", "sx", "core")
    size = lax.axis_size("sx")
    patches = size * size * 2
    core, at_x, at_y = (lax.axis_index(name) for name in ("core", "sx", "sy"))
    place = jnp.stack([core, jnp.where(core == 0, at_x, at_y), jnp.where(core == 0, at_y, at_x)])
    odd = lax.axis_index("section") % 2

    low, high = exposures[:, :reach, :], exposures[:, rows - reach :, :]
    first, second = trade(jnp.where(odd == 1, low, high), jnp.where(odd == 1, high, low))
    odd = odd[None]

    labels = jnp.concatenate(
        [exposure_weight[:, None], intersection_patch, intersection_shift], axis=1
    )
    swap = [(0, 1), (1, 0)]
    other_labels = lax.ppermute(labels, "core", swap)

    profile = profiles(coef_code, coef_table, basis_rows.T, basis_cols.T)
    table = slot_table(labels, other_labels, patches)
    table, profile = lax.optimization_barrier((table, profile))
    mine, send = match(odd, place, profile, exposures, first, second)
    other = lax.ppermute(send, "core", swap)

    steps = (2, 3, 1)
    move = lambda rows, step, by: lax.ppermute(rows, sky, role_pairs(step, size, by))
    (far,) = pile((2,), (bf16,), size, place, table, mine, other)
    came = [move(far, 0, 2)]
    far, table = lax.optimization_barrier((far, table))
    behind, ahead = pile((3, 1), (bf16, bf16), size, place, table, mine, other)
    came += [move(behind, 0, 3), move(ahead, 0, 1)]
    ahead, table = lax.optimization_barrier((ahead, table))
    (own,) = pile((0,), (f32,), size, place, table, mine, other)
    keep, *sends = fold(own, came)
    came = [move(sends[by - 1], 1, by) for by in steps]
    mine, send = meet(place, keep, came)
    other = lax.ppermute(send, "core", swap)
    coadd, rounded, first, second = coadd_of(odd, place, mine, other, rows, cols, wide_reach)
    first, second = trade(first, second)
    acc, profile = detect_own(psf_kernels, rounded)
    detect, coadd = detect_halo(odd, profile, first, second, acc, coadd, rows, wide)
    return (coadd[None], detect[None])


def solution(mesh):
    sections, sky = mesh.devices.shape
    grid = Mesh(mesh.devices.reshape(sections, 4, sky // 8, 2), ("section", "sy", "sx", "core"))
    sky = ("sy", "sx", "core")
    return jax.shard_map(
        on_device,
        mesh=grid,
        in_specs=(
            P(sky, "section", None),
            P(sky, None),
            P(),
            P(),
            P(),
            P(sky),
            P(sky, None),
            P(sky, None),
            P(),
        ),
        out_specs=(P(sky, "section", None), P(sky, None, "section", None)),
        check_vma=False,
    )
```

```python
import functools

import jax
import jax.numpy as jnp
from jax import lax
from jax.experimental import pallas as pl
from jax.experimental.pallas import tpu as pltpu
from jax.sharding import Mesh, PartitionSpec as P

f32 = jnp.float32
bf16 = jnp.bfloat16

lanes = 128
half = 64
group = 4
mib = 1024 * 1024


def one_hot(rows, cols, at):
    row = lax.broadcasted_iota(jnp.int32, (rows, cols), 0)
    col = lax.broadcasted_iota(jnp.int32, (rows, cols), 1)
    return (col == at(row)).astype(f32)


def lane_places(taps):
    first = one_hot(taps, lanes, lambda j: (lanes - j) % lanes)
    second = one_hot(taps, lanes, lambda j: half - j)
    return first, second


def row_places(rows, taps):
    return one_hot(rows, taps, lambda t: t), one_hot(rows, taps, lambda t: t - 1)


def lane_ids(rows):
    return lax.broadcasted_iota(jnp.int32, (rows, lanes), 1)


def band_mask(depth, taps):
    k = lax.broadcasted_iota(jnp.int32, (depth, lanes), 0)
    gap = k - lane_ids(depth) % half
    return (gap >= 0) & (gap < taps)


def band_tile(row, mask):
    depth = mask.shape[0]
    wide = jnp.broadcast_to(row, (depth, lanes))
    turned = pltpu.roll(wide, 0, 1, stride=1, stride_axis=0)
    return jnp.where(mask, turned, 0.0).astype(bf16)


def put_frame(frame, tiles, row, reach):
    count = len(tiles)
    rows = tiles[0].shape[0]
    lane = lane_ids(rows)
    zero = jnp.zeros((rows, lanes), f32)
    right = [pltpu.roll(t, reach, 1).astype(f32) for t in tiles]
    left = [pltpu.roll(t, half + reach, 1).astype(f32) for t in tiles]
    for m in range(count):
        before = right[m - 1] if m else zero
        frame[0, m, row : row + rows, :] = jnp.where(lane < reach, before, right[m])
        after = left[m + 1] if m + 1 < count else zero
        frame[1, m, row : row + rows, :] = jnp.where(lane < half + reach, left[m], after)


def put_lhs(lhs, frame, spans, row):
    tiles = frame.shape[1]
    for t in range(spans):
        for par in range(2):
            for m in range(tiles):
                at = (par * tiles + m) * 16
                piece = frame[par, m, pl.ds(row + t, 16, stride=group), :]
                lhs[at : at + 16, t * lanes : (t + 1) * lanes] = piece.astype(bf16)


def split_rows(even, odd, lane):
    first = jnp.where(lane < half, even, pltpu.roll(odd, half, 1))
    second = jnp.where(lane < half, pltpu.roll(even, half, 1), odd)
    return first, second


def columns(rows):
    return [rows[:, m * lanes : (m + 1) * lanes] for m in range(rows.shape[1] // lanes)]


def put_band(w, profile, taps, mask, first, last, at):
    depth = mask.shape[0]
    for u in range(max(first - 2, 0), min(last, taps + 1)):
        tile = band_tile(profile[u : u + 1, :], mask)
        if u >= first:
            row = (u - first) * lanes
            w[row : row + depth, at : at + lanes] = tile
        if first <= u + 2 < last:
            row = (u + 2 - first) * lanes
            w[row : row + depth, at + lanes : at + 2 * lanes] = tile


def clear_band(w, taps, depth, first, last):
    width = w.shape[1]
    for t in range(first, last):
        row = (t - first) * lanes
        w[row + depth : row + lanes, :] = jnp.zeros((lanes - depth, width), bf16)
        for u, at in ((t, 0), (t - 2, lanes)):
            if not 0 <= u <= taps:
                for n in range(at, width, 2 * lanes):
                    w[row : row + depth, n : n + lanes] = jnp.zeros((depth, lanes), bf16)


def edge_spans(taps):
    return (taps // 2 + 1) // 2 * 2


def put_edge_lhs(lhs, frame, spans):
    tiles = frame.shape[1]
    for t in range(spans):
        for par in range(2):
            for m in range(0, tiles, 2):
                pair = [frame[par, m + i, pl.ds(t, 8, stride=group), :] for i in range(2)]
                at = (par * tiles + m) * 8
                lhs[at : at + 16, t * lanes : (t + 1) * lanes] = jnp.concatenate(pair, axis=0).astype(bf16)


def edge_scratch(taps, tiles, width):
    spans = edge_spans(taps)
    return [
        pltpu.VMEM((2, 2, tiles, 48, lanes), f32),
        pltpu.VMEM((2, 128, spans * lanes), bf16),
        pltpu.VMEM((2, spans * lanes, width), bf16),
    ]


def put_edges(taps, frame, lhs, lo, hi):
    reach = taps // 2
    spans = edge_spans(taps)
    put_frame(frame.at[0], columns(lo), 0, reach)
    put_frame(frame.at[1], columns(hi), 28 - reach + spans, reach)
    for side in range(2):
        put_edge_lhs(lhs.at[side], frame.at[side], spans)


def halo_pair(odd, first, second):
    return jnp.where(odd, first, second), jnp.where(odd, second, first)


ways = 8


def profile_body(code, table, base_rows, base_cols, out, g):
    number, spans, _ = out.shape
    taps = base_rows.shape[0]
    exact = lax.Precision.HIGHEST
    rows_ab = [
        jnp.dot(places, base_rows[...], precision=exact, preferred_element_type=f32)
        for places in row_places(spans, taps)
    ]
    cols_ab = [
        lax.dot_general(
            base_cols[...], places, (((0,), (0,)), ((), ())), precision=exact, preferred_element_type=f32
        )
        for places in lane_places(taps)
    ]
    for b in range(g.shape[0]):
        g[b] = sum(r[:, b : b + 1] * c[b : b + 1, :] for r, c in zip(rows_ab, cols_ab))

    def one(e, _):
        total = jnp.zeros((spans, lanes), f32)
        for b in range(g.shape[0]):
            total = total + table[b, code[e, b]] * g[b]
        out[e] = total.astype(bf16).astype(f32)
        return 0

    lax.fori_loop(0, number, one, 0)


def profiles(code, table, base_rows, base_cols):
    number, basis = code.shape
    taps = base_rows.shape[0]
    smem = pl.BlockSpec(memory_space=pltpu.SMEM)
    vmem = pl.BlockSpec(memory_space=pltpu.VMEM)
    return pl.pallas_call(
        profile_body,
        in_specs=[smem, smem, vmem, vmem],
        out_specs=vmem,
        out_shape=jax.ShapeDtypeStruct((number, taps + 1, lanes), f32),
        scratch_shapes=[pltpu.VMEM((basis, taps + 1, lanes), f32)],
        compiler_params=pltpu.CompilerParams(vmem_limit_bytes=4 * mib),
        name="profiles",
    )(code, table, base_rows, base_cols)


def match_body(taps, odd, place, profile, x, first, second, keep, send, frame, lhs, w):
    number, _, cols = x.shape
    reach = taps // 2
    spans = taps + 3
    count = cols // lanes
    depth = 96
    mask = band_mask(depth, taps)
    lane = lane_ids(16)
    for way in range(ways):
        clear_band(w.at[way], taps, depth, 0, spans)

    def one(e, way):
        put_band(w.at[way], profile[e], taps, mask, 0, spans, 0)
        lo, hi = halo_pair(odd[0] == 1, first[e], second[e])
        for piece, row in ((lo, 16 - reach), (x[e], 16), (hi, 80)):
            put_frame(frame.at[way], columns(piece), row, reach)
        put_lhs(lhs.at[way], frame.at[way], spans, 16 - reach)
        acc = jnp.dot(lhs[way], w[way], preferred_element_type=f32)
        for h in range(2):
            cut = slice(h * lanes, (h + 1) * lanes)
            parts = []
            for m in range(count):
                blocks = [acc[n * 16 : n * 16 + 16, cut] for n in (m, count + m)]
                parts.append([part.astype(bf16) for part in split_rows(*blocks, lane)])
            for b in range(2):
                rows = slice((2 * h + b) * 16, (2 * h + b) * 16 + 16)
                tiles = [part[b] for part in parts]
                low = [jnp.zeros((16, lanes), bf16)] + tiles[: count // 2]
                high = tiles[count // 2 - 1 :]
                for k in range(count // 2 + 1):
                    at = slice(k * lanes, (k + 1) * lanes)
                    keep[e, rows, at] = jnp.where(place[0] == 0, low[k], high[k])
                    send[e, rows, at] = jnp.where(place[0] == 0, high[k], low[k])

    def some(i, _):
        for way in range(ways):
            one(ways * i + way, way)
        return 0

    lax.fori_loop(0, number // ways, some, 0)


def match(odd, place, profile, x, first, second):
    number, rows, cols = x.shape
    taps = profile.shape[1] - 1
    smem = pl.BlockSpec(memory_space=pltpu.SMEM)
    vmem = pl.BlockSpec(memory_space=pltpu.VMEM)
    spans = taps + 3
    return pl.pallas_call(
        functools.partial(match_body, taps),
        in_specs=[smem, smem] + [vmem] * 4,
        out_specs=(vmem, vmem),
        out_shape=(jax.ShapeDtypeStruct((number, rows, cols // 2 + lanes), bf16),) * 2,
        scratch_shapes=[
            pltpu.VMEM((ways, 2, cols // lanes, 96, lanes), f32),
            pltpu.VMEM((ways, 256, spans * lanes), bf16),
            pltpu.VMEM((ways, spans * lanes, 256), bf16),
        ],
        compiler_params=pltpu.CompilerParams(vmem_limit_bytes=40 * mib),
        cost_estimate=pl.CostEstimate(
            flops=number * 2 * 256 * 256 * spans * lanes, bytes_accessed=4 * x.size, transcendentals=0
        ),
        name="match",
    )(odd, place, profile, x, first, second)


slots = 8


def slot_body(mine, other, out):
    number = mine.shape[0]
    per = (mine.shape[1] - 1) // 2
    patches = out.shape[0] // (slots + 1)

    def clear(p, _):
        out[p] = 0
        for s in range(slots):
            out[patches + p * slots + s] = 0
        return 0

    lax.fori_loop(0, patches, clear, 0)
    for base, labels in ((0, mine), (number, other)):

        def one(e, _):
            plane = (labels[e, 0] * 2 * number + base + e) * 256
            for k in range(per):
                p = labels[e, 1 + k]
                at = out[p]
                out[patches + p * slots + at] = plane + labels[e, 1 + per + k]
                out[p] = at + 1
            return 0

        lax.fori_loop(0, number, one, 0)


def slot_table(mine, other, patches):
    smem = pl.BlockSpec(memory_space=pltpu.SMEM)
    return pl.pallas_call(
        slot_body,
        in_specs=[smem, smem],
        out_specs=smem,
        out_shape=jax.ShapeDtypeStruct((patches * (slots + 1),), jnp.int32),
        compiler_params=pltpu.CompilerParams(vmem_limit_bytes=mib),
        name="slot_table",
    )(mine, other)


def role_pairs(step, size, shift):
    index = lambda y, x, core: ((y % size) * size + x % size) * 2 + core
    pairs = []
    for y in range(size):
        for x in range(size):
            for core in range(2):
                to = (y, x + shift) if core == step else (y + shift, x)
                pairs.append((index(y, x, core), index(*to, core)))
    return pairs


def pile_body(chunks, size, place, table, mine, other, *rest):
    outs, planes = rest[:-1], rest[-1]
    number, rows, cols = mine.shape
    tiles = cols // lanes - 1
    patches = table.shape[0] // (slots + 1)
    core = place[0]
    planes[0:number] = mine[...]
    planes[number:] = other[...]
    lane = lane_ids(16)
    tail = lax.broadcasted_iota(jnp.int32, (16, lanes), 0)

    for chunk, out in zip(chunks, outs):

        def patch(i, _):
            u = (place[1] + chunk) % size
            v = (place[2] + i) % size
            p = jnp.where(core == 0, v * size + u, u * size + v) * 2

            def some(used):
                entries = []
                for c in range(2):
                    words = [table[patches + (p + c) * slots + s] for s in range(used)]
                    entries.append(
                        [
                            ((word >> 8) & (2 * number - 1), word & 255, (word >> 12).astype(f32))
                            for word in words
                        ]
                    )
                for r in range(rows // 16):
                    for c in range(2):
                        total = [jnp.zeros((16, lanes), f32)] * tiles
                        for e, o, weight in entries[c]:
                            early = lane < o
                            before = None
                            for k in range(tiles + 1):
                                piece = planes[e, r * 16 : r * 16 + 16, k * lanes : (k + 1) * lanes]
                                turned = pltpu.roll(piece, o, 1).astype(f32)
                                if k:
                                    part = jnp.where(early, before, turned)
                                    total[k - 1] = total[k - 1] + weight * part
                                before = turned
                        for k in range(tiles):
                            at = k * rows + r * 16
                            out[2 * i + c, at : at + 16, :] = total[k].astype(out.dtype)
                for c in range(2):
                    cover = jnp.zeros((16, lanes), f32)
                    whole = jnp.zeros((16, lanes), f32)
                    for e, o, weight in entries[c]:
                        cover = cover + jnp.where(lane < o, 0.0, weight)
                        whole = whole + weight
                    last = jnp.where(tail == 0, cover, whole)
                    out[2 * i + c, tiles * rows :, :] = last.astype(out.dtype)

            used = jnp.maximum(table[p], table[p + 1])
            for top in range(2, slots + 1, 2):
                low = top - 2 if top > 2 else -1

                @pl.when((used > low) & (used <= top))
                def _():
                    some(top)

            return 0

        lax.fori_loop(0, size, patch, 0)


def pile(chunks, kinds, size, place, table, mine, other):
    number, rows, cols = mine.shape
    smem = pl.BlockSpec(memory_space=pltpu.SMEM)
    vmem = pl.BlockSpec(memory_space=pltpu.VMEM)
    shape = (2 * size, (cols // lanes - 1) * rows + 16, lanes)
    return pl.pallas_call(
        functools.partial(pile_body, chunks, size),
        in_specs=[smem, smem, vmem, vmem],
        out_specs=[vmem] * len(chunks),
        out_shape=[jax.ShapeDtypeStruct(shape, kind) for kind in kinds],
        scratch_shapes=[pltpu.VMEM((2 * number, rows, cols), bf16)],
        compiler_params=pltpu.CompilerParams(vmem_limit_bytes=8 * mib),
        cost_estimate=pl.CostEstimate(
            flops=len(chunks) * 1000000000, bytes_accessed=4 * mine.size, transcendentals=0
        ),
        name="pile_" + "_".join(str(chunk) for chunk in chunks),
    )(place, table, mine, other)


def fold_body(own, *rest):
    came, keep, sends = rest[: len(rest) // 2], rest[len(rest) // 2], rest[len(rest) // 2 + 1 :]
    rows = own.shape[1]
    for i in range(own.shape[0]):
        for at in range(0, rows, 16):
            total = own[i, at : at + 16, :]
            for ref in came:
                total = total + ref[i, at : at + 16, :].astype(f32)
            if i < 2:
                keep[i, at : at + 16, :] = total
            else:
                sends[i // 2 - 1][i % 2, at : at + 16, :] = total.astype(bf16)


def fold(own, came):
    vmem = pl.BlockSpec(memory_space=pltpu.VMEM)
    shape = (2,) + own.shape[1:]
    return pl.pallas_call(
        fold_body,
        in_specs=[vmem] * (1 + len(came)),
        out_specs=[vmem] * (1 + len(came)),
        out_shape=[jax.ShapeDtypeStruct(shape, f32)] + [jax.ShapeDtypeStruct(shape, bf16)] * len(came),
        compiler_params=pltpu.CompilerParams(vmem_limit_bytes=4 * mib),
        name="fold",
    )(own, *came)


def meet_body(place, own, *rest):
    came, mine, send = rest[:-2], rest[-2], rest[-1]
    core = place[0]
    for at in range(0, own.shape[1], 16):
        for out, i in ((mine, core), (send, 1 - core)):
            total = own[i, at : at + 16, :]
            for ref in came:
                total = total + ref[i, at : at + 16, :].astype(f32)
            out[at : at + 16, :] = total


def meet(place, own, came):
    smem = pl.BlockSpec(memory_space=pltpu.SMEM)
    vmem = pl.BlockSpec(memory_space=pltpu.VMEM)
    return pl.pallas_call(
        meet_body,
        in_specs=[smem] + [vmem] * (1 + len(came)),
        out_specs=[vmem] * 2,
        out_shape=[jax.ShapeDtypeStruct(own.shape[1:], f32)] * 2,
        compiler_params=pltpu.CompilerParams(vmem_limit_bytes=4 * mib),
        name="meet",
    )(place, own, *came)


def coadd_body(reach, odd, place, mine, other, coadd, rounded, first, second, stage):
    rows, cols = coadd.shape
    tiles = cols // lanes
    near = place[0] == 0

    def pick(low, at):
        a, b = mine[at : at + 16, :], other[at : at + 16, :]
        return jnp.where(near, a, b) if low else jnp.where(near, b, a)

    cover = pick(True, tiles // 2 * rows)
    scales = [1.0 / jnp.maximum(cover[r : r + 1, :], 1.0) for r in (0, 1)]
    for m in range(tiles):
        for b in range(group):
            at = m % (tiles // 2) * rows + b * 16
            stage[m, pl.ds(b, 16, stride=group), :] = pick(m < tiles // 2, at) * scales[min(m, 1)]
        cut = slice(m * lanes, (m + 1) * lanes)
        coadd[:, cut] = stage[m]
        rounded[:, cut] = stage[m].astype(bf16)
        low = stage[m, 0:reach, :]
        high = stage[m, rows - reach : rows, :]
        first[:, cut] = jnp.where(odd[0] == 1, low, high).astype(bf16)
        second[:, cut] = jnp.where(odd[0] == 1, high, low).astype(bf16)


def coadd_of(odd, place, mine, other, rows, cols, reach):
    edge = jax.ShapeDtypeStruct((reach, cols), bf16)
    smem = pl.BlockSpec(memory_space=pltpu.SMEM)
    vmem = pl.BlockSpec(memory_space=pltpu.VMEM)
    return pl.pallas_call(
        functools.partial(coadd_body, reach),
        in_specs=[smem, smem, vmem, vmem],
        out_specs=(vmem,) * 4,
        out_shape=(
            jax.ShapeDtypeStruct((rows, cols), f32),
            jax.ShapeDtypeStruct((rows, cols), bf16),
            edge,
            edge,
        ),
        scratch_shapes=[pltpu.VMEM((cols // lanes, rows, lanes), f32)],
        compiler_params=pltpu.CompilerParams(vmem_limit_bytes=8 * mib),
        name="coadd",
    )(odd, place, mine, other)


def detect_own_body(taps, psf, x, acc, profile, frame, lhs, w):
    reach = taps // 2
    rows, cols = x.shape
    spans = taps + 3
    mask = band_mask(112, taps)
    for row in (0, 24 + rows):
        frame[:, :, row : row + 24, :] = jnp.zeros((2, cols // lanes, 24, lanes), f32)
    put_frame(frame, columns(x[...]), 24, reach)
    put_lhs(lhs, frame, spans, 24 - reach)
    clear_band(w, taps, 112, 0, spans)
    for s in range(psf.shape[0]):
        total = 0.0
        for rows_at, cols_at in zip(row_places(profile.shape[1], taps), lane_places(taps)):
            moved = jnp.dot(rows_at.astype(bf16), psf[s], preferred_element_type=f32)
            total = total + jnp.dot(
                moved.astype(bf16), cols_at.astype(bf16), preferred_element_type=f32
            )
        profile[s] = total
        put_band(w, total, taps, mask, 0, spans, 256 * s)
    acc[...] = jnp.dot(lhs[...], w[...], preferred_element_type=f32)


def detect_own(psf, x):
    rows, cols = x.shape
    scales, _, taps = psf.shape
    spans = taps + 3
    return pl.pallas_call(
        functools.partial(detect_own_body, taps),
        out_shape=(
            jax.ShapeDtypeStruct((256, scales * 256), f32),
            jax.ShapeDtypeStruct((scales, 48, lanes), f32),
        ),
        scratch_shapes=[
            pltpu.VMEM((2, cols // lanes, 24 + rows + 24, lanes), f32),
            pltpu.VMEM((256, spans * lanes), bf16),
            pltpu.VMEM((spans * lanes, scales * 256), bf16),
        ],
        compiler_params=pltpu.CompilerParams(vmem_limit_bytes=20 * mib),
        cost_estimate=pl.CostEstimate(
            flops=scales * 2 * 256 * 256 * spans * lanes, bytes_accessed=4 * x.size, transcendentals=0
        ),
        name="detect_own",
    )(psf, x)


def detect_halo_body(
    taps, odd, profile, first, second, acc, coadd, out, again, frame, lhs, w, stage, ready, leave
):
    scales, rows, cols = out.shape
    go = [pltpu.make_async_copy(ready.at[s], out.at[s], leave.at[s]) for s in range(scales)]
    go.append(pltpu.make_async_copy(coadd, again, leave.at[scales]))
    go[scales].start()
    count = cols // lanes
    spans = edge_spans(taps)
    frame[...] = jnp.zeros_like(frame)
    clear_band(w.at[0], taps, 112, 0, spans)
    clear_band(w.at[1], taps, 112, taps + 3 - spans, taps + 3)
    mask = band_mask(112, taps)
    lane = lane_ids(16)
    lo, hi = halo_pair(odd[0] == 1, first[...], second[...])
    put_edges(taps, frame, lhs, lo, hi)
    for s in range(scales):
        put_band(w.at[0], profile[s], taps, mask, 0, spans, 256 * s)
        put_band(w.at[1], profile[s], taps, mask, taps + 3 - spans, taps + 3, 256 * s)
    for s in range(scales):
        at = 256 * s
        ends = [
            jnp.dot(lhs[side], w[side, :, at : at + 256], preferred_element_type=f32)
            for side in range(2)
        ]
        for m in range(count):
            for h in range(2):
                cut = slice(h * lanes, (h + 1) * lanes)
                blocks = []
                for n in (m, count + m):
                    more = jnp.concatenate([end[n * 8 : n * 8 + 8, cut] for end in ends], axis=0)
                    own = acc[n * 16 : n * 16 + 16, at + h * lanes : at + (h + 1) * lanes]
                    blocks.append(own + more)
                for b, part in enumerate(split_rows(*blocks, lane)):
                    stage[s, m, pl.ds(2 * h + b, 16, stride=group), :] = part
            ready[s, :, m * lanes : (m + 1) * lanes] = stage[s, m]
        go[s].start()
    for copy in go:
        copy.wait()


def detect_halo(odd, profile, first, second, acc, coadd, rows, taps):
    cols = first.shape[1]
    scales = profile.shape[0]
    smem = pl.BlockSpec(memory_space=pltpu.SMEM)
    vmem = pl.BlockSpec(memory_space=pltpu.VMEM)
    return pl.pallas_call(
        functools.partial(detect_halo_body, taps),
        in_specs=[smem] + [vmem] * 5,
        out_specs=(pl.BlockSpec(memory_space=pl.ANY),) * 2,
        out_shape=(
            jax.ShapeDtypeStruct((scales, rows, cols), f32),
            jax.ShapeDtypeStruct((rows, cols), f32),
        ),
        scratch_shapes=edge_scratch(taps, cols // lanes, scales * 256)
        + [
            pltpu.VMEM((scales, cols // lanes, rows, lanes), f32),
            pltpu.VMEM((scales, rows, cols), f32),
            pltpu.SemaphoreType.DMA((scales + 1,)),
        ],
        compiler_params=pltpu.CompilerParams(vmem_limit_bytes=20 * mib),
        name="detect_halo",
    )(odd, profile, first, second, acc, coadd)


def trade(first, second):
    count = lax.axis_size("section")
    out = []
    for start, rows in ((0, first), (1, second)):
        pairs = [(i, i + 1) for i in range(start, count - 1, 2)]
        out.append(lax.ppermute(rows, "section", pairs + [(b, a) for a, b in pairs]))
    return out


def on_device(
    exposures,
    coef_code,
    coef_table,
    basis_rows,
    basis_cols,
    exposure_weight,
    intersection_patch,
    intersection_shift,
    psf_kernels,
):
    number, rows, cols = exposures.shape
    taps = basis_rows.shape[1]
    reach = taps // 2
    wide = psf_kernels.shape[-1]
    wide_reach = wide // 2
    sky = ("sy", "sx", "core")
    size = lax.axis_size("sx")
    patches = size * size * 2
    core, at_x, at_y = (lax.axis_index(name) for name in ("core", "sx", "sy"))
    place = jnp.stack([core, jnp.where(core == 0, at_x, at_y), jnp.where(core == 0, at_y, at_x)])
    odd = lax.axis_index("section") % 2

    low, high = exposures[:, :reach, :], exposures[:, rows - reach :, :]
    first, second = trade(jnp.where(odd == 1, low, high), jnp.where(odd == 1, high, low))
    odd = odd[None]

    labels = jnp.concatenate(
        [exposure_weight[:, None], intersection_patch, intersection_shift], axis=1
    )
    swap = [(0, 1), (1, 0)]
    other_labels = lax.ppermute(labels, "core", swap)

    profile = profiles(coef_code, coef_table, basis_rows.T, basis_cols.T)
    table = slot_table(labels, other_labels, patches)
    table, profile = lax.optimization_barrier((table, profile))
    mine, send = match(odd, place, profile, exposures, first, second)
    other = lax.ppermute(send, "core", swap)

    steps = (2, 3, 1)
    move = lambda rows, step, by: lax.ppermute(rows, sky, role_pairs(step, size, by))
    (far,) = pile((2,), (bf16,), size, place, table, mine, other)
    came = [move(far, 0, 2)]
    far, table = lax.optimization_barrier((far, table))
    behind, ahead = pile((3, 1), (bf16, bf16), size, place, table, mine, other)
    came += [move(behind, 0, 3), move(ahead, 0, 1)]
    ahead, table = lax.optimization_barrier((ahead, table))
    (own,) = pile((0,), (f32,), size, place, table, mine, other)
    keep, *sends = fold(own, came)
    came = [move(sends[by - 1], 1, by) for by in steps]
    mine, send = meet(place, keep, came)
    other = lax.ppermute(send, "core", swap)
    coadd, rounded, first, second = coadd_of(odd, place, mine, other, rows, cols, wide_reach)
    first, second = trade(first, second)
    acc, profile = detect_own(psf_kernels, rounded)
    detect, coadd = detect_halo(odd, profile, first, second, acc, coadd, rows, wide)
    return (coadd[None], detect[None])


def solution(mesh):
    sections, sky = mesh.devices.shape
    grid = Mesh(mesh.devices.reshape(sections, 4, sky // 8, 2), ("section", "sy", "sx", "core"))
    sky = ("sy", "sx", "core")
    return jax.shard_map(
        on_device,
        mesh=grid,
        in_specs=(
            P(sky, "section", None),
            P(sky, None),
            P(),
            P(),
            P(),
            P(sky),
            P(sky, None),
            P(sky, None),
            P(),
        ),
        out_specs=(P(sky, "section", None), P(sky, None, "section", None)),
        check_vma=False,
    )
```
